32 devices in a mesh: dp: 8 (over y, x, core), mp: 4 (over z).
Axes of the slice: x: 2, y: 2, z: 4, core: 2. Of those that a mesh axis runs over, the one named last changes fastest.
Arguments:
- patches: bfloat16 [32, 529, 768], P('dp'), may hold values from -6 to 6
- fill_lengths: int32 [32], P('dp'), may hold values from 33 to 529
- cotangent: bfloat16 [32, 529, 768], P('dp'), may hold values from -6 to 6
- norm1_gain: float32 [768], replicated, may hold values from 0.5 to 1.5
- norm1_shift: float32 [768], replicated, may hold values from -2 to 2
- w_qkv: bfloat16 [768, 3, 768], P(None, None, 'mp'), may hold values from -0.21875 to 0.21875
- qv_bias: float32 [2, 768], P(None, 'mp'), may hold values from -0.4 to 0.4
- w_out: bfloat16 [768, 768], P('mp'), may hold values from -1.5 to 1.5
- out_bias: float32 [768], replicated, may hold values from -2 to 2
- norm2_gain: float32 [768], replicated, may hold values from 0.5 to 1.5
- norm2_shift: float32 [768], replicated, may hold values from -2 to 2
- w_up: bfloat16 [768, 3072], P(None, 'mp'), may hold values from -0.21875 to 0.21875
- up_bias: float32 [3072], P('mp'), may hold values from -2 to 2
- w_down: bfloat16 [3072, 768], P('mp'), may hold values from -0.15625 to 0.15625
- down_bias: float32 [768], replicated, may hold values from -2 to 2
Outputs:
- layer_out: bfloat16 [32, 529, 768], P('dp')
- patches_grad: float32 [32, 529, 768], P('dp')
- norm1_gain_grad: float32 [768], P('dp')
- norm1_shift_grad: float32 [768], P('dp')
- w_qkv_grad: float32 [768, 3, 768], P('dp', None, 'mp')
- qv_bias_grad: float32 [2, 768], P(None, ('mp', 'dp'))
- w_out_grad: float32 [768, 768], P('mp', 'dp')
- out_bias_grad: float32 [768], P('dp')
- norm2_gain_grad: float32 [768], P('dp')
- norm2_shift_grad: float32 [768], P('dp')
- w_up_grad: float32 [768, 3072], P('dp', 'mp')
- up_bias_grad: float32 [3072], P(('mp', 'dp'))
- w_down_grad: float32 [3072, 768], P('mp', 'dp')
- down_bias_grad: float32 [768], P('dp')
The draws below stay inside these ranges and needn't reach their ends.
Inputs may be any that keep to these rules, and one draw needn't show every extreme that they name: Patches of item i at positions fill_lengths[i] and beyond are not keys.
All inputs are finite; a program needn't handle non-finite values.
Results may differ from the reference program's by a relative error of at most 0.012.
Values may be sent and summed in bfloat16 or wider, within the bound.
A program may use at most 192 MiB of HBM per device.

```python
import jax
import jax.numpy as jnp
from jax import lax

D = 768
HEADS = 12
HD = 64
FF = 3072
PATCHES = 529
ITEMS = 32


def draw_patches(key, part):
    key = jax.random.fold_in(key, 11)
    scale_key = jax.random.fold_in(key, 1)
    value_key = jax.random.fold_in(key, 2)
    row_scale = jnp.exp(jax.random.uniform(scale_key, (ITEMS, PATCHES, 1), jnp.float32, -0.7, 0.7))
    values = jax.random.normal(value_key, (ITEMS, PATCHES, D), jnp.float32)
    return jnp.clip(values * row_scale, -6.0, 6.0).astype(jnp.bfloat16)


def touch_ends(values, own_key, smallest, high):
    shape = values.shape
    spot = [jax.random.randint(jax.random.fold_in(own_key, axis), (), 0, shape[axis]) for axis in range(len(shape))]
    values = values.at[tuple(spot)].set(smallest)
    longest = shape.index(max(shape))
    spot[longest] = (spot[longest] + 1) % shape[longest]
    return values.at[tuple(spot)].set(high)


def raised(values, rng, source, target, shards_of, factor):
    def block_of(axis_at):
        return (jnp.arange(values.shape[axis_at]) // (values.shape[axis_at] // shards_of)).reshape((-1,) + (1,) * (values.ndim - 1 - axis_at))

    one_side = jax.random.permutation(rng, shards_of)[block_of(target)]
    far = (block_of(target) + shards_of // 2) % shards_of
    return jnp.where((block_of(source) == one_side) | (block_of(source) == far), factor * values, values)


def block_levels(stream_key, shape, pieces, smallest, largest):
    loudness, own = 1.0, jax.random.fold_in(stream_key, 6)
    for dim, parts in pieces:
        steps = jnp.exp(jax.random.uniform(jax.random.fold_in(own, dim), (parts,), jnp.float32, smallest / len(pieces), largest / len(pieces)))
        loudness = loudness * jnp.repeat(steps, shape[dim] // parts).reshape([-1 if axis == dim else 1 for axis in range(len(shape))])
    return loudness


def bell_draw(key, shape, scale, most, split=(), kind=jnp.bfloat16):
    factor_of = block_levels(key, shape, split, -0.22, 0.18) if split else 1.0
    values = jax.random.normal(key, shape, jnp.float32) * scale * factor_of
    return jnp.minimum(jnp.maximum(values, -most), most).astype(kind)


def bell_draw_with(own_key, extent, scale, bound, shards, heavy, kind=jnp.bfloat16):
    array = scale * jax.random.normal(own_key, extent, jnp.float32)
    if shards:
        array = array * block_levels(own_key, extent, shards, -0.22, 0.18)
    return jnp.clip(raised(array, jax.random.fold_in(own_key, 3), *heavy), -bound, bound).astype(kind)


def setup_inputs(seed: int = 0) -> dict:
    key_list = jax.random.split(jax.random.key(seed), 16)
    return {
        "patches": draw_patches(jax.random.fold_in(key_list[15], 71), 0),
        "fill_lengths": touch_ends(jax.random.randint(key_list[1], (ITEMS,), max(1, PATCHES // 16), PATCHES + 1), jax.random.fold_in(key_list[1], 1), max(1, PATCHES // 16), PATCHES).astype(jnp.int32),
        "cotangent": bell_draw_with(key_list[2], (ITEMS, PATCHES, D), 1.0, 6.0, ((0, 8),), (0, 2, 8, 2.0)),
        "norm1_gain": jnp.clip(1.0 + 0.1 * jax.random.normal(key_list[3], (D,), jnp.float32), 0.5, 1.5),
        "norm1_shift": bell_draw(key_list[4], (D,), 0.3, 2.0, (), jnp.float32),
        "w_qkv": bell_draw(key_list[5], (D, 3, HEADS * HD), D ** -0.5, 0.21875, ((2, 4),)),
        "qv_bias": bell_draw(key_list[6], (2, HEADS * HD), 0.05, 0.4, ((1, 4),), jnp.float32),
        "w_out": bell_draw(key_list[7], (HEADS * HD, D), 16 ** -0.5, 1.5, ((0, 4),)),
        "out_bias": bell_draw(key_list[8], (D,), 0.3, 2.0, (), jnp.float32),
        "norm2_gain": jnp.clip(1.0 + 0.1 * jax.random.normal(key_list[9], (D,), jnp.float32), 0.5, 1.5),
        "norm2_shift": bell_draw(key_list[10], (D,), 0.3, 2.0, (), jnp.float32),
        "w_up": bell_draw(key_list[11], (D, FF), D ** -0.5, 0.21875, ((1, 4),)),
        "up_bias": bell_draw(key_list[12], (FF,), 0.3, 2.0, ((0, 4),), jnp.float32),
        "w_down": bell_draw(key_list[13], (FF, D), (FF // 2) ** -0.5, 0.15625, ((0, 4),)),
        "down_bias": bell_draw(key_list[14], (D,), 0.3, 2.0, (), jnp.float32),
    }


@jax.custom_vjp
def low(v):
    return lax.optimization_barrier(v.astype(jnp.bfloat16)).astype(jnp.float32)

@jax.custom_vjp
def low_back(v):
    return v

def low_keep(v):
    return (low(v), None)

def low_pass(kept, grad):
    return (grad,)

def back_keep(v):
    return (v, None)

def back_low(kept, grad):
    return (low(grad),)
low.defvjp(low_keep, low_pass)
low_back.defvjp(back_keep, back_low)
epsilon = 1e-06
highest = lax.Precision.HIGHEST

def normalize(values, gain, shift):
    center = values - lax.optimization_barrier(jnp.mean(values, axis=-1, keepdims=True))
    inverse = lax.rsqrt(lax.optimization_barrier(jnp.mean(center * center, axis=-1, keepdims=True)) + epsilon)
    return center * inverse * gain + shift

def attend(operands):
    query_rows, key_rows, value_rows, usable = operands
    queries = query_rows.reshape(PATCHES, HEADS, HD)
    keyset = key_rows.reshape(PATCHES, HEADS, HD)
    valueset = value_rows.reshape(PATCHES, HEADS, HD)
    scores = low_back(jnp.einsum('qhd,khd->hqk', queries, keyset, precision=highest))
    scores = jnp.where(usable[None, None, :], scores, -1e+30)
    peak = lax.optimization_barrier(jnp.max(scores, axis=-1, keepdims=True))
    expsum = jnp.exp(scores - peak)
    probs = low(expsum / lax.optimization_barrier(jnp.sum(expsum, axis=-1, keepdims=True)))
    mixed = jnp.einsum('hqk,khd->qhd', probs, valueset, precision=highest)
    return low_back(low(mixed.reshape(PATCHES, HEADS * HD)))

def forward(patches, fill_lengths, norm1_gain, norm1_shift, w_qkv, qv_bias, w_out, out_bias, norm2_gain, norm2_shift, w_up, up_bias, w_down, down_bias):
    scaling = HD ** (-0.5)
    normed1 = low(normalize(patches, norm1_gain, norm1_shift))
    projected = jnp.einsum('isd,dtc->istc', normed1, w_qkv, precision=highest)
    queries = low_back(low((projected[:, :, 0] + qv_bias[0]) * scaling))
    key_rows = low_back(low(projected[:, :, 1]))
    value_rows = low_back(low(projected[:, :, 2] + qv_bias[1]))
    usable = jnp.arange(PATCHES, dtype=jnp.int32)[None, :] < fill_lengths[:, None]
    heads_out = lax.map(jax.checkpoint(attend), (queries, key_rows, value_rows, usable))
    attention = low_back(jnp.einsum('isc,cd->isd', heads_out, w_out, precision=highest))
    residual1 = patches + attention + out_bias
    normed2 = low(normalize(residual1, norm2_gain, norm2_shift))
    preact = low_back(jnp.einsum('isd,df->isf', normed2, w_up, precision=highest) + up_bias)
    hidden = low(jax.nn.gelu(preact))
    feedforward = low_back(jnp.einsum('isf,fd->isd', hidden, w_down, precision=highest))
    return residual1 + feedforward + down_bias

def reference(patches, fill_lengths, cotangent, norm1_gain, norm1_shift, w_qkv, qv_bias, w_out, out_bias, norm2_gain, norm2_shift, w_up, up_bias, w_down, down_bias):
    params = [patches, norm1_gain, norm1_shift, w_qkv, qv_bias, w_out, out_bias, norm2_gain, norm2_shift, w_up, up_bias, w_down, down_bias]
    params = [item.astype(jnp.float32) for item in params]

    def wrapped(*values):
        return forward(values[0], fill_lengths, *values[1:])
    result, backward = jax.vjp(wrapped, *params)
    grads = backward(cotangent.astype(jnp.float32))
    return (result.astype(jnp.bfloat16), grads[0], grads[1], grads[2], grads[3], grads[4], grads[5], grads[6], grads[7], grads[8], grads[9], grads[10], grads[11], grads[12])
```

```python
import functools
import jax
import jax.numpy as jnp
from jax import lax
from jax.experimental import pallas as pl
from jax.experimental.pallas import tpu as pltpu
from jax.sharding import PartitionSpec as P

MESH = pl.DeviceIdType.MESH
BF = jnp.bfloat16
F32 = jnp.float32
HD = 64
LANES = 128
EPS = 1e-6
MASKED = -1e30
GELU_A = 0.7978845608028654
GELU_B = 0.044715

NN = (((1,), (0,)), ((), ()))
NT = (((1,), (1,)), ((), ()))
TN = (((0,), (0,)), ((), ()))


def dot(a, b, dims):
    return lax.dot_general(a, b, dims, preferred_element_type=F32)


def place():
    d = lax.axis_index("dp")
    m = lax.axis_index("mp")
    y, x, c = d // 4, (d // 2) % 2, d % 2
    px = d + 2 - 4 * x
    py = d + 4 - 8 * y
    pc = d + 1 - 2 * c
    return d, m, y, x, c, px, py, pc


def other_z(m, k):
    low = (m % 2 + k % 2) % 2
    high = (m // 2 + k // 2) % 2
    return 2 * high + low


def enter(d, m, px, py, pc):
    barrier = pltpu.get_barrier_semaphore()
    for peer in ((px, m), (py, m), (pc, m)):
        pl.semaphore_signal(barrier, inc=1, device_id=peer, device_id_type=MESH)
    for k in (1, 2, 3):
        pl.semaphore_signal(barrier, inc=1, device_id=(d, other_z(m, k)), device_id_type=MESH)
    pl.semaphore_wait(barrier, 6)


def forward_kernel(
    fill_ref,
    x_ref,
    wa_in,
    wu_in,
    wd_in,
    bias_in,
    vec_ref,
    layer_out,
    qa_out,
    k_out,
    v_out,
    ho_out,
    n1_out,
    n2_out,
    r1_out,
    hid_out,
    gp_out,
    wa_out,
    wu_out,
    wd_out,
    wa,
    wu,
    wd,
    bias,
    q_s,
    k_s,
    v_s,
    ho_s,
    n1_s,
    n2_s,
    qa_s,
    r1_s,
    acc,
    hid_s,
    gp_s,
    lo_s,
    zs,
    zr,
    s1s,
    s1r,
    s2s,
    s2r,
    cs,
    cr,
    bs,
    br,
    load,
    out,
):
    d, m, y, x, c, px, py, pc = place()
    rows = x_ref.shape[0]
    half = rows // 2
    shards = (wa_in, wu_in, wd_in)

    def part(w, mk, ys, xs, core, start, size):
        if w == 0:
            return wa.at[ys, xs, pl.ds(mk * 192 + core * 96 + start, size)]
        full = wu if w == 1 else wd
        return full.at[mk, ys, xs, pl.ds(core * 96 + start, size)]

    every = slice(None)

    def remote(src, dst, send, recv, peer):
        return pltpu.make_async_remote_copy(
            src_ref=src, dst_ref=dst, send_sem=send, recv_sem=recv, device_id=peer, device_id_type=MESH
        )

    def z_copy(w, k):
        src = shards[w].at[y, x, pl.ds(c * 96, 96)]
        return remote(src, part(w, m, y, x, c, 0, 96), zs.at[w, k - 1], zr.at[w, k - 1], (d, other_z(m, k)))

    def z_wait(w, k):
        here = part(w, other_z(m, k), y, x, c, 0, 96)
        remote(here, here, zs.at[w, k - 1], zr.at[w, k - 1], (d, other_z(m, k))).wait_recv()

    def s1(w, k, h):
        mk = other_z(m, k)
        here = part(w, mk, y, x, c, 48 * h, 48)
        peer = (px, m) if h == 0 else (py, m)
        return remote(here, here, s1s.at[w, k - 1, h], s1r.at[w, k - 1, h], peer)

    def s1_wait(w, k, h):
        mk = other_z(m, k)
        here = part(w, mk, y, 1 - x, c, 0, 48) if h == 0 else part(w, mk, 1 - y, x, c, 48, 48)
        peer = (px, m) if h == 0 else (py, m)
        remote(here, here, s1s.at[w, k - 1, h], s1r.at[w, k - 1, h], peer).wait_recv()

    def s2(w, k, h):
        mk = other_z(m, k)
        here = part(w, mk, y, every, c, 0, 48) if h == 0 else part(w, mk, every, x, c, 48, 48)
        peer = (py, m) if h == 0 else (px, m)
        return remote(here, here, s2s.at[w, k - 1, h], s2r.at[w, k - 1, h], peer)

    def s2_wait(w, k, h):
        mk = other_z(m, k)
        here = part(w, mk, 1 - y, every, c, 0, 48) if h == 0 else part(w, mk, every, 1 - x, c, 48, 48)
        peer = (py, m) if h == 0 else (px, m)
        remote(here, here, s2s.at[w, k - 1, h], s2r.at[w, k - 1, h], peer).wait_recv()

    def core(w, k):
        here = part(w, other_z(m, k), every, every, c, 0, 96)
        return remote(here, here, cs.at[w, k - 1], cr.at[w, k - 1], (pc, m))

    def core_wait(w, k):
        here = part(w, other_z(m, k), every, every, 1 - c, 0, 96)
        remote(here, here, cs.at[w, k - 1], cr.at[w, k - 1], (pc, m)).wait_recv()

    def go1(w, k):
        z_wait(w, k)
        s1(w, k, 0).start()
        s1(w, k, 1).start()

    def go2(w, k):
        s1_wait(w, k, 0)
        s1_wait(w, k, 1)
        s2(w, k, 0).start()
        s2(w, k, 1).start()

    def go3(w, k):
        s2_wait(w, k, 0)
        s2_wait(w, k, 1)
        core(w, k).start()

    def own(w):
        return pltpu.make_async_copy(shards[w], part(w, m, every, every, 0, 0, 192), load.at[w])

    def bias_copy(k):
        return remote(bias_in, bias.at[m], bs.at[k - 1], br.at[k - 1], (d, other_z(m, k)))

    def bias_wait(k):
        here = bias.at[other_z(m, k)]
        remote(here, here, bs.at[k - 1], br.at[k - 1], (d, other_z(m, k))).wait_recv()

    enter(d, m, px, py, pc)
    for k in (1, 2, 3):
        z_copy(0, k).start()
    for k in (1, 2, 3):
        bias_copy(k).start()
    for w in range(3):
        own(w).start()
    own_bias = pltpu.make_async_copy(bias_in, bias.at[m], load.at[3])
    own_bias.start()

    def norm(values, gain, shift):
        center = values - jnp.mean(values, axis=-1, keepdims=True)
        inverse = lax.rsqrt(jnp.mean(center * center, axis=-1, keepdims=True) + EPS)
        return center * inverse * gain + shift

    n1_s[...] = norm(x_ref[...].astype(F32), vec_ref[0:1], vec_ref[1:2]).astype(BF)
    save = [pltpu.make_async_copy(n1_s, n1_out, out.at[0])]
    save[0].start()

    go1(0, 1)
    go2(0, 1)
    go1(0, 2)
    go1(0, 3)
    for k in (1, 2, 3):
        z_copy(1, k).start()
    go3(0, 1)
    go2(0, 2)
    go2(0, 3)
    for w in range(3):
        own(w).wait()
    own_bias.wait()
    for k in (1, 2, 3):
        bias_wait(k)
    core_wait(0, 1)

    group0 = m // 2
    key_row = lax.broadcasted_iota(jnp.int32, (rows, LANES), 0)
    lane = lax.broadcasted_iota(jnp.int32, (rows, LANES), 1)
    mask_add = jnp.where(key_row < fill_ref[0], 0.0, MASKED)
    lane_half = lax.broadcasted_iota(jnp.int32, (half, LANES), 1)

    def project(g):
        rows_w = pl.ds(pl.multiple_of(g * 384, 128), 384)
        lanes = rows_w
        qb = bias[0, 1:2, lanes] + bias[1, 1:2, lanes] + bias[2, 1:2, lanes] + bias[3, 1:2, lanes]
        vb = bias[0, 2:3, lanes] + bias[1, 2:3, lanes] + bias[2, 2:3, lanes] + bias[3, 2:3, lanes]
        n1 = n1_s[...]
        q_s[:, lanes] = ((dot(n1, wa[0, 0, rows_w], NT) + qb) * (HD**-0.5)).astype(BF)
        k_s[:, lanes] = dot(n1, wa[0, 1, rows_w], NT).astype(BF)
        v_s[:, lanes] = (dot(n1, wa[1, 0, rows_w], NT) + vb).astype(BF)

    def attend(p):
        lanes = pl.ds(pl.multiple_of(p * LANES, LANES), LANES)
        kp = k_s[:, lanes].astype(F32)
        vp = v_s[:, lanes]
        keys = []
        for h in (0, 1):
            own_lane = (lane < HD) if h == 0 else (lane >= HD)
            first = HD if h == 0 else 0
            extra = jnp.where(lane == first, mask_add, jnp.where(lane < first + 4, 1.0, 0.0))
            keys.append(jnp.where(own_lane, kp, extra).astype(BF))
        for b in (0, 1):
            block = pl.ds(b * half, half)
            qp = q_s[block, lanes].astype(F32)
            mixed = []
            for h in (0, 1):
                own_lane = (lane_half < HD) if h == 0 else (lane_half >= HD)
                first = HD if h == 0 else 0
                base = jnp.where(own_lane, qp, jnp.where(lane_half == first, 1.0, 0.0))
                s = dot(base.astype(BF), keys[h], NT)
                peak = jnp.max(s, axis=-1, keepdims=True)
                e = jnp.exp(s - peak)
                total = jnp.sum(e, axis=-1, keepdims=True)
                mixed.append(dot(e.astype(BF), vp, NN) / total)
                lse = peak + jnp.log(total)
                hi = lse.astype(BF).astype(F32)
                lo = (lse - hi).astype(BF).astype(F32)
                rest = lse - hi - lo
                extra = jnp.where(
                    lane_half == first + 1, -hi, jnp.where(lane_half == first + 2, -lo, jnp.where(lane_half == first + 3, -rest, 0.0))
                )
                extra = jnp.where(lane_half == first, 1.0, extra)
                qa_s[2 * p + h, block] = jnp.where(own_lane, qp, extra).astype(BF)
            ho_s[block, lanes] = jnp.where(lane_half < HD, mixed[0], mixed[1]).astype(BF)

    project(group0)
    go3(0, 2)
    go3(0, 3)

    def first_group(j, carry):
        attend(group0 * 3 + j)
        go1(1, j + 1)
        return carry

    lax.fori_loop(0, 3, first_group, 0)
    for k in (1, 2, 3):
        z_copy(2, k).start()
    for k in (1, 2, 3):
        go2(1, k)
    core_wait(0, 2)
    core_wait(0, 3)
    project(1 - group0)

    def second_group(j, carry):
        attend((1 - group0) * 3 + j)
        go3(1, j + 1)
        go1(2, j + 1)
        return carry

    lax.fori_loop(0, 3, second_group, 0)
    for k in (1, 2, 3):
        go2(2, k)
    pairs = ((qa_s, qa_out), (k_s, k_out), (v_s, v_out), (ho_s, ho_out))
    for i, (a, b) in enumerate(pairs):
        save.append(pltpu.make_async_copy(a, b, out.at[1 + i]))
        save[-1].start()
    r1 = x_ref[...].astype(F32) + dot(ho_s[...], wa[1, 1], NN) + vec_ref[2:3]
    r1_s[...] = r1
    n2_s[...] = norm(r1, vec_ref[3:4], vec_ref[4:5]).astype(BF)
    acc[...] = r1 + vec_ref[5:6]
    more = ((r1_s, r1_out), (n2_s, n2_out), (wa, wa_out))
    for i, (a, b) in enumerate(more):
        save.append(pltpu.make_async_copy(a, b, out.at[5 + i]))
        save[-1].start()
    for k in (1, 2, 3):
        go3(2, k)

    def feed(k, carry):
        mk = other_z(m, k)

        @pl.when(k > 0)
        def _():
            core_wait(1, k)
            core_wait(2, k)

        def up(n, inner):
            cols = pl.ds(pl.multiple_of(n * 256, 256), 256)
            w = wu[mk, :, :, :, cols].reshape(768, 256)
            v = dot(n2_s[...], w, NN) + bias[mk, 0:1, cols]
            sq = v * v
            t = jnp.tanh(v * (GELU_A + GELU_A * GELU_B * sq))
            hid_s[mk, :, cols] = (0.5 * v * (1.0 + t)).astype(BF)
            slope = 0.5 * (1.0 + t) + 0.5 * v * (1.0 - t * t) * (GELU_A + 3.0 * GELU_A * GELU_B * sq)
            gp_s[mk, :, cols] = slope.astype(BF)
            return inner

        lax.fori_loop(0, 3, up, 0)

        def down(n, inner):
            cols = pl.ds(pl.multiple_of(n * 256, 256), 256)
            w = wd[mk, :, :, :, cols].reshape(768, 256)
            acc[:, cols] += dot(hid_s[mk], w, NN)
            return inner

        lax.fori_loop(0, 3, down, 0)
        return carry

    lax.fori_loop(0, 4, feed, 0)
    lo_s[...] = acc[...].astype(BF)
    last = ((hid_s, hid_out), (gp_s, gp_out), (wu, wu_out), (wd, wd_out), (lo_s, layer_out))
    for i, (a, b) in enumerate(last):
        save.append(pltpu.make_async_copy(a, b, out.at[8 + i]))
        save[-1].start()
    for one in save:
        one.wait()
    for k in (1, 2, 3):
        bias_copy(k).wait_send()
    for w in range(3):
        for k in (1, 2, 3):
            z_copy(w, k).wait_send()
            for h in (0, 1):
                s1(w, k, h).wait_send()
                s2(w, k, h).wait_send()
            core(w, k).wait_send()


def forward_call(fill, x, wa, wu, wd, bias, vec):
    rows, width = x.shape
    any_spec = pl.BlockSpec(memory_space=pl.ANY)
    vmem = pl.BlockSpec(memory_space=pltpu.VMEM)
    flat = (rows, width)

    def hbm(shape, kind=BF):
        return jax.ShapeDtypeStruct(shape, kind)

    outs = [
        hbm(flat),
        hbm((12, rows, LANES)),
        hbm(flat),
        hbm(flat),
        hbm(flat),
        hbm(flat),
        hbm(flat),
        hbm(flat, F32),
        hbm((4, rows, 768)),
        hbm((4, rows, 768)),
        hbm((2, 2, 768, 768)),
        hbm((4, 2, 2, 192, 768)),
        hbm((4, 2, 2, 192, 768)),
    ]
    dma = pltpu.SemaphoreType.DMA
    scratch = [
        pltpu.VMEM((2, 2, 768, 768), BF),
        pltpu.VMEM((4, 2, 2, 192, 768), BF),
        pltpu.VMEM((4, 2, 2, 192, 768), BF),
        pltpu.VMEM((4, 8, 768), F32),
        pltpu.VMEM(flat, BF),
        pltpu.VMEM(flat, BF),
        pltpu.VMEM(flat, BF),
        pltpu.VMEM(flat, BF),
        pltpu.VMEM(flat, BF),
        pltpu.VMEM(flat, BF),
        pltpu.VMEM((12, rows, LANES), BF),
        pltpu.VMEM(flat, F32),
        pltpu.VMEM(flat, F32),
        pltpu.VMEM((4, rows, 768), BF),
        pltpu.VMEM((4, rows, 768), BF),
        pltpu.VMEM(flat, BF),
        dma((3, 3)),
        dma((3, 3)),
        dma((3, 3, 2)),
        dma((3, 3, 2)),
        dma((3, 3, 2)),
        dma((3, 3, 2)),
        dma((3, 3)),
        dma((3, 3)),
        dma((3,)),
        dma((3,)),
        dma((4,)),
        dma((13,)),
    ]
    return pl.pallas_call(
        forward_kernel,
        out_shape=outs,
        in_specs=[pl.BlockSpec(memory_space=pltpu.SMEM), vmem, any_spec, any_spec, any_spec, any_spec, vmem],
        out_specs=[any_spec] * len(outs),
        scratch_shapes=scratch,
        compiler_params=pltpu.CompilerParams(collective_id=0, has_side_effects=True, vmem_limit_bytes=60 << 20),
        name="forward",
    )(fill, x, wa, wu, wd, bias, vec)


def prepare(patches, fill_lengths, cotangent, norm1_gain, norm1_shift, w_qkv, qv_bias, w_out, out_bias, norm2_gain, norm2_shift, w_up, up_bias, w_down, down_bias):
    m = lax.axis_index("mp")
    length, width = patches.shape[1:]
    rows = -(-length // 32) * 32
    pad = ((0, rows - length), (0, 0))
    x = jnp.pad(lax.dynamic_index_in_dim(patches, m, 0, keepdims=False), pad)
    cot = jnp.pad(lax.dynamic_index_in_dim(cotangent, m, 0, keepdims=False), pad)
    fill = lax.dynamic_slice(fill_lengths, (m,), (1,))
    wa = jnp.concatenate([jnp.transpose(w_qkv, (1, 2, 0)).reshape(576, width), w_out], axis=0)
    wa = wa.reshape(2, 2, 192, width)
    wu = w_up.reshape(2, 2, 192, width)
    wd = w_down.reshape(2, 2, 192, width)
    placed = lax.dynamic_update_slice(jnp.zeros((2, width), F32), qv_bias, (0, m * 192))
    bias = jnp.concatenate([up_bias[None], placed, jnp.zeros((5, width), F32)], axis=0)
    zero = jnp.zeros_like(norm1_gain)
    vec = jnp.stack([norm1_gain, norm1_shift, out_bias, norm2_gain, norm2_shift, down_bias, zero, zero])
    return x, cot, fill, wa, wu, wd, bias, vec


def one_item(*args):
    (patches, fill_lengths, cotangent, norm1_gain, norm1_shift, w_qkv, qv_bias, w_out, out_bias, norm2_gain, norm2_shift, w_up, up_bias, w_down, down_bias) = args
    x, cot, fill, wa, wu, wd, bias, vec = prepare(*args)
    length, width = patches.shape[1:]
    lo, qa, k, v, ho, n1, n2, r1, hid, gp, waf, wuf, wdf = forward_call(fill, x, wa, wu, wd, bias, vec)
    rows = x.shape[0]
    layer_out = lax.all_gather(lo[:length], "mp", axis=0)
    wdf = wdf.reshape(3072, width)
    wuf = wuf.reshape(4, width, 768)
    waf = waf.reshape(4, 768, width)
    G = cot
    hid2 = jnp.transpose(hid, (1, 0, 2)).reshape(rows, 3072)
    ein = functools.partial(jnp.einsum, preferred_element_type=F32)
    gw_down = ein("rd,rf->df", G, hid2)
    hg = ein("rd,fd->rf", G, wdf)
    pg = (hg * jnp.transpose(gp, (1, 0, 2)).reshape(rows, 3072)).astype(BF)
    gw_up = ein("rd,rf->df", n2, pg)
    U2 = ein("rmf,mdf->rd", pg.reshape(rows, 4, 768), wuf)

    def stats(vals):
        c = vals - jnp.mean(vals, -1, keepdims=True)
        r = lax.rsqrt(jnp.mean(c * c, -1, keepdims=True) + EPS)
        return c * r, r

    def back(U, n, r, g):
        s = U * g
        return r * (s - s.mean(-1, keepdims=True) - n * (s * n).mean(-1, keepdims=True))

    nn2, rr2 = stats(r1)
    r1g = G.astype(F32) + back(U2, nn2, rr2, norm2_gain)
    R = r1g.astype(BF)
    gw_out = ein("rd,rc->dc", R, ho)
    dho = ein("rd,cd->rc", R, waf[3]).astype(BF)
    lanes = jnp.arange(128)
    dq, dk, dv = [], [], []
    for h in range(12):
        sl = slice(h * 64, h * 64 + 64)
        first = 64 if h % 2 == 0 else 0
        mine = slice(64 - first, 128 - first)
        kk = k[:, sl]
        mask = jnp.where(jnp.arange(rows) < fill[0], 0.0, MASKED)[None]
        q = qa[h][:, mine]
        lse = -(qa[h][:, first + 1 : first + 4].astype(F32).sum(-1, keepdims=True))
        s = ein("qd,kd->qk", q, kk) + mask
        p = jnp.exp(s - lse)
        dO = dho[:, sl]
        dv.append(ein("qk,qd->kd", p.astype(BF), dO))
        dp = ein("qd,kd->qk", dO, v[:, sl])
        D = jnp.sum(dO.astype(F32) * ho[:, sl].astype(F32), -1, keepdims=True)
        ds = (p * (dp - D)).astype(BF)
        dq.append(ein("qk,kd->qd", ds, kk))
        dk.append(ein("qk,qd->kd", ds, q))
    dq, dk, dv = [jnp.concatenate(t, -1).astype(BF) for t in (dq, dk, dv)]
    dq = dq * jnp.asarray(0.125, BF)
    gw_qkv = jnp.stack([ein("rd,rc->dc", n1, t) for t in (dq, dk, dv)], 1)
    U1 = sum(ein("rc,cd->rd", t, waf[i]) for i, t in enumerate((dq, dk, dv)))
    nn1, rr1 = stats(x.astype(F32))
    pgrad = r1g + back(U1, nn1, rr1, norm1_gain)
    patches_grad = lax.all_gather(pgrad[:length].astype(BF), "mp", axis=0).astype(F32)
    scat = functools.partial(lax.psum_scatter, tiled=True)

    def both(t, dim_dp, dim_mp):
        t = scat(t, "mp", scatter_dimension=dim_mp)
        return scat(t, "dp", scatter_dimension=dim_dp)

    def vecsum(t):
        return scat(lax.psum(t, "mp"), "dp", scatter_dimension=0)

    g_qkv = both(gw_qkv, 0, 2)
    g_out = both(gw_out, 0, 1).T
    g_up = both(gw_up, 0, 1)
    g_down = both(gw_down, 0, 1).T
    qv = jnp.stack([dq.astype(F32).sum(0), dv.astype(F32).sum(0)])
    qv = both(qv, 1, 1)
    ub = both(pg.astype(F32).sum(0), 0, 0)
    return (
        layer_out,
        patches_grad,
        vecsum((U1 * nn1).sum(0)),
        vecsum(U1.sum(0)),
        g_qkv,
        qv,
        g_out,
        vecsum(r1g.sum(0)),
        vecsum((U2 * nn2).sum(0)),
        vecsum(U2.sum(0)),
        g_up,
        ub,
        g_down,
        vecsum(G.astype(F32).sum(0)),
    )


def normalize(values, gain, shift):
    center = values - jnp.mean(values, axis=-1, keepdims=True)
    inverse = lax.rsqrt(jnp.mean(center * center, axis=-1, keepdims=True) + EPS)
    unit = center * inverse
    return (unit, inverse, unit * gain + shift)


def normalize_back(upstream, unit, inverse, gain):
    gain_grad = jnp.sum(upstream * unit, axis=(0, 1))
    shift_grad = jnp.sum(upstream, axis=(0, 1))
    scaled = upstream * gain
    result = inverse * (
        scaled
        - jnp.mean(scaled, axis=-1, keepdims=True)
        - unit * jnp.mean(scaled * unit, axis=-1, keepdims=True)
    )
    return (gain_grad, shift_grad, result)


def split_heads(rows):
    return rows.reshape(rows.shape[0], rows.shape[1] // HD, HD)


def masked_scores(queries, keyset, usable):
    scores = jnp.einsum("qhd,khd->hqk", queries, keyset, preferred_element_type=jnp.float32)
    return jnp.where(usable[None, None, :], scores, -1e30)


def attend_items(operands):
    query_rows, key_rows, value_rows, usable = operands
    scores = masked_scores(split_heads(query_rows), split_heads(key_rows), usable)
    peak = jnp.max(scores, axis=-1, keepdims=True)
    expsum = jnp.exp(scores - peak)
    total = jnp.sum(expsum, axis=-1, keepdims=True)
    weights = (expsum / total).astype(jnp.bfloat16)
    mixed = jnp.einsum(
        "hqk,khd->qhd", weights, split_heads(value_rows), preferred_element_type=jnp.float32
    )
    return (
        mixed.reshape(query_rows.shape).astype(jnp.bfloat16),
        peak[..., 0] + jnp.log(total[..., 0]),
    )


def attend_items_back(operands):
    query_rows, key_rows, value_rows, usable, logsum, upstream = operands
    queries = split_heads(query_rows)
    keyset = split_heads(key_rows)
    scores = masked_scores(queries, keyset, usable)
    probs = jnp.exp(scores - logsum[..., None])
    weights = probs.astype(jnp.bfloat16)
    grad_heads = split_heads(upstream)
    value_grad = jnp.einsum("hqk,qhd->khd", weights, grad_heads, preferred_element_type=jnp.float32)
    prob_grad = jnp.einsum(
        "qhd,khd->hqk", grad_heads, split_heads(value_rows), preferred_element_type=jnp.float32
    )
    center = jnp.sum(probs * prob_grad, axis=-1, keepdims=True)
    score_grad = (probs * (prob_grad - center)).astype(jnp.bfloat16)
    query_grad = jnp.einsum("hqk,khd->qhd", score_grad, keyset, preferred_element_type=jnp.float32)
    key_grad = jnp.einsum("hqk,qhd->khd", score_grad, queries, preferred_element_type=jnp.float32)
    shape = query_rows.shape
    return (
        query_grad.reshape(shape).astype(jnp.bfloat16),
        key_grad.reshape(shape).astype(jnp.bfloat16),
        value_grad.reshape(shape).astype(jnp.bfloat16),
    )


def shards(
    patches,
    fill_lengths,
    cotangent,
    norm1_gain,
    norm1_shift,
    w_qkv,
    qv_bias,
    w_out,
    out_bias,
    norm2_gain,
    norm2_shift,
    w_up,
    up_bias,
    w_down,
    down_bias,
):
    scaling = HD ** (-0.5)
    seq_len = patches.shape[1]
    inputs = patches.astype(jnp.float32)
    unit1, inverse1, normed1_full = normalize(inputs, norm1_gain, norm1_shift)
    normed1 = normed1_full.astype(jnp.bfloat16)
    projected = jnp.einsum("isd,dtc->istc", normed1, w_qkv, preferred_element_type=jnp.float32)
    queries = ((projected[:, :, 0] + qv_bias[0]) * scaling).astype(jnp.bfloat16)
    key_rows = projected[:, :, 1].astype(jnp.bfloat16)
    value_rows = (projected[:, :, 2] + qv_bias[1]).astype(jnp.bfloat16)
    usable = jnp.arange(seq_len, dtype=jnp.int32)[None, :] < fill_lengths[:, None]
    heads_out, logsum = lax.map(attend_items, (queries, key_rows, value_rows, usable))
    partial_attn = jnp.einsum("isc,cd->isd", heads_out, w_out, preferred_element_type=jnp.float32)
    attention = lax.psum(partial_attn, "mp")
    residual1 = inputs + attention + out_bias
    unit2, inverse2, normed2_full = normalize(residual1, norm2_gain, norm2_shift)
    normed2 = normed2_full.astype(jnp.bfloat16)
    preact = jnp.einsum("isd,df->isf", normed2, w_up, preferred_element_type=jnp.float32) + up_bias
    activated, gelu_back = jax.vjp(jax.nn.gelu, preact)
    hidden = activated.astype(jnp.bfloat16)
    partial_ff = jnp.einsum("isf,fd->isd", hidden, w_down, preferred_element_type=jnp.float32)
    feedforward = lax.psum(partial_ff, "mp")
    layer_out = (residual1 + feedforward + down_bias).astype(jnp.bfloat16)
    upstream = cotangent.astype(jnp.float32)
    down_bias_grad = jnp.sum(upstream, axis=(0, 1))
    w_down_grad = jnp.einsum("isf,isd->fd", hidden, cotangent, preferred_element_type=jnp.float32)
    hidden_grad = jnp.einsum("isd,fd->isf", cotangent, w_down, preferred_element_type=jnp.float32)
    preact_grad = gelu_back(hidden_grad)[0].astype(jnp.bfloat16)
    up_bias_grad = jnp.sum(preact_grad.astype(jnp.float32), axis=(0, 1))
    w_up_grad = jnp.einsum("isd,isf->df", normed2, preact_grad, preferred_element_type=jnp.float32)
    partial_norm2 = jnp.einsum("isf,df->isd", preact_grad, w_up, preferred_element_type=jnp.float32)
    normed2_grad = lax.psum(partial_norm2, "mp")
    norm2_gain_grad, norm2_shift_grad, through_norm2 = normalize_back(
        normed2_grad, unit2, inverse2, norm2_gain
    )
    residual1_grad = upstream + through_norm2
    out_bias_grad = jnp.sum(residual1_grad, axis=(0, 1))
    residual_low = residual1_grad.astype(jnp.bfloat16)
    w_out_grad = jnp.einsum(
        "isc,isd->cd", heads_out, residual_low, preferred_element_type=jnp.float32
    )
    heads_grad = jnp.einsum(
        "isd,cd->isc", residual_low, w_out, preferred_element_type=jnp.float32
    ).astype(jnp.bfloat16)
    query_grad, key_grad, value_grad = lax.map(
        attend_items_back, (queries, key_rows, value_rows, usable, logsum, heads_grad)
    )
    query_scaled = query_grad * scaling
    proj_grad = jnp.stack([query_scaled, key_grad, value_grad], axis=2)
    w_qkv_grad = jnp.einsum("isd,istc->dtc", normed1, proj_grad, preferred_element_type=jnp.float32)
    qv_bias_grad = jnp.stack(
        [
            jnp.sum(query_scaled.astype(jnp.float32), axis=(0, 1)),
            jnp.sum(value_grad.astype(jnp.float32), axis=(0, 1)),
        ]
    )
    partial_norm1 = jnp.einsum(
        "istc,dtc->isd", proj_grad, w_qkv, preferred_element_type=jnp.float32
    )
    normed1_grad = lax.psum(partial_norm1, "mp")
    norm1_gain_grad, norm1_shift_grad, through_norm1 = normalize_back(
        normed1_grad, unit1, inverse1, norm1_gain
    )
    patches_grad = residual1_grad + through_norm1
    summed = (
        lax.psum_scatter(norm1_gain_grad, "dp", scatter_dimension=0, tiled=True),
        lax.psum_scatter(norm1_shift_grad, "dp", scatter_dimension=0, tiled=True),
        lax.psum_scatter(w_qkv_grad, "dp", scatter_dimension=0, tiled=True),
        lax.psum_scatter(qv_bias_grad, "dp", scatter_dimension=1, tiled=True),
        lax.psum_scatter(w_out_grad, "dp", scatter_dimension=1, tiled=True),
        lax.psum_scatter(out_bias_grad, "dp", scatter_dimension=0, tiled=True),
        lax.psum_scatter(w_up_grad, "dp", scatter_dimension=0, tiled=True),
        lax.psum_scatter(up_bias_grad, "dp", scatter_dimension=0, tiled=True),
        lax.psum_scatter(w_down_grad, "dp", scatter_dimension=1, tiled=True),
        lax.psum_scatter(down_bias_grad, "dp", scatter_dimension=0, tiled=True),
        lax.psum_scatter(norm2_gain_grad, "dp", scatter_dimension=0, tiled=True),
        lax.psum_scatter(norm2_shift_grad, "dp", scatter_dimension=0, tiled=True),
    )
    return (
        layer_out,
        patches_grad,
        summed[0],
        summed[1],
        summed[2],
        summed[3],
        summed[4],
        summed[5],
        summed[10],
        summed[11],
        summed[6],
        summed[7],
        summed[8],
        summed[9],
    )


def solution(mesh):
    body = one_item if (mesh.shape['dp'], mesh.shape['mp']) == (8, 4) else shards
    return jax.shard_map(
        body,
        mesh=mesh,
        in_specs=(
            P("dp", None, None),
            P("dp"),
            P("dp", None, None),
            P(),
            P(),
            P(None, None, "mp"),
            P(None, "mp"),
            P("mp", None),
            P(),
            P(),
            P(),
            P(None, "mp"),
            P("mp"),
            P("mp", None),
            P(),
        ),
        out_specs=(
            P("dp", None, None),
            P("dp", None, None),
            P("dp"),
            P("dp"),
            P("dp", None, "mp"),
            P(None, ("mp", "dp")),
            P("mp", "dp"),
            P("dp"),
            P("dp"),
            P("dp"),
            P("dp", "mp"),
            P(("mp", "dp")),
            P("mp", "dp"),
            P("dp"),
        ),
        check_vma=False,
    )
```

```python
import functools
import jax
import jax.numpy as jnp
from jax import lax
from jax.experimental import pallas as pl
from jax.experimental.pallas import tpu as pltpu
from jax.sharding import PartitionSpec as P

MESH = pl.DeviceIdType.MESH
BF = jnp.bfloat16
F32 = jnp.float32
HD = 64
LANES = 128
EPS = 1e-6
MASKED = -1e30
GELU_A = 0.7978845608028654
GELU_B = 0.044715

NN = (((1,), (0,)), ((), ()))
NT = (((1,), (1,)), ((), ()))
TN = (((0,), (0,)), ((), ()))


def dot(a, b, dims):
    return lax.dot_general(a, b, dims, preferred_element_type=F32)


def place():
    d = lax.axis_index("dp")
    m = lax.axis_index("mp")
    y, x, c = d // 4, (d // 2) % 2, d % 2
    px = d + 2 - 4 * x
    py = d + 4 - 8 * y
    pc = d + 1 - 2 * c
    return d, m, y, x, c, px, py, pc


def other_z(m, k):
    low = (m % 2 + k % 2) % 2
    high = (m // 2 + k // 2) % 2
    return 2 * high + low


def enter(d, m, px, py, pc):
    barrier = pltpu.get_barrier_semaphore()
    for peer in ((px, m), (py, m), (pc, m)):
        pl.semaphore_signal(barrier, inc=1, device_id=peer, device_id_type=MESH)
    for k in (1, 2, 3):
        pl.semaphore_signal(barrier, inc=1, device_id=(d, other_z(m, k)), device_id_type=MESH)
    pl.semaphore_wait(barrier, 6)


def forward_kernel(
    fill_ref,
    x_ref,
    wa_in,
    wu_in,
    wd_in,
    bias_in,
    vec_ref,
    layer_out,
    qa_out,
    k_out,
    v_out,
    ho_out,
    n1_out,
    n2_out,
    r1_out,
    hid_out,
    gp_out,
    wa_out,
    wu_out,
    wd_out,
    wa,
    wu,
    wd,
    bias,
    q_s,
    k_s,
    v_s,
    ho_s,
    n1_s,
    n2_s,
    qa_s,
    r1_s,
    acc,
    hid_s,
    gp_s,
    lo_s,
    zs,
    zr,
    s1s,
    s1r,
    s2s,
    s2r,
    cs,
    cr,
    bs,
    br,
    load,
    out,
):
    d, m, y, x, c, px, py, pc = place()
    rows = x_ref.shape[0]
    half = rows // 2
    shards = (wa_in, wu_in, wd_in)

    def part(w, mk, ys, xs, core, start, size):
        if w == 0:
            return wa.at[ys, xs, pl.ds(mk * 192 + core * 96 + start, size)]
        full = wu if w == 1 else wd
        return full.at[mk, ys, xs, pl.ds(core * 96 + start, size)]

    every = slice(None)

    def remote(src, dst, send, recv, peer):
        return pltpu.make_async_remote_copy(
            src_ref=src, dst_ref=dst, send_sem=send, recv_sem=recv, device_id=peer, device_id_type=MESH
        )

    def z_copy(w, k):
        src = shards[w].at[y, x, pl.ds(c * 96, 96)]
        return remote(src, part(w, m, y, x, c, 0, 96), zs.at[w, k - 1], zr.at[w, k - 1], (d, other_z(m, k)))

    def z_wait(w, k):
        here = part(w, other_z(m, k), y, x, c, 0, 96)
        remote(here, here, zs.at[w, k - 1], zr.at[w, k - 1], (d, other_z(m, k))).wait_recv()

    def s1(w, k, h):
        mk = other_z(m, k)
        here = part(w, mk, y, x, c, 48 * h, 48)
        peer = (px, m) if h == 0 else (py, m)
        return remote(here, here, s1s.at[w, k - 1, h], s1r.at[w, k - 1, h], peer)

    def s1_wait(w, k, h):
        mk = other_z(m, k)
        here = part(w, mk, y, 1 - x, c, 0, 48) if h == 0 else part(w, mk, 1 - y, x, c, 48, 48)
        peer = (px, m) if h == 0 else (py, m)
        remote(here, here, s1s.at[w, k - 1, h], s1r.at[w, k - 1, h], peer).wait_recv()

    def s2(w, k, h):
        mk = other_z(m, k)
        here = part(w, mk, y, every, c, 0, 48) if h == 0 else part(w, mk, every, x, c, 48, 48)
        peer = (py, m) if h == 0 else (px, m)
        return remote(here, here, s2s.at[w, k - 1, h], s2r.at[w, k - 1, h], peer)

    def s2_wait(w, k, h):
        mk = other_z(m, k)
        here = part(w, mk, 1 - y, every, c, 0, 48) if h == 0 else part(w, mk, every, 1 - x, c, 48, 48)
        peer = (py, m) if h == 0 else (px, m)
        remote(here, here, s2s.at[w, k - 1, h], s2r.at[w, k - 1, h], peer).wait_recv()

    def core(w, k):
        here = part(w, other_z(m, k), every, every, c, 0, 96)
        return remote(here, here, cs.at[w, k - 1], cr.at[w, k - 1], (pc, m))

    def core_wait(w, k):
        here = part(w, other_z(m, k), every, every, 1 - c, 0, 96)
        remote(here, here, cs.at[w, k - 1], cr.at[w, k - 1], (pc, m)).wait_recv()

    def go1(w, k):
        z_wait(w, k)
        s1(w, k, 0).start()
        s1(w, k, 1).start()

    def go2(w, k):
        s1_wait(w, k, 0)
        s1_wait(w, k, 1)
        s2(w, k, 0).start()
        s2(w, k, 1).start()

    def go3(w, k):
        s2_wait(w, k, 0)
        s2_wait(w, k, 1)
        core(w, k).start()

    def own(w):
        return pltpu.make_async_copy(shards[w], part(w, m, every, every, 0, 0, 192), load.at[w])

    def bias_copy(k):
        return remote(bias_in, bias.at[m], bs.at[k - 1], br.at[k - 1], (d, other_z(m, k)))

    def bias_wait(k):
        here = bias.at[other_z(m, k)]
        remote(here, here, bs.at[k - 1], br.at[k - 1], (d, other_z(m, k))).wait_recv()

    enter(d, m, px, py, pc)
    for k in (1, 2, 3):
        z_copy(0, k).start()
    for k in (1, 2, 3):
        bias_copy(k).start()
    for w in range(3):
        own(w).start()
    own_bias = pltpu.make_async_copy(bias_in, bias.at[m], load.at[3])
    own_bias.start()

    def norm(values, gain, shift):
        center = values - jnp.mean(values, axis=-1, keepdims=True)
        inverse = lax.rsqrt(jnp.mean(center * center, axis=-1, keepdims=True) + EPS)
        return center * inverse * gain + shift

    n1_s[...] = norm(x_ref[...].astype(F32), vec_ref[0:1], vec_ref[1:2]).astype(BF)
    save = [pltpu.make_async_copy(n1_s, n1_out, out.at[0])]
    save[0].start()

    go1(0, 1)
    go2(0, 1)
    go1(0, 2)
    go1(0, 3)
    for k in (1, 2, 3):
        z_copy(1, k).start()
    go3(0, 1)
    go2(0, 2)
    go2(0, 3)
    for w in range(3):
        own(w).wait()
    own_bias.wait()
    for k in (1, 2, 3):
        bias_wait(k)
    core_wait(0, 1)

    group0 = m // 2
    key_row = lax.broadcasted_iota(jnp.int32, (rows, LANES), 0)
    lane = lax.broadcasted_iota(jnp.int32, (rows, LANES), 1)
    mask_add = jnp.where(key_row < fill_ref[0], 0.0, MASKED)
    lane_half = lax.broadcasted_iota(jnp.int32, (half, LANES), 1)

    def project(g):
        rows_w = pl.ds(pl.multiple_of(g * 384, 128), 384)
        lanes = rows_w
        qb = bias[0, 1:2, lanes] + bias[1, 1:2, lanes] + bias[2, 1:2, lanes] + bias[3, 1:2, lanes]
        vb = bias[0, 2:3, lanes] + bias[1, 2:3, lanes] + bias[2, 2:3, lanes] + bias[3, 2:3, lanes]
        n1 = n1_s[...]
        q_s[:, lanes] = ((dot(n1, wa[0, 0, rows_w], NT) + qb) * (HD**-0.5)).astype(BF)
        k_s[:, lanes] = dot(n1, wa[0, 1, rows_w], NT).astype(BF)
        v_s[:, lanes] = (dot(n1, wa[1, 0, rows_w], NT) + vb).astype(BF)

    def attend(p):
        lanes = pl.ds(pl.multiple_of(p * LANES, LANES), LANES)
        kp = k_s[:, lanes].astype(F32)
        vp = v_s[:, lanes]
        keys = []
        for h in (0, 1):
            own_lane = (lane < HD) if h == 0 else (lane >= HD)
            first = HD if h == 0 else 0
            extra = jnp.where(lane == first, mask_add, jnp.where(lane < first + 4, 1.0, 0.0))
            keys.append(jnp.where(own_lane, kp, extra).astype(BF))
        for b in (0, 1):
            block = pl.ds(b * half, half)
            qp = q_s[block, lanes].astype(F32)
            mixed = []
            for h in (0, 1):
                own_lane = (lane_half < HD) if h == 0 else (lane_half >= HD)
                first = HD if h == 0 else 0
                base = jnp.where(own_lane, qp, jnp.where(lane_half == first, 1.0, 0.0))
                s = dot(base.astype(BF), keys[h], NT)
                peak = jnp.max(s, axis=-1, keepdims=True)
                e = jnp.exp(s - peak)
                total = jnp.sum(e, axis=-1, keepdims=True)
                mixed.append(dot(e.astype(BF), vp, NN) / total)
                lse = peak + jnp.log(total)
                hi = lse.astype(BF).astype(F32)
                lo = (lse - hi).astype(BF).astype(F32)
                rest = lse - hi - lo
                extra = jnp.where(
                    lane_half == first + 1, -hi, jnp.where(lane_half == first + 2, -lo, jnp.where(lane_half == first + 3, -rest, 0.0))
                )
                extra = jnp.where(lane_half == first, 1.0, extra)
                qa_s[2 * p + h, block] = jnp.where(own_lane, qp, extra).astype(BF)
            ho_s[block, lanes] = jnp.where(lane_half < HD, mixed[0], mixed[1]).astype(BF)

    project(group0)
    go3(0, 2)
    go3(0, 3)

    def first_group(j, carry):
        attend(group0 * 3 + j)
        go1(1, j + 1)
        return carry

    lax.fori_loop(0, 3, first_group, 0)
    for k in (1, 2, 3):
        z_copy(2, k).start()
    for k in (1, 2, 3):
        go2(1, k)
    core_wait(0, 2)
    core_wait(0, 3)
    project(1 - group0)

    def second_group(j, carry):
        attend((1 - group0) * 3 + j)
        go3(1, j + 1)
        go1(2, j + 1)
        return carry

    lax.fori_loop(0, 3, second_group, 0)
    for k in (1, 2, 3):
        go2(2, k)
    pairs = ((qa_s, qa_out), (k_s, k_out), (v_s, v_out), (ho_s, ho_out))
    for i, (a, b) in enumerate(pairs):
        save.append(pltpu.make_async_copy(a, b, out.at[1 + i]))
        save[-1].start()
    r1 = x_ref[...].astype(F32) + dot(ho_s[...], wa[1, 1], NN) + vec_ref[2:3]
    r1_s[...] = r1
    n2_s[...] = norm(r1, vec_ref[3:4], vec_ref[4:5]).astype(BF)
    acc[...] = r1 + vec_ref[5:6]
    more = ((r1_s, r1_out), (n2_s, n2_out), (wa, wa_out))
    for i, (a, b) in enumerate(more):
        save.append(pltpu.make_async_copy(a, b, out.at[5 + i]))
        save[-1].start()
    for k in (1, 2, 3):
        go3(2, k)

    def feed(k, carry):
        mk = other_z(m, k)

        @pl.when(k > 0)
        def _():
            core_wait(1, k)
            core_wait(2, k)

        def up(n, inner):
            cols = pl.ds(pl.multiple_of(n * 256, 256), 256)
            w = wu[mk, :, :, :, cols].reshape(768, 256)
            v = dot(n2_s[...], w, NN) + bias[mk, 0:1, cols]
            sq = v * v
            t = jnp.tanh(v * (GELU_A + GELU_A * GELU_B * sq))
            hid_s[mk, :, cols] = (0.5 * v * (1.0 + t)).astype(BF)
            slope = 0.5 * (1.0 + t) + 0.5 * v * (1.0 - t * t) * (GELU_A + 3.0 * GELU_A * GELU_B * sq)
            gp_s[mk, :, cols] = slope.astype(BF)
            return inner

        lax.fori_loop(0, 3, up, 0)

        def down(n, inner):
            cols = pl.ds(pl.multiple_of(n * 256, 256), 256)
            w = wd[mk, :, :, :, cols].reshape(768, 256)
            acc[:, cols] += dot(hid_s[mk], w, NN)
            return inner

        lax.fori_loop(0, 3, down, 0)
        return carry

    lax.fori_loop(0, 4, feed, 0)
    lo_s[...] = acc[...].astype(BF)
    last = ((hid_s, hid_out), (gp_s, gp_out), (wu, wu_out), (wd, wd_out), (lo_s, layer_out))
    for i, (a, b) in enumerate(last):
        save.append(pltpu.make_async_copy(a, b, out.at[8 + i]))
        save[-1].start()
    for one in save:
        one.wait()
    for k in (1, 2, 3):
        bias_copy(k).wait_send()
    for w in range(3):
        for k in (1, 2, 3):
            z_copy(w, k).wait_send()
            for h in (0, 1):
                s1(w, k, h).wait_send()
                s2(w, k, h).wait_send()
            core(w, k).wait_send()


def forward_call(fill, x, wa, wu, wd, bias, vec):
    rows, width = x.shape
    any_spec = pl.BlockSpec(memory_space=pl.ANY)
    vmem = pl.BlockSpec(memory_space=pltpu.VMEM)
    flat = (rows, width)

    def hbm(shape, kind=BF):
        return jax.ShapeDtypeStruct(shape, kind)

    outs = [
        hbm(flat),
        hbm((12, rows, LANES)),
        hbm(flat),
        hbm(flat),
        hbm(flat),
        hbm(flat),
        hbm(flat),
        hbm(flat, F32),
        hbm((4, rows, 768)),
        hbm((4, rows, 768)),
        hbm((2, 2, 768, 768)),
        hbm((4, 2, 2, 192, 768)),
        hbm((4, 2, 2, 192, 768)),
    ]
    dma = pltpu.SemaphoreType.DMA
    scratch = [
        pltpu.VMEM((2, 2, 768, 768), BF),
        pltpu.VMEM((4, 2, 2, 192, 768), BF),
        pltpu.VMEM((4, 2, 2, 192, 768), BF),
        pltpu.VMEM((4, 8, 768), F32),
        pltpu.VMEM(flat, BF),
        pltpu.VMEM(flat, BF),
        pltpu.VMEM(flat, BF),
        pltpu.VMEM(flat, BF),
        pltpu.VMEM(flat, BF),
        pltpu.VMEM(flat, BF),
        pltpu.VMEM((12, rows, LANES), BF),
        pltpu.VMEM(flat, F32),
        pltpu.VMEM(flat, F32),
        pltpu.VMEM((4, rows, 768), BF),
        pltpu.VMEM((4, rows, 768), BF),
        pltpu.VMEM(flat, BF),
        dma((3, 3)),
        dma((3, 3)),
        dma((3, 3, 2)),
        dma((3, 3, 2)),
        dma((3, 3, 2)),
        dma((3, 3, 2)),
        dma((3, 3)),
        dma((3, 3)),
        dma((3,)),
        dma((3,)),
        dma((4,)),
        dma((13,)),
    ]
    return pl.pallas_call(
        forward_kernel,
        out_shape=outs,
        in_specs=[pl.BlockSpec(memory_space=pltpu.SMEM), vmem, any_spec, any_spec, any_spec, any_spec, vmem],
        out_specs=[any_spec] * len(outs),
        scratch_shapes=scratch,
        compiler_params=pltpu.CompilerParams(collective_id=0, has_side_effects=True, vmem_limit_bytes=60 << 20),
        name="forward",
    )(fill, x, wa, wu, wd, bias, vec)


def backward_kernel(
    fill_ref,
    vec_ref,
    lo_in,
    g_in,
    x_in,
    qa_in,
    k_in,
    v_in,
    ho_in,
    n1_in,
    n2_in,
    r1_in,
    hid_in,
    gp_in,
    wa_in,
    wu_in,
    wd_in,
    lo_all,
    pg_all,
    grads,
    sums,
    g_s,
    x_s,
    qa_s,
    k_s,
    v_s,
    ho_s,
    n1_s,
    n2_s,
    r1_s,
    wa,
    hid_b,
    gp_b,
    wu_b,
    wd_b,
    pre_s,
    acc,
    res_s,
    dho_s,
    dq_s,
    dk_s,
    dv_s,
    unit,
    rc,
    rx,
    ry,
    rz,
    vs0,
    vs_r,
    vs_z,
    los,
    lor,
    pgs,
    pgr,
    cs,
    cr,
    s1s,
    s1r,
    s2s,
    s2r,
    zs,
    zr,
    vss,
    vsr,
    vzs,
    vzr,
    load,
    chunk_load,
    own_sem,
):
    d, m, y, x, c, px, py, pc = place()
    rows = g_in.shape[0]
    half = rows // 2
    every = slice(None)

    def remote(src, dst, send, recv, peer):
        return pltpu.make_async_remote_copy(
            src_ref=src, dst_ref=dst, send_sem=send, recv_sem=recv, device_id=peer, device_id_type=MESH
        )

    quarter = rows // 64 * 16
    starts = [(i * quarter, quarter if i < 3 else rows - 3 * quarter) for i in range(4)]

    class Line:
        def __init__(self, own, full, send, recv):
            self.own, self.full, self.send, self.recv = own, full, send, recv

        def copy(self, up, dist, j, sending):
            step = 1 if up else -1
            begin, size = starts[j]
            source = m - step * (dist - 1) if sending else m - step * dist
            there = self.full.at[source, pl.ds(begin, size)]
            here = self.own.at[pl.ds(begin, size)] if (sending and dist == 1) else there
            i = 0 if up else 1
            return remote(here, there, self.send.at[i, dist - 1, j], self.recv.at[i, dist - 1, j], (d, m + step if sending else m - step))

        def sends(self, up, dist):
            return ((m >= dist - 1) & (m <= 2)) if up else ((m <= 4 - dist) & (m >= 1))

        def gets(self, up, dist):
            return (m >= dist) if up else (m <= 3 - dist)

        def begin(self):
            for j in range(4):
                for up in (True, False):
                    @pl.when(self.sends(up, 1))
                    def _(up=up, j=j):
                        self.copy(up, 1, j, True).start()

        def relay(self, dist, j):
            for up in (True, False):
                @pl.when(self.gets(up, dist))
                def _(up=up):
                    self.copy(up, dist, j, False).wait_recv()

                if dist < 3:
                    @pl.when(self.sends(up, dist + 1))
                    def _(up=up):
                        self.copy(up, dist + 1, j, True).start()

        def finish(self):
            for dist in (1, 2, 3):
                for j in range(4):
                    for up in (True, False):
                        @pl.when(self.sends(up, dist))
                        def _(up=up, dist=dist, j=j):
                            self.copy(up, dist, j, True).wait_send()

    def core_send(a, u):
        return remote(unit.at[a, u, every, every, 1 - c], rc.at[a, u], cs.at[a, u], cr.at[a, u], (pc, m))

    def s1(a, u, h):
        if h == 0:
            return remote(unit.at[a, u, every, 1 - x, c, pl.ds(0, 48)], rx.at[a, u, 0], s1s.at[a, u, 0], s1r.at[a, u, 0], (px, m))
        return remote(unit.at[a, u, 1 - y, every, c, pl.ds(48, 48)], rx.at[a, u, 1], s1s.at[a, u, 1], s1r.at[a, u, 1], (py, m))

    def s2(a, u, h):
        if h == 0:
            return remote(unit.at[a, u, 1 - y, x, c, pl.ds(0, 48)], ry.at[a, u, 0], s2s.at[a, u, 0], s2r.at[a, u, 0], (py, m))
        return remote(unit.at[a, u, y, 1 - x, c, pl.ds(48, 48)], ry.at[a, u, 1], s2s.at[a, u, 1], s2r.at[a, u, 1], (px, m))

    def z_send(a, u):
        return remote(unit.at[a, u, y, x, c], rz.at[a, u - 1], zs.at[a, u - 1], zr.at[a, u - 1], (d, other_z(m, u)))

    def go1(a, u):
        core_send(a, u).wait_recv()
        unit[a, u, :, :, c] = (unit[a, u, :, :, c].astype(F32) + rc[a, u].astype(F32)).astype(BF)
        s1(a, u, 0).start()
        s1(a, u, 1).start()

    def go2(a, u):
        s1(a, u, 0).wait_recv()
        unit[a, u, :, x, c, 0:48] = (unit[a, u, :, x, c, 0:48].astype(F32) + rx[a, u, 0].astype(F32)).astype(BF)
        s2(a, u, 0).start()
        s1(a, u, 1).wait_recv()
        unit[a, u, y, :, c, 48:96] = (unit[a, u, y, :, c, 48:96].astype(F32) + rx[a, u, 1].astype(F32)).astype(BF)
        s2(a, u, 1).start()

    def go3(a, u):
        for h in (0, 1):
            s2(a, u, h).wait_recv()
            part = pl.ds(48 * h, 48)
            unit[a, u, y, x, c, part] = (unit[a, u, y, x, c, part].astype(F32) + ry[a, u, h].astype(F32)).astype(BF)

        @pl.when(u > 0)
        def _():
            z_send(a, u).start()

    def go4(a):
        total = unit[a, 0, y, x, c].astype(F32)
        for k in (1, 2, 3):
            z_send(a, k).wait_recv()
            total = total + rz[a, k - 1].astype(F32)
        grads[a] = total

    def copies(i):
        pairs = (
            (g_in, g_s),
            (n2_in, n2_s),
            (r1_in, r1_s),
            (ho_in, ho_s),
            (wa_in, wa),
            (qa_in, qa_s),
            (k_in, k_s),
            (v_in, v_s),
            (n1_in, n1_s),
            (x_in, x_s),
        )
        return pltpu.make_async_copy(pairs[i][0], pairs[i][1], load.at[i])

    def chunk(k):
        slot = k % 2
        mk = other_z(m, 3 - k)
        pairs = ((wd_in, wd_b), (gp_in, gp_b), (hid_in, hid_b), (wu_in, wu_b))
        return [pltpu.make_async_copy(a.at[mk], b.at[slot], chunk_load.at[i, slot]) for i, (a, b) in enumerate(pairs)]

    line_lo = Line(lo_in, lo_all, los, lor)
    line_pg = Line(dho_s, pg_all, pgs, pgr)

    copies(0).start()
    for one in chunk(0):
        one.start()
    enter(d, m, px, py, pc)
    line_lo.begin()
    own_lo = pltpu.make_async_copy(lo_in, lo_all.at[m], own_sem.at[0])
    own_lo.start()
    for i in range(1, 10):
        copies(i).start()
    copies(0).wait()
    copies(1).wait()
    sums_row = jnp.zeros((1, 768), F32)
    for i in range(vs0.shape[0]):
        vs0[i : i + 1] = sums_row
    acc[...] = jnp.zeros_like(acc)

    def feed(k, carry):
        slot = k % 2
        u = 3 - k
        mk = other_z(m, u)

        @pl.when(k < 3)
        def _():
            for one in chunk(k + 1):
                one.start()

        for one in chunk(k):
            one.wait()

        def first(n, inner):
            cols = pl.ds(pl.multiple_of(n * 256, 256), 256)
            hg = dot(g_s[...], wd_b[slot, cols], NT)
            low = (hg * gp_b[slot, :, cols].astype(F32)).astype(BF)
            pre_s[:, cols] = low
            vs0[pl.ds(8 + mk, 1), cols] = jnp.sum(low.astype(F32), axis=0, keepdims=True)
            return inner

        lax.fori_loop(0, 3, first, 0)

        def second(n, inner):
            cols = pl.ds(pl.multiple_of(n * 384, 128), 384)
            unit[0, u, n] = dot(g_s[:, cols], hid_b[slot], TN).astype(BF).reshape(2, 2, 96, 768)
            unit[1, u, n] = dot(n2_s[:, cols], pre_s[...], TN).astype(BF).reshape(2, 2, 96, 768)
            return inner

        lax.fori_loop(0, 2, second, 0)
        core_send(0, u).start()
        core_send(1, u).start()

        def third(n, inner):
            cols = pl.ds(pl.multiple_of(n * 256, 256), 256)
            acc[:, cols] += dot(pre_s[...], wu_b[slot, cols], NT)
            return inner

        lax.fori_loop(0, 3, third, 0)
        go1(0, u)
        go1(1, u)
        return carry

    lax.fori_loop(0, 4, feed, 0)
    for j in range(4):
        line_lo.relay(1, j)

    def norm_back(values, upstream, gain):
        center = values - jnp.mean(values, axis=-1, keepdims=True)
        inverse = lax.rsqrt(jnp.mean(center * center, axis=-1, keepdims=True) + EPS)
        n = center * inverse
        scaled = upstream * gain
        result = inverse * (
            scaled - jnp.mean(scaled, axis=-1, keepdims=True) - n * jnp.mean(scaled * n, axis=-1, keepdims=True)
        )
        gain_part = jnp.sum(upstream * n, axis=0, keepdims=True)
        return result, gain_part, jnp.sum(upstream, axis=0, keepdims=True)

    for i in (2, 3, 4):
        copies(i).wait()

    def second_norm(i, carry):
        block = pl.ds(pl.multiple_of(i * 32, 32), 32)
        upstream = acc[block]
        through, gain_part, shift_part = norm_back(r1_s[block], upstream, vec_ref[3:4])
        g = g_s[block].astype(F32)
        res = g + through
        r1_s[block] = res
        res_s[block] = res.astype(BF)
        parts = (gain_part, shift_part, jnp.sum(res, axis=0, keepdims=True), jnp.sum(g, axis=0, keepdims=True))
        return tuple(a + b for a, b in zip(carry, parts))

    zero = jnp.zeros((1, 768), F32)
    n2g, n2s, ob, db = lax.fori_loop(0, rows // 32, second_norm, (zero, zero, zero, zero))
    vs0[2:3] = ob
    vs0[3:4] = n2g
    vs0[4:5] = n2s
    vs0[5:6] = db

    def heads_grad(n, carry):
        cols = pl.ds(pl.multiple_of(n * 256, 256), 256)
        dho_s[:, cols] = dot(res_s[...], wa[1, 1, cols], NT).astype(BF)
        return carry

    lax.fori_loop(0, 3, heads_grad, 0)
    for i in (5, 6, 7):
        copies(i).wait()

    key_row = lax.broadcasted_iota(jnp.int32, (rows, LANES), 0)
    lane = lax.broadcasted_iota(jnp.int32, (rows, LANES), 1)
    mask_add = jnp.where(key_row < fill_ref[0], 0.0, MASKED)
    lane_half = lax.broadcasted_iota(jnp.int32, (half, LANES), 1)
    lane_turned = lax.broadcasted_iota(jnp.int32, (LANES, rows), 0)

    def attend(p):
        lanes = pl.ds(pl.multiple_of(p * LANES, LANES), LANES)
        kp = k_s[:, lanes].astype(F32)
        vp = v_s[:, lanes].astype(F32)
        dop = dho_s[:, lanes]
        dof = dop.astype(F32)
        both = dof * ho_s[:, lanes].astype(F32)
        ups = []
        for h in (0, 1):
            own_lane = (lane < HD) if h == 0 else (lane >= HD)
            first = HD if h == 0 else 0
            center = jnp.sum(jnp.where(own_lane, both, 0.0), axis=-1, keepdims=True)
            hi = center.astype(BF).astype(F32)
            lo = (center - hi).astype(BF).astype(F32)
            rest = center - hi - lo
            extra = jnp.where(lane == first, -hi, jnp.where(lane == first + 1, -lo, jnp.where(lane == first + 2, -rest, 0.0)))
            ups.append(jnp.where(own_lane, dof, extra).astype(BF))
        turned = [None, None]
        for b in (0, 1):
            block = slice(b * half, (b + 1) * half)
            dks, dvs = [], []
            for h in (0, 1):
                own_lane = (lane_half < HD) if h == 0 else (lane_half >= HD)
                first = HD if h == 0 else 0
                extra = jnp.where(lane_half == first, mask_add[block], jnp.where(lane_half < first + 4, 1.0, 0.0))
                keys = jnp.where(own_lane, kp[block], extra).astype(BF)
                values = jnp.where(own_lane, vp[block], jnp.where(lane_half < first + 3, 1.0, 0.0)).astype(BF)
                qa = qa_s[2 * p + h]
                probs = jnp.exp(dot(keys, qa, NT))
                dvs.append(dot(probs.astype(BF), dop, NN))
                ds = (probs * dot(values, ups[h], NT)).astype(BF)
                dks.append(dot(ds, qa, NN))
                t = dot(keys, ds, TN)
                turned[h] = t if b == 0 else turned[h] + t
            here = pl.ds(b * half, half)
            dk_s[here, lanes] = jnp.where(lane_half < HD, dks[0], dks[1]).astype(BF)
            dv_s[here, lanes] = jnp.where(lane_half < HD, dvs[0], dvs[1]).astype(BF)
        dq = jnp.where(lane_turned < HD, turned[0], turned[1])
        dq_s[:, lanes] = (jnp.transpose(dq) * (HD**-0.5)).astype(BF)

    def pair(p, carry):
        attend(p)

        @pl.when(p < 4)
        def _():
            go2(0, 3 - p)
            go2(1, 3 - p)

        @pl.when(p >= 2)
        def _():
            go3(0, 5 - p)
            go3(1, 5 - p)

        for j in range(4):
            @pl.when(p == j + 1)
            def _(j=j):
                line_lo.relay(2, j)

        return carry

    lax.fori_loop(0, 6, pair, 0)
    vs0[6:7] = jnp.sum(dq_s[...].astype(F32), axis=0, keepdims=True)
    vs0[7:8] = jnp.sum(dv_s[...].astype(F32), axis=0, keepdims=True)
    copies(8).wait()
    copies(9).wait()

    def last_product(n, carry):
        cols = pl.ds(pl.multiple_of(n * 256, 256), 256)
        acc[:, cols] = (
            dot(dq_s[...], wa[0, 0, :, cols], NN) + dot(dk_s[...], wa[0, 1, :, cols], NN) + dot(dv_s[...], wa[1, 0, :, cols], NN)
        )
        return carry

    lax.fori_loop(0, 3, last_product, 0)

    def first_norm(i, carry):
        block = pl.ds(pl.multiple_of(i * 32, 32), 32)
        through, gain_part, shift_part = norm_back(x_s[block].astype(F32), acc[block], vec_ref[0:1])
        dho_s[block] = (r1_s[block] + through).astype(BF)
        return tuple(a + b for a, b in zip(carry, (gain_part, shift_part)))

    n1g, n1s = lax.fori_loop(0, rows // 32, first_norm, (zero, zero))
    vs0[0:1] = n1g
    vs0[1:2] = n1s
    line_pg.begin()
    own_pg = pltpu.make_async_copy(dho_s, pg_all.at[m], own_sem.at[1])
    own_pg.start()

    lane_tile = lax.broadcasted_iota(jnp.int32, (384, LANES), 1)

    def turn(v):
        return pltpu.roll(v, HD, 1)

    def attention_grads(e, carry):
        def tile(n, inner):
            cols = pl.ds(pl.multiple_of(n * 384, 128), 384)
            heads = pl.ds(pl.multiple_of(e * 384, 128), 384)
            n1 = n1_s[:, cols]
            q, k, v = [dot(n1, t[:, heads], TN) for t in (dq_s, dk_s, dv_s)]
            o = dot(res_s[:, cols], ho_s[:, heads], TN)

            def block(t, i):
                return t[:, i * LANES : (i + 1) * LANES]

            def low(a, b):
                return jnp.where(lane_tile < HD, block(a, 1), turn(block(b, 1)))

            def high(a, b):
                return jnp.where(lane_tile < HD, turn(block(a, 1)), block(b, 1))

            even = [block(q, 0), low(q, k), block(k, 0), block(v, 0), low(v, o), block(o, 0)]
            odd = [high(q, k), block(q, 2), block(k, 2), high(v, o), block(v, 2), block(o, 2)]
            ue, uo = other_z(m, 2 * e), other_z(m, 2 * e + 1)
            for i in range(6):
                lanes = slice(i * LANES, (i + 1) * LANES)
                unit[2, ue, n, :, :, :, lanes] = even[i].astype(BF).reshape(2, 2, 96, LANES)
                unit[2, uo, n, :, :, :, lanes] = odd[i].astype(BF).reshape(2, 2, 96, LANES)
            return inner

        lax.fori_loop(0, 2, tile, 0)
        core_send(2, other_z(m, 2 * e)).start()
        core_send(2, other_z(m, 2 * e + 1)).start()
        return carry

    lax.fori_loop(0, 2, attention_grads, 0)

    def run(stage, start=3):
        def body(i, carry):
            stage(2, 3 - i)
            return carry

        lax.fori_loop(0, 4, body, 0)

    run(go1)

    peers = ((pc, m), (px, m), (py, m))

    def small(i):
        return remote(vs0, vs_r.at[i], vss.at[i], vsr.at[i], peers[i])

    for i in range(3):
        small(i).start()
        small(i).wait()
        vs0[...] += vs_r[i]

    def small_z(k):
        return remote(vs0, vs_z.at[k - 1], vzs.at[k - 1], vzr.at[k - 1], (d, other_z(m, k)))

    for k in (1, 2, 3):
        small_z(k).start()
    run(go2)
    run(go3)
    for j in range(4):
        line_pg.relay(1, j)
    for j in range(4):
        line_lo.relay(3, j)
    for j in range(4):
        line_pg.relay(2, j)
    go4(0)
    go4(1)
    go4(2)
    total = vs0[...]
    for k in (1, 2, 3):
        small_z(k).wait_recv()
        total = total + vs_z[k - 1]
    sums[...] = total
    for j in range(4):
        line_pg.relay(3, j)
    line_lo.finish()
    line_pg.finish()
    own_lo.wait()
    own_pg.wait()
    for k in (1, 2, 3):
        small_z(k).wait_send()
    for a in range(3):
        for u in range(4):
            core_send(a, u).wait_send()
            for h in (0, 1):
                s1(a, u, h).wait_send()
                s2(a, u, h).wait_send()
            if u > 0:
                z_send(a, u).wait_send()


def backward_call(fill, vec, lo, g, x, qa, k, v, ho, n1, n2, r1, hid, gp, wa, wu, wd):
    rows, width = x.shape
    any_spec = pl.BlockSpec(memory_space=pl.ANY)
    vmem = pl.BlockSpec(memory_space=pltpu.VMEM)
    flat = (rows, width)
    outs = [
        jax.ShapeDtypeStruct((4, rows, width), BF),
        jax.ShapeDtypeStruct((4, rows, width), BF),
        jax.ShapeDtypeStruct((3, 96, 768), F32),
        jax.ShapeDtypeStruct((16, width), F32),
    ]
    dma = pltpu.SemaphoreType.DMA
    scratch = [
        pltpu.VMEM(flat, BF),
        pltpu.VMEM(flat, BF),
        pltpu.VMEM((12, rows, LANES), BF),
        pltpu.VMEM(flat, BF),
        pltpu.VMEM(flat, BF),
        pltpu.VMEM(flat, BF),
        pltpu.VMEM(flat, BF),
        pltpu.VMEM(flat, BF),
        pltpu.VMEM(flat, F32),
        pltpu.VMEM((2, 2, 768, 768), BF),
        pltpu.VMEM((2, rows, 768), BF),
        pltpu.VMEM((2, rows, 768), BF),
        pltpu.VMEM((2, 768, 768), BF),
        pltpu.VMEM((2, 768, 768), BF),
        pltpu.VMEM(flat, BF),
        pltpu.VMEM(flat, F32),
        pltpu.VMEM(flat, BF),
        pltpu.VMEM(flat, BF),
        pltpu.VMEM(flat, BF),
        pltpu.VMEM(flat, BF),
        pltpu.VMEM(flat, BF),
        pltpu.VMEM((3, 4, 2, 2, 2, 96, 768), BF),
        pltpu.VMEM((3, 4, 2, 2, 96, 768), BF),
        pltpu.VMEM((3, 4, 2, 2, 48, 768), BF),
        pltpu.VMEM((3, 4, 2, 48, 768), BF),
        pltpu.VMEM((3, 3, 96, 768), BF),
        pltpu.VMEM((16, width), F32),
        pltpu.VMEM((3, 16, width), F32),
        pltpu.VMEM((3, 16, width), F32),
        dma((2, 3, 4)),
        dma((2, 3, 4)),
        dma((2, 3, 4)),
        dma((2, 3, 4)),
        dma((3, 4)),
        dma((3, 4)),
        dma((3, 4, 2)),
        dma((3, 4, 2)),
        dma((3, 4, 2)),
        dma((3, 4, 2)),
        dma((3, 3)),
        dma((3, 3)),
        dma((3,)),
        dma((3,)),
        dma((3,)),
        dma((3,)),
        dma((10,)),
        dma((4, 2)),
        dma((2,)),
    ]
    return pl.pallas_call(
        backward_kernel,
        out_shape=outs,
        in_specs=[pl.BlockSpec(memory_space=pltpu.SMEM), vmem] + [any_spec] * 15,
        out_specs=[any_spec, any_spec, vmem, vmem],
        scratch_shapes=scratch,
        compiler_params=pltpu.CompilerParams(collective_id=1, has_side_effects=True, vmem_limit_bytes=62 << 20),
        name="backward",
    )(fill, vec, lo, g, x, qa, k, v, ho, n1, n2, r1, hid, gp, wa, wu, wd)


def prepare(patches, fill_lengths, cotangent, norm1_gain, norm1_shift, w_qkv, qv_bias, w_out, out_bias, norm2_gain, norm2_shift, w_up, up_bias, w_down, down_bias):
    m = lax.axis_index("mp")
    length, width = patches.shape[1:]
    rows = -(-length // 32) * 32
    pad = ((0, rows - length), (0, 0))
    x = jnp.pad(lax.dynamic_index_in_dim(patches, m, 0, keepdims=False), pad)
    cot = jnp.pad(lax.dynamic_index_in_dim(cotangent, m, 0, keepdims=False), pad)
    fill = lax.dynamic_slice(fill_lengths, (m,), (1,))
    wa = jnp.concatenate([jnp.transpose(w_qkv, (1, 2, 0)).reshape(576, width), w_out], axis=0)
    wa = wa.reshape(2, 2, 192, width)
    wu = w_up.reshape(2, 2, 192, width)
    wd = w_down.reshape(2, 2, 192, width)
    placed = lax.dynamic_update_slice(jnp.zeros((2, width), F32), qv_bias, (0, m * 192))
    bias = jnp.concatenate([up_bias[None], placed, jnp.zeros((5, width), F32)], axis=0)
    zero = jnp.zeros_like(norm1_gain)
    vec = jnp.stack([norm1_gain, norm1_shift, out_bias, norm2_gain, norm2_shift, down_bias, zero, zero])
    return x, cot, fill, wa, wu, wd, bias, vec


def one_item(*args):
    length, width = args[0].shape[1:]
    x, cot, fill, wa, wu, wd, bias, vec = prepare(*args)
    lo, qa, k, v, ho, n1, n2, r1, hid, gp, wa, wu, wd = forward_call(fill, x, wa, wu, wd, bias, vec)
    wu = wu.reshape(4, width, 768)
    wd = wd.reshape(4, 768, width)
    lo_all, pg_all, grads, sums = backward_call(fill, vec, lo, cot, x, qa, k, v, ho, n1, n2, r1, hid, gp, wa, wu, wd)
    d = lax.axis_index("dp")
    m = lax.axis_index("mp")
    layer_out = lo_all[:, :length]
    patches_grad = pg_all[:, :length].astype(F32)
    g = grads[2]
    is_even = m % 2 == 0

    def pick(even, odd):
        def join(parts):
            return jnp.concatenate([g[:, a:b] for a, b in parts], axis=1)

        return jnp.where(is_even, join(even), join(odd))

    q_grad = pick([(0, 192)], [(0, 64), (128, 256)])
    k_grad = pick([(256, 384), (192, 256)], [(64, 128), (256, 384)])
    v_grad = pick([(384, 576)], [(384, 448), (512, 640)])
    o_grad = pick([(640, 768), (576, 640)], [(448, 512), (640, 768)])
    mine = lax.dynamic_slice(sums, (0, d * 96), (8, 96))
    qv = lax.dynamic_slice(sums, (6, m * 192 + d * 24), (2, 24))
    up_grad = lax.dynamic_slice(sums, (8 + m, d * 96), (1, 96))[0]
    return (
        layer_out,
        patches_grad,
        mine[0],
        mine[1],
        jnp.stack([q_grad, k_grad, v_grad], axis=1),
        qv,
        o_grad.T,
        mine[2],
        mine[3],
        mine[4],
        grads[1],
        up_grad,
        grads[0].T,
        mine[5],
    )


def normalize(values, gain, shift):
    center = values - jnp.mean(values, axis=-1, keepdims=True)
    inverse = lax.rsqrt(jnp.mean(center * center, axis=-1, keepdims=True) + EPS)
    unit = center * inverse
    return (unit, inverse, unit * gain + shift)


def normalize_back(upstream, unit, inverse, gain):
    gain_grad = jnp.sum(upstream * unit, axis=(0, 1))
    shift_grad = jnp.sum(upstream, axis=(0, 1))
    scaled = upstream * gain
    result = inverse * (
        scaled
        - jnp.mean(scaled, axis=-1, keepdims=True)
        - unit * jnp.mean(scaled * unit, axis=-1, keepdims=True)
    )
    return (gain_grad, shift_grad, result)


def split_heads(rows):
    return rows.reshape(rows.shape[0], rows.shape[1] // HD, HD)


def masked_scores(queries, keyset, usable):
    scores = jnp.einsum("qhd,khd->hqk", queries, keyset, preferred_element_type=jnp.float32)
    return jnp.where(usable[None, None, :], scores, -1e30)


def attend_items(operands):
    query_rows, key_rows, value_rows, usable = operands
    scores = masked_scores(split_heads(query_rows), split_heads(key_rows), usable)
    peak = jnp.max(scores, axis=-1, keepdims=True)
    expsum = jnp.exp(scores - peak)
    total = jnp.sum(expsum, axis=-1, keepdims=True)
    weights = (expsum / total).astype(jnp.bfloat16)
    mixed = jnp.einsum(
        "hqk,khd->qhd", weights, split_heads(value_rows), preferred_element_type=jnp.float32
    )
    return (
        mixed.reshape(query_rows.shape).astype(jnp.bfloat16),
        peak[..., 0] + jnp.log(total[..., 0]),
    )


def attend_items_back(operands):
    query_rows, key_rows, value_rows, usable, logsum, upstream = operands
    queries = split_heads(query_rows)
    keyset = split_heads(key_rows)
    scores = masked_scores(queries, keyset, usable)
    probs = jnp.exp(scores - logsum[..., None])
    weights = probs.astype(jnp.bfloat16)
    grad_heads = split_heads(upstream)
    value_grad = jnp.einsum("hqk,qhd->khd", weights, grad_heads, preferred_element_type=jnp.float32)
    prob_grad = jnp.einsum(
        "qhd,khd->hqk", grad_heads, split_heads(value_rows), preferred_element_type=jnp.float32
    )
    center = jnp.sum(probs * prob_grad, axis=-1, keepdims=True)
    score_grad = (probs * (prob_grad - center)).astype(jnp.bfloat16)
    query_grad = jnp.einsum("hqk,khd->qhd", score_grad, keyset, preferred_element_type=jnp.float32)
    key_grad = jnp.einsum("hqk,qhd->khd", score_grad, queries, preferred_element_type=jnp.float32)
    shape = query_rows.shape
    return (
        query_grad.reshape(shape).astype(jnp.bfloat16),
        key_grad.reshape(shape).astype(jnp.bfloat16),
        value_grad.reshape(shape).astype(jnp.bfloat16),
    )


def shards(
    patches,
    fill_lengths,
    cotangent,
    norm1_gain,
    norm1_shift,
    w_qkv,
    qv_bias,
    w_out,
    out_bias,
    norm2_gain,
    norm2_shift,
    w_up,
    up_bias,
    w_down,
    down_bias,
):
    scaling = HD ** (-0.5)
    seq_len = patches.shape[1]
    inputs = patches.astype(jnp.float32)
    unit1, inverse1, normed1_full = normalize(inputs, norm1_gain, norm1_shift)
    normed1 = normed1_full.astype(jnp.bfloat16)
    projected = jnp.einsum("isd,dtc->istc", normed1, w_qkv, preferred_element_type=jnp.float32)
    queries = ((projected[:, :, 0] + qv_bias[0]) * scaling).astype(jnp.bfloat16)
    key_rows = projected[:, :, 1].astype(jnp.bfloat16)
    value_rows = (projected[:, :, 2] + qv_bias[1]).astype(jnp.bfloat16)
    usable = jnp.arange(seq_len, dtype=jnp.int32)[None, :] < fill_lengths[:, None]
    heads_out, logsum = lax.map(attend_items, (queries, key_rows, value_rows, usable))
    partial_attn = jnp.einsum("isc,cd->isd", heads_out, w_out, preferred_element_type=jnp.float32)
    attention = lax.psum(partial_attn, "mp")
    residual1 = inputs + attention + out_bias
    unit2, inverse2, normed2_full = normalize(residual1, norm2_gain, norm2_shift)
    normed2 = normed2_full.astype(jnp.bfloat16)
    preact = jnp.einsum("isd,df->isf", normed2, w_up, preferred_element_type=jnp.float32) + up_bias
    activated, gelu_back = jax.vjp(jax.nn.gelu, preact)
    hidden = activated.astype(jnp.bfloat16)
    partial_ff = jnp.einsum("isf,fd->isd", hidden, w_down, preferred_element_type=jnp.float32)
    feedforward = lax.psum(partial_ff, "mp")
    layer_out = (residual1 + feedforward + down_bias).astype(jnp.bfloat16)
    upstream = cotangent.astype(jnp.float32)
    down_bias_grad = jnp.sum(upstream, axis=(0, 1))
    w_down_grad = jnp.einsum("isf,isd->fd", hidden, cotangent, preferred_element_type=jnp.float32)
    hidden_grad = jnp.einsum("isd,fd->isf", cotangent, w_down, preferred_element_type=jnp.float32)
    preact_grad = gelu_back(hidden_grad)[0].astype(jnp.bfloat16)
    up_bias_grad = jnp.sum(preact_grad.astype(jnp.float32), axis=(0, 1))
    w_up_grad = jnp.einsum("isd,isf->df", normed2, preact_grad, preferred_element_type=jnp.float32)
    partial_norm2 = jnp.einsum("isf,df->isd", preact_grad, w_up, preferred_element_type=jnp.float32)
    normed2_grad = lax.psum(partial_norm2, "mp")
    norm2_gain_grad, norm2_shift_grad, through_norm2 = normalize_back(
        normed2_grad, unit2, inverse2, norm2_gain
    )
    residual1_grad = upstream + through_norm2
    out_bias_grad = jnp.sum(residual1_grad, axis=(0, 1))
    residual_low = residual1_grad.astype(jnp.bfloat16)
    w_out_grad = jnp.einsum(
        "isc,isd->cd", heads_out, residual_low, preferred_element_type=jnp.float32
    )
    heads_grad = jnp.einsum(
        "isd,cd->isc", residual_low, w_out, preferred_element_type=jnp.float32
    ).astype(jnp.bfloat16)
    query_grad, key_grad, value_grad = lax.map(
        attend_items_back, (queries, key_rows, value_rows, usable, logsum, heads_grad)
    )
    query_scaled = query_grad * scaling
    proj_grad = jnp.stack([query_scaled, key_grad, value_grad], axis=2)
    w_qkv_grad = jnp.einsum("isd,istc->dtc", normed1, proj_grad, preferred_element_type=jnp.float32)
    qv_bias_grad = jnp.stack(
        [
            jnp.sum(query_scaled.astype(jnp.float32), axis=(0, 1)),
            jnp.sum(value_grad.astype(jnp.float32), axis=(0, 1)),
        ]
    )
    partial_norm1 = jnp.einsum(
        "istc,dtc->isd", proj_grad, w_qkv, preferred_element_type=jnp.float32
    )
    normed1_grad = lax.psum(partial_norm1, "mp")
    norm1_gain_grad, norm1_shift_grad, through_norm1 = normalize_back(
        normed1_grad, unit1, inverse1, norm1_gain
    )
    patches_grad = residual1_grad + through_norm1
    summed = (
        lax.psum_scatter(norm1_gain_grad, "dp", scatter_dimension=0, tiled=True),
        lax.psum_scatter(norm1_shift_grad, "dp", scatter_dimension=0, tiled=True),
        lax.psum_scatter(w_qkv_grad, "dp", scatter_dimension=0, tiled=True),
        lax.psum_scatter(qv_bias_grad, "dp", scatter_dimension=1, tiled=True),
        lax.psum_scatter(w_out_grad, "dp", scatter_dimension=1, tiled=True),
        lax.psum_scatter(out_bias_grad, "dp", scatter_dimension=0, tiled=True),
        lax.psum_scatter(w_up_grad, "dp", scatter_dimension=0, tiled=True),
        lax.psum_scatter(up_bias_grad, "dp", scatter_dimension=0, tiled=True),
        lax.psum_scatter(w_down_grad, "dp", scatter_dimension=1, tiled=True),
        lax.psum_scatter(down_bias_grad, "dp", scatter_dimension=0, tiled=True),
        lax.psum_scatter(norm2_gain_grad, "dp", scatter_dimension=0, tiled=True),
        lax.psum_scatter(norm2_shift_grad, "dp", scatter_dimension=0, tiled=True),
    )
    return (
        layer_out,
        patches_grad,
        summed[0],
        summed[1],
        summed[2],
        summed[3],
        summed[4],
        summed[5],
        summed[10],
        summed[11],
        summed[6],
        summed[7],
        summed[8],
        summed[9],
    )


def solution(mesh):
    body = one_item if (mesh.shape['dp'], mesh.shape['mp']) == (8, 4) else shards
    return jax.shard_map(
        body,
        mesh=mesh,
        in_specs=(
            P("dp", None, None),
            P("dp"),
            P("dp", None, None),
            P(),
            P(),
            P(None, None, "mp"),
            P(None, "mp"),
            P("mp", None),
            P(),
            P(),
            P(),
            P(None, "mp"),
            P("mp"),
            P("mp", None),
            P(),
        ),
        out_specs=(
            P("dp", None, None),
            P("dp", None, None),
            P("dp"),
            P("dp"),
            P("dp", None, "mp"),
            P(None, ("mp", "dp")),
            P("mp", "dp"),
            P("dp"),
            P("dp"),
            P("dp"),
            P("dp", "mp"),
            P(("mp", "dp")),
            P("mp", "dp"),
            P("dp"),
        ),
        check_vma=False,
    )
```

```python
import functools
import jax
import jax.numpy as jnp
from jax import lax
from jax.experimental import pallas as pl
from jax.experimental.pallas import tpu as pltpu
from jax.sharding import PartitionSpec as P

MESH = pl.DeviceIdType.MESH
BF = jnp.bfloat16
F32 = jnp.float32
HD = 64
LANES = 128
EPS = 1e-6
MASKED = -1e30
GELU_A = 0.7978845608028654
GELU_B = 0.044715

NN = (((1,), (0,)), ((), ()))
NT = (((1,), (1,)), ((), ()))
TN = (((0,), (0,)), ((), ()))


def dot(a, b, dims):
    return lax.dot_general(a, b, dims, preferred_element_type=F32)


def place():
    d = lax.axis_index("dp")
    m = lax.axis_index("mp")
    y, x, c = d // 4, (d // 2) % 2, d % 2
    px = d + 2 - 4 * x
    py = d + 4 - 8 * y
    pc = d + 1 - 2 * c
    return d, m, y, x, c, px, py, pc


def other_z(m, k):
    low = (m % 2 + k % 2) % 2
    high = (m // 2 + k // 2) % 2
    return 2 * high + low


def enter(d, m, px, py, pc):
    barrier = pltpu.get_barrier_semaphore()
    for peer in ((px, m), (py, m), (pc, m)):
        pl.semaphore_signal(barrier, inc=1, device_id=peer, device_id_type=MESH)
    for k in (1, 2, 3):
        pl.semaphore_signal(barrier, inc=1, device_id=(d, other_z(m, k)), device_id_type=MESH)
    pl.semaphore_wait(barrier, 6)


def forward_kernel(
    fill_ref,
    x_ref,
    wq_in,
    wo_in,
    wu_in,
    wd_in,
    qv_bias,
    up_bias,
    gain1,
    shift1,
    out_bias,
    gain2,
    shift2,
    down_bias,
    layer_out,
    qa_out,
    k_out,
    v_out,
    ho_out,
    n1_out,
    n2_out,
    r1_out,
    hid_out,
    gp_out,
    wa_out,
    wu_out,
    wd_out,
    wa,
    wu,
    wd,
    bias,
    q_s,
    k_s,
    v_s,
    ho_s,
    n1_s,
    n2_s,
    qa_s,
    r1_s,
    acc,
    hid_s,
    gp_s,
    lo_s,
    zs,
    zr,
    fs,
    s1s,
    s1r,
    s2s,
    s2r,
    cs,
    cr,
    bs,
    br,
    load,
    out,
    chunk_out,
):
    d, m, y, x, c, px, py, pc = place()
    rows = x_ref.shape[0]
    half = rows // 2

    def part(w, s, ys, xs, core, start, size):
        if w == 0:
            return wa.at[ys, xs, pl.ds(s * 192 + core * 96 + start, size)]
        full = wu if w == 1 else wd
        return full.at[s, ys, xs, pl.ds(core * 96 + start, size)]

    every = slice(None)

    def remote(src, dst, send, recv, peer):
        return pltpu.make_async_remote_copy(
            src_ref=src, dst_ref=dst, send_sem=send, recv_sem=recv, device_id=peer, device_id_type=MESH
        )

    inner = (m == 1) | (m == 2)
    k2 = 2 + ((m + 1) // 2) % 2
    k3 = 5 - k2

    def z_views(w, s):
        if w < 2:
            return (part(w, s, y, x, c, 0, 96),)
        return part(w, s, every, x, c, 0, 48), part(w, s, y, every, c, 48, 48)

    def z_copies(w, k):
        peer = (d, other_z(m, k))
        return [remote(v, v, zs.at[w, k - 1, h], zr.at[w, k - 1, h], peer) for h, v in enumerate(z_views(w, m))]

    def z_forwards(w, k):
        peer = (d, other_z(m, 1))
        views = z_views(w, other_z(m, k))
        return [remote(v, v, fs.at[w, k - 2, h], zr.at[w, 4 - k, h], peer) for h, v in enumerate(views)]

    def z_begin(w):
        for k in (1, k2):
            for one in z_copies(w, k):
                one.start()

    def z_wait(w, k):
        s = other_z(m, k)
        for h, v in enumerate(z_views(w, s)):
            remote(v, v, zs.at[w, k - 1, h], zr.at[w, k - 1, h], (d, s)).wait_recv()

    def forward(w, k):
        @pl.when(inner)
        def _():
            z_wait(w, k)
            for one in z_forwards(w, k):
                one.start()

    def arrive(w, k):
        if isinstance(k, int):
            z_wait(w, k)
        else:

            @pl.when((m == 0) | (m == 3))
            def _():
                z_wait(w, k)

    def s1(w, s, h):
        here = part(w, s, y, x, c, 48 * h, 48)
        peer = (px, m) if h == 0 else (py, m)
        return remote(here, here, s1s.at[w, s, h], s1r.at[w, s, h], peer)

    def s1_wait(w, s, h):
        here = part(w, s, y, 1 - x, c, 0, 48) if h == 0 else part(w, s, 1 - y, x, c, 48, 48)
        peer = (px, m) if h == 0 else (py, m)
        remote(here, here, s1s.at[w, s, h], s1r.at[w, s, h], peer).wait_recv()

    def s2(w, s, h):
        here = part(w, s, y, every, c, 0, 48) if h == 0 else part(w, s, every, x, c, 48, 48)
        peer = (py, m) if h == 0 else (px, m)
        return remote(here, here, s2s.at[w, s, h], s2r.at[w, s, h], peer)

    def s2_wait(w, s, h):
        here = part(w, s, 1 - y, every, c, 0, 48) if h == 0 else part(w, s, every, 1 - x, c, 48, 48)
        peer = (py, m) if h == 0 else (px, m)
        remote(here, here, s2s.at[w, s, h], s2r.at[w, s, h], peer).wait_recv()

    def core(w, s):
        here = part(w, s, every, every, c, 0, 96)
        return remote(here, here, cs.at[w, s], cr.at[w, s], (pc, m))

    def core_wait(w, k):
        s = other_z(m, k)
        here = part(w, s, every, every, 1 - c, 0, 96)
        remote(here, here, cs.at[w, s], cr.at[w, s], (pc, m)).wait_recv()

    def go1(w, k):
        s = other_z(m, k)
        arrive(w, k)
        if w < 2:
            s1(w, s, 0).start()
            s1(w, s, 1).start()
        else:
            last(s, 0).start()
            last(s, 1).start()

    def last(s, h):
        here = part(2, s, every, x, c, 0, 48) if h == 0 else part(2, s, y, every, c, 48, 48)
        peer = (px, m) if h == 0 else (py, m)
        return remote(here, here, s2s.at[2, s, h], s2r.at[2, s, h], peer)

    def last_wait(s, h):
        here = part(2, s, every, 1 - x, c, 0, 48) if h == 0 else part(2, s, 1 - y, every, c, 48, 48)
        peer = (px, m) if h == 0 else (py, m)
        remote(here, here, s2s.at[2, s, h], s2r.at[2, s, h], peer).wait_recv()

    def go2(w, k):
        s = other_z(m, k)
        s1_wait(w, s, 0)
        s2(w, s, 0).start()
        s1_wait(w, s, 1)
        s2(w, s, 1).start()

    def go3(w, k):
        s = other_z(m, k)
        wait = functools.partial(s2_wait, w) if w < 2 else last_wait
        wait(s, 0)
        wait(s, 1)
        core(w, s).start()

    def own(w):
        if w == 0:
            mine = pl.ds(m * 192, 192)
            return [pltpu.make_async_copy(wq_in.at[t], wa.at[t // 2, t % 2, mine], load.at[t]) for t in range(3)] + [
                pltpu.make_async_copy(wo_in, wa.at[1, 1, mine], load.at[3])
            ]
        src = wu_in if w == 1 else wd_in
        return [pltpu.make_async_copy(src, part(w, m, every, every, 0, 0, 192), load.at[3 + w])]

    def bias_copy(k):
        return remote(bias.at[m], bias.at[m], bs.at[k - 1], br.at[k - 1], (d, other_z(m, k)))

    def bias_wait(k):
        here = bias.at[other_z(m, k)]
        remote(here, here, bs.at[k - 1], br.at[k - 1], (d, other_z(m, k))).wait_recv()

    for w in range(3):
        for one in own(w):
            one.start()
    bias[m, 0:1] = up_bias[...].reshape(1, 768)
    bias[m, 1:3] = qv_bias[...]
    bias[m, 3:8] = jnp.zeros((5, 768), F32)
    enter(d, m, px, py, pc)
    for one in own(0):
        one.wait()
    z_begin(0)
    for k in (1, 2, 3):
        bias_copy(k).start()
    for one in own(1):
        one.wait()
    z_begin(1)

    def norm(values, gain, shift):
        center = values - jnp.mean(values, axis=-1, keepdims=True)
        inverse = lax.rsqrt(jnp.mean(center * center, axis=-1, keepdims=True) + EPS)
        return center * inverse * gain + shift

    def blocks(body):
        for i in range(rows // 32):
            body(pl.ds(i * 32, 32))

    def first_norm(block):
        n1_s[block] = norm(x_ref[block].astype(F32), gain1[...].reshape(1, 768), shift1[...].reshape(1, 768)).astype(BF)

    blocks(first_norm)
    save = [pltpu.make_async_copy(n1_s, n1_out, out.at[0])]
    save[0].start()
    for one in own(2):
        one.wait()

    go1(0, 1)
    forward(0, 3)
    forward(0, 2)
    z_begin(2)
    go1(0, k2)
    go2(0, 1)
    forward(1, 3)
    go1(0, k3)
    go1(1, 1)
    go2(0, k2)
    forward(1, 2)
    go3(0, 1)
    for k in (1, 2, 3):
        bias_wait(k)
    core_wait(0, 1)

    group0 = m // 2
    key_row = lax.broadcasted_iota(jnp.int32, (rows, LANES), 0)
    lane = lax.broadcasted_iota(jnp.int32, (rows, LANES), 1)
    mask_add = jnp.where(key_row < fill_ref[m], 0.0, MASKED)
    lane_half = lax.broadcasted_iota(jnp.int32, (half, LANES), 1)

    def project(g):
        rows_w = pl.ds(pl.multiple_of(g * 384, 128), 384)
        lanes = rows_w
        qb = bias[0, 1:2, lanes] + bias[1, 1:2, lanes] + bias[2, 1:2, lanes] + bias[3, 1:2, lanes]
        vb = bias[0, 2:3, lanes] + bias[1, 2:3, lanes] + bias[2, 2:3, lanes] + bias[3, 2:3, lanes]
        n1 = n1_s[...]
        q_s[:, lanes] = ((dot(n1, wa[0, 0, rows_w], NT) + qb) * (HD**-0.5)).astype(BF)
        k_s[:, lanes] = dot(n1, wa[0, 1, rows_w], NT).astype(BF)
        v_s[:, lanes] = (dot(n1, wa[1, 0, rows_w], NT) + vb).astype(BF)

    def attend(p):
        lanes = pl.ds(pl.multiple_of(p * LANES, LANES), LANES)
        kp = k_s[:, lanes].astype(F32)
        vp = v_s[:, lanes]
        keys = []
        for h in (0, 1):
            own_lane = (lane < HD) if h == 0 else (lane >= HD)
            first = HD if h == 0 else 0
            extra = jnp.where(lane == first, mask_add, jnp.where(lane < first + 4, 1.0, 0.0))
            keys.append(jnp.where(own_lane, kp, extra).astype(BF))
        for b in (0, 1):
            block = pl.ds(b * half, half)
            qp = q_s[block, lanes].astype(F32)
            mixed = []
            for h in (0, 1):
                own_lane = (lane_half < HD) if h == 0 else (lane_half >= HD)
                first = HD if h == 0 else 0
                base = jnp.where(own_lane, qp, jnp.where(lane_half == first, 1.0, 0.0))
                s = dot(base.astype(BF), keys[h], NT)
                peak = jnp.max(s, axis=-1, keepdims=True)
                e = jnp.exp(s - peak)
                total = jnp.sum(e, axis=-1, keepdims=True)
                mixed.append(dot(e.astype(BF), vp, NN) / total)
                lse = peak + jnp.log(total)
                hi = lse.astype(BF).astype(F32)
                lo = (lse - hi).astype(BF).astype(F32)
                rest = lse - hi - lo
                extra = jnp.where(
                    lane_half == first + 1, -hi, jnp.where(lane_half == first + 2, -lo, jnp.where(lane_half == first + 3, -rest, 0.0))
                )
                extra = jnp.where(lane_half == first, 1.0, extra)
                qa_s[2 * p + h, block] = jnp.where(own_lane, qp, extra).astype(BF)
            ho_s[block, lanes] = jnp.where(lane_half < HD, mixed[0], mixed[1]).astype(BF)

    project(group0)

    def steps(j, lists):
        for i, todo in enumerate(lists):

            @pl.when(j == i)
            def _(todo=todo):
                for stage, w, k in todo:
                    stage(w, k)

    def first_group(j, carry):
        attend(group0 * 3 + j)
        steps(
            j,
            (
                ((go2, 0, k3), (go3, 0, k2), (go1, 1, k2), (go2, 1, 1), (forward, 2, 3)),
                ((go3, 0, k3), (go1, 1, k3), (go2, 1, k2), (forward, 2, 2), (go1, 2, 1)),
                ((go3, 1, 1), (go2, 1, k3)),
            ),
        )
        return carry

    lax.fori_loop(0, 3, first_group, 0)
    core_wait(0, 2)
    core_wait(0, 3)
    save.append(pltpu.make_async_copy(wa, wa_out, out.at[7]))
    save[-1].start()
    project(1 - group0)

    def second_group(j, carry):
        attend((1 - group0) * 3 + j)
        steps(j, (((go3, 1, k2), (go1, 2, k2)), ((go3, 1, k3), (go3, 2, 1)), ((go1, 2, k3),)))
        return carry

    lax.fori_loop(0, 3, second_group, 0)
    pairs = ((qa_s, qa_out), (k_s, k_out), (v_s, v_out), (ho_s, ho_out))
    for i, (a, b) in enumerate(pairs):
        save.append(pltpu.make_async_copy(a, b, out.at[1 + i]))
        save[-1].start()

    def finish_attention(n, carry):
        cols = pl.ds(pl.multiple_of(n * 256, 256), 256)
        acc[:, cols] = dot(ho_s[...], wa[1, 1, :, cols], NN)
        return carry

    lax.fori_loop(0, 3, finish_attention, 0)

    def second_norm(block):
        r1 = x_ref[block].astype(F32) + acc[block] + out_bias[...].reshape(1, 768)
        r1_s[block] = r1
        n2_s[block] = norm(r1, gain2[...].reshape(1, 768), shift2[...].reshape(1, 768)).astype(BF)
        acc[block] = r1 + down_bias[...].reshape(1, 768)

    blocks(second_norm)
    more = ((r1_s, r1_out), (n2_s, n2_out))
    for i, (a, b) in enumerate(more):
        save.append(pltpu.make_async_copy(a, b, out.at[5 + i]))
        save[-1].start()
    go3(2, k2)

    def in_order(k):
        return k + (k // 2) * (k2 - 2) * (5 - 2 * k)

    def chunk_save(k):
        mk = other_z(m, in_order(k))
        pairs = ((wu, wu_out), (wd, wd_out), (hid_s, hid_out), (gp_s, gp_out))
        return [pltpu.make_async_copy(a.at[mk], b.at[mk], chunk_out.at[i, k]) for i, (a, b) in enumerate(pairs)]

    def feed(k, carry):
        ke = in_order(k)
        mk = other_z(m, ke)

        @pl.when(k == 1)
        def _():
            go3(2, k3)

        @pl.when(k > 0)
        def _():
            core_wait(1, ke)
            core_wait(2, ke)

        for one in chunk_save(k)[:2]:
            one.start()

        def up(n, inner):
            cols = pl.ds(pl.multiple_of(n * 256, 256), 256)
            w = wu[mk, :, :, :, cols].reshape(768, 256)
            v = dot(n2_s[...], w, NN) + bias[mk, 0:1, cols]
            sq = v * v
            t = jnp.tanh(v * (GELU_A + GELU_A * GELU_B * sq))
            hid_s[mk, :, cols] = (0.5 * v * (1.0 + t)).astype(BF)
            slope = 0.5 * (1.0 + t) + 0.5 * v * (1.0 - t * t) * (GELU_A + 3.0 * GELU_A * GELU_B * sq)
            gp_s[mk, :, cols] = slope.astype(BF)
            return inner

        lax.fori_loop(0, 3, up, 0)
        for one in chunk_save(k)[2:]:
            one.start()

        def down(n, inner):
            cols = pl.ds(pl.multiple_of(n * 256, 256), 256)
            w = wd[mk, :, :, :, cols].reshape(768, 256)
            acc[:, cols] += dot(hid_s[mk], w, NN)
            return inner

        lax.fori_loop(0, 3, down, 0)
        return carry

    lax.fori_loop(0, 4, feed, 0)
    lo_s[...] = acc[...].astype(BF)
    save.append(pltpu.make_async_copy(lo_s, layer_out, out.at[8]))
    save[-1].start()
    for one in save:
        one.wait()
    for k in range(4):
        for one in chunk_save(k):
            one.wait()
    for k in (1, 2, 3):
        bias_copy(k).wait_send()
    for w in range(3):
        for k in (1, 2, 3):
            s = other_z(m, k)
            for h in (0, 1):
                if w < 2:
                    s1(w, s, h).wait_send()
                    s2(w, s, h).wait_send()
                else:
                    last(s, h).wait_send()
            core(w, s).wait_send()

        for k in (1, k2):
            for one in z_copies(w, k):
                one.wait_send()

        @pl.when(inner)
        def _(w=w):
            for k in (2, 3):
                for one in z_forwards(w, k):
                    one.wait_send()


def forward_call(fill, x, weights, vectors):
    rows, width = x.shape
    any_spec = pl.BlockSpec(memory_space=pl.ANY)
    vmem = pl.BlockSpec(memory_space=pltpu.VMEM)
    flat = (rows, width)

    def hbm(shape, kind=BF):
        return jax.ShapeDtypeStruct(shape, kind)

    outs = [
        hbm(flat),
        hbm((12, rows, LANES)),
        hbm(flat),
        hbm(flat),
        hbm(flat),
        hbm(flat),
        hbm(flat),
        hbm(flat, F32),
        hbm((4, rows, 768)),
        hbm((4, rows, 768)),
        hbm((2, 2, 768, 768)),
        hbm((4, 2, 2, 192, 768)),
        hbm((4, 2, 2, 192, 768)),
    ]
    dma = pltpu.SemaphoreType.DMA
    scratch = [
        pltpu.VMEM((2, 2, 768, 768), BF),
        pltpu.VMEM((4, 2, 2, 192, 768), BF),
        pltpu.VMEM((4, 2, 2, 192, 768), BF),
        pltpu.VMEM((4, 8, 768), F32),
        pltpu.VMEM(flat, BF),
        pltpu.VMEM(flat, BF),
        pltpu.VMEM(flat, BF),
        pltpu.VMEM(flat, BF),
        pltpu.VMEM(flat, BF),
        pltpu.VMEM(flat, BF),
        pltpu.VMEM((12, rows, LANES), BF),
        pltpu.VMEM(flat, F32),
        pltpu.VMEM(flat, F32),
        pltpu.VMEM((4, rows, 768), BF),
        pltpu.VMEM((4, rows, 768), BF),
        pltpu.VMEM(flat, BF),
        dma((3, 3, 2)),
        dma((3, 3, 2)),
        dma((3, 2, 2)),
        dma((3, 4, 2)),
        dma((3, 4, 2)),
        dma((3, 4, 2)),
        dma((3, 4, 2)),
        dma((3, 4)),
        dma((3, 4)),
        dma((3,)),
        dma((3,)),
        dma((6,)),
        dma((9,)),
        dma((4, 4)),
    ]
    return pl.pallas_call(
        forward_kernel,
        out_shape=outs,
        in_specs=[pl.BlockSpec(memory_space=pltpu.SMEM), vmem] + [any_spec] * 4 + [vmem] * 8,
        out_specs=[any_spec] * len(outs),
        scratch_shapes=scratch,
        compiler_params=pltpu.CompilerParams(collective_id=0, has_side_effects=True, vmem_limit_bytes=60 << 20),
        name="forward",
    )(fill, x, *weights, *vectors)


def backward_kernel(
    fill_ref,
    gain1,
    gain2,
    lo_in,
    g_in,
    x_in,
    qa_in,
    k_in,
    v_in,
    ho_in,
    n1_in,
    n2_in,
    r1_in,
    hid_in,
    gp_in,
    wa_in,
    wu_in,
    wd_in,
    lo_all,
    pg_all,
    grads,
    sums,
    g_s,
    x_s,
    qa_s,
    k_s,
    v_s,
    ho_s,
    n1_s,
    n2_s,
    r1_s,
    wa,
    hid_b,
    gp_b,
    wu_b,
    wd_b,
    pre_s,
    acc,
    res_s,
    dho_s,
    dq_s,
    dk_s,
    dv_s,
    unit,
    rc,
    rx,
    ry,
    rz,
    vs0,
    vs_r,
    vs_z,
    los,
    lor,
    pgs,
    pgr,
    cs,
    cr,
    s1s,
    s1r,
    s2s,
    s2r,
    zs,
    zr,
    vss,
    vsr,
    vzs,
    vzr,
    load,
    chunk_load,
    own_sem,
):
    d, m, y, x, c, px, py, pc = place()
    rows = g_in.shape[0]
    half = rows // 2
    every = slice(None)

    def remote(src, dst, send, recv, peer):
        return pltpu.make_async_remote_copy(
            src_ref=src, dst_ref=dst, send_sem=send, recv_sem=recv, device_id=peer, device_id_type=MESH
        )

    quarter = rows // 64 * 16
    starts = [(i * quarter, quarter if i < 3 else rows - 3 * quarter) for i in range(4)]

    class Line:
        def __init__(self, own, full, send, recv):
            self.own, self.full, self.send, self.recv = own, full, send, recv

        def copy(self, up, dist, j, sending):
            step = 1 if up else -1
            begin, size = starts[j]
            source = m - step * (dist - 1) if sending else m - step * dist
            there = self.full.at[source, pl.ds(begin, size)]
            here = self.own.at[pl.ds(begin, size)] if (sending and dist == 1) else there
            i = 0 if up else 1
            return remote(here, there, self.send.at[i, dist - 1, j], self.recv.at[i, dist - 1, j], (d, m + step if sending else m - step))

        def sends(self, up, dist):
            return ((m >= dist - 1) & (m <= 2)) if up else ((m <= 4 - dist) & (m >= 1))

        def gets(self, up, dist):
            return (m >= dist) if up else (m <= 3 - dist)

        def begin(self):
            for j in range(4):
                for up in (True, False):
                    @pl.when(self.sends(up, 1))
                    def _(up=up, j=j):
                        self.copy(up, 1, j, True).start()

        def pass_on(self, up, dist, j):
            self.copy(up, dist, j, False).wait_recv()
            self.copy(up, dist + 1, j, True).start()

        def outward(self, dist, j):
            for at, up in ((1, False), (2, True)):
                @pl.when(m == at)
                def _(up=up):
                    self.pass_on(up, dist, j)

        def inward(self, j):
            for at, up in ((1, True), (2, False)):
                @pl.when(m == at)
                def _(up=up):
                    self.pass_on(up, 1, j)

        def rest(self):
            for dist in (1, 2, 3):
                for j in range(4):
                    for up in (True, False):
                        stays = self.gets(up, dist)
                        if dist < 3:
                            stays = stays & ((m == 3) if up else (m == 0))

                        @pl.when(stays)
                        def _(up=up, dist=dist, j=j):
                            self.copy(up, dist, j, False).wait_recv()

        def finish(self):
            for dist in (1, 2, 3):
                for j in range(4):
                    for up in (True, False):
                        @pl.when(self.sends(up, dist))
                        def _(up=up, dist=dist, j=j):
                            self.copy(up, dist, j, True).wait_send()

    def core_send(a, u):
        return remote(unit.at[a, u, every, every, 1 - c], rc.at[a, u], cs.at[a, u], cr.at[a, u], (pc, m))

    def s1(a, u, h):
        if h == 0:
            return remote(unit.at[a, u, every, 1 - x, c, pl.ds(0, 48)], rx.at[a, u, 0], s1s.at[a, u, 0], s1r.at[a, u, 0], (px, m))
        return remote(unit.at[a, u, 1 - y, every, c, pl.ds(48, 48)], rx.at[a, u, 1], s1s.at[a, u, 1], s1r.at[a, u, 1], (py, m))

    def s2(a, u, h):
        if h == 0:
            return remote(unit.at[a, u, 1 - y, x, c, pl.ds(0, 48)], ry.at[a, u, 0], s2s.at[a, u, 0], s2r.at[a, u, 0], (py, m))
        return remote(unit.at[a, u, y, 1 - x, c, pl.ds(48, 48)], ry.at[a, u, 1], s2s.at[a, u, 1], s2r.at[a, u, 1], (px, m))

    def z_send(a, up, dist):
        p = m + dist if up else m - dist
        slot = 4 if (up and dist == 1) else p
        peer = m + 1 if up else m - 1
        return remote(unit.at[a, other_z(m, p), y, x, c], rz.at[a, slot], zs.at[a, p], zr.at[a, slot], (d, peer))

    def z_recv(a, slot):
        remote(rz.at[a, slot], rz.at[a, slot], zs.at[a, 0], zr.at[a, slot], (d, other_z(m, 1))).wait_recv()

    def z_has(up, dist):
        return (m + dist <= 3) if up else (m >= dist)

    def z_step(a, dist):
        for up in (True, False):

            @pl.when(z_has(up, dist))
            def _(up=up):
                p = m + dist if up else m - dist
                if dist < 3:

                    @pl.when((m > 0) if up else (m < 3))
                    def _():
                        z_recv(a, p)
                        u = other_z(m, p)
                        unit[a, u, y, x, c] = (unit[a, u, y, x, c].astype(F32) + rz[a, p].astype(F32)).astype(BF)

                z_send(a, up, dist).start()

    def go1(a, u):
        core_send(a, u).wait_recv()
        unit[a, u, :, :, c] = (unit[a, u, :, :, c].astype(F32) + rc[a, u].astype(F32)).astype(BF)
        s1(a, u, 0).start()
        s1(a, u, 1).start()

    def go2(a, u):
        s1(a, u, 0).wait_recv()
        unit[a, u, :, x, c, 0:48] = (unit[a, u, :, x, c, 0:48].astype(F32) + rx[a, u, 0].astype(F32)).astype(BF)
        s2(a, u, 0).start()
        s1(a, u, 1).wait_recv()
        unit[a, u, y, :, c, 48:96] = (unit[a, u, y, :, c, 48:96].astype(F32) + rx[a, u, 1].astype(F32)).astype(BF)
        s2(a, u, 1).start()

    def go3(a, u):
        for h in (0, 1):
            s2(a, u, h).wait_recv()
            part = pl.ds(48 * h, 48)
            unit[a, u, y, x, c, part] = (unit[a, u, y, x, c, part].astype(F32) + ry[a, u, h].astype(F32)).astype(BF)

    def go4(a):
        grads[a] = unit[a, 0, y, x, c].astype(F32)

        @pl.when(m < 3)
        def _():
            z_recv(a, m)
            grads[a] += rz[a, m].astype(F32)

        @pl.when(m > 0)
        def _():
            z_recv(a, 4)
            grads[a] += rz[a, 4].astype(F32)

    def copies(i):
        pairs = (
            (g_in, g_s),
            (n2_in, n2_s),
            (r1_in, r1_s),
            (ho_in, ho_s),
            (wa_in, wa),
            (qa_in, qa_s),
            (k_in, k_s),
            (v_in, v_s),
            (n1_in, n1_s),
            (x_in, x_s),
        )
        return pltpu.make_async_copy(pairs[i][0], pairs[i][1], load.at[i])

    def chunk(k):
        slot = k % 2
        mk = other_z(m, 3 - k)
        pairs = ((wd_in, wd_b), (gp_in, gp_b), (hid_in, hid_b), (wu_in, wu_b))
        return [pltpu.make_async_copy(a.at[mk], b.at[slot], chunk_load.at[i, slot]) for i, (a, b) in enumerate(pairs)]

    line_lo = Line(lo_in, lo_all, los, lor)
    line_pg = Line(dho_s, pg_all, pgs, pgr)

    copies(0).start()
    for one in chunk(0):
        one.start()
    enter(d, m, px, py, pc)
    line_lo.begin()
    own_lo = pltpu.make_async_copy(lo_in, lo_all.at[m], own_sem.at[0])
    own_lo.start()
    for i in range(1, 10):
        copies(i).start()
    copies(0).wait()
    copies(1).wait()
    sums_row = jnp.zeros((1, 768), F32)
    for i in range(vs0.shape[0]):
        vs0[i : i + 1] = sums_row
    acc[...] = jnp.zeros_like(acc)

    def feed(k, carry):
        slot = k % 2
        u = 3 - k
        mk = other_z(m, u)

        @pl.when(k < 3)
        def _():
            for one in chunk(k + 1):
                one.start()

        for one in chunk(k):
            one.wait()

        def first(n, inner):
            cols = pl.ds(pl.multiple_of(n * 256, 256), 256)
            hg = dot(g_s[...], wd_b[slot, cols], NT)
            low = (hg * gp_b[slot, :, cols].astype(F32)).astype(BF)
            pre_s[:, cols] = low
            vs0[pl.ds(8 + mk, 1), cols] = jnp.sum(low.astype(F32), axis=0, keepdims=True)
            return inner

        lax.fori_loop(0, 3, first, 0)

        def second(n, inner):
            cols = pl.ds(pl.multiple_of(n * 384, 128), 384)
            unit[0, u, n] = dot(g_s[:, cols], hid_b[slot], TN).astype(BF).reshape(2, 2, 96, 768)
            unit[1, u, n] = dot(n2_s[:, cols], pre_s[...], TN).astype(BF).reshape(2, 2, 96, 768)
            return inner

        lax.fori_loop(0, 2, second, 0)
        core_send(0, u).start()
        core_send(1, u).start()

        def third(n, inner):
            cols = pl.ds(pl.multiple_of(n * 256, 256), 256)
            acc[:, cols] += dot(pre_s[...], wu_b[slot, cols], NT)
            return inner

        @pl.when(k > 0)
        def _():
            go1(0, u + 1)
            go1(1, u + 1)

        lax.fori_loop(0, 3, third, 0)
        return carry

    lax.fori_loop(0, 4, feed, 0)
    line_lo.outward(1, 0)
    line_lo.inward(0)
    line_lo.outward(1, 1)
    line_lo.inward(1)

    def norm_back(values, upstream, gain):
        center = values - jnp.mean(values, axis=-1, keepdims=True)
        inverse = lax.rsqrt(jnp.mean(center * center, axis=-1, keepdims=True) + EPS)
        n = center * inverse
        scaled = upstream * gain
        result = inverse * (
            scaled - jnp.mean(scaled, axis=-1, keepdims=True) - n * jnp.mean(scaled * n, axis=-1, keepdims=True)
        )
        gain_part = jnp.sum(upstream * n, axis=0, keepdims=True)
        return result, gain_part, jnp.sum(upstream, axis=0, keepdims=True)

    for i in (2, 3, 4):
        copies(i).wait()

    zero = jnp.zeros((1, 768), F32)
    carry = (zero, zero, zero, zero)
    for i in range(rows // 32):
        block = pl.ds(i * 32, 32)
        upstream = acc[block]
        through, gain_part, shift_part = norm_back(r1_s[block], upstream, gain2[...].reshape(1, 768))
        g = g_s[block].astype(F32)
        res = g + through
        r1_s[block] = res
        res_s[block] = res.astype(BF)
        parts = (gain_part, shift_part, jnp.sum(res, axis=0, keepdims=True), jnp.sum(g, axis=0, keepdims=True))
        carry = tuple(a + b for a, b in zip(carry, parts))
    n2g, n2s, ob, db = carry
    go1(0, 0)
    go1(1, 0)
    line_lo.outward(1, 2)
    line_lo.inward(2)
    vs0[2:3] = ob
    vs0[3:4] = n2g
    vs0[4:5] = n2s
    vs0[5:6] = db

    def heads_grad(n, carry):
        cols = pl.ds(pl.multiple_of(n * 256, 256), 256)
        dho_s[:, cols] = dot(res_s[...], wa[1, 1, cols], NT).astype(BF)
        return carry

    lax.fori_loop(0, 3, heads_grad, 0)
    line_lo.outward(1, 3)
    line_lo.inward(3)
    for i in (5, 6, 7):
        copies(i).wait()

    key_row = lax.broadcasted_iota(jnp.int32, (rows, LANES), 0)
    lane = lax.broadcasted_iota(jnp.int32, (rows, LANES), 1)
    mask_add = jnp.where(key_row < fill_ref[m], 0.0, MASKED)
    lane_half = lax.broadcasted_iota(jnp.int32, (half, LANES), 1)
    lane_turned = lax.broadcasted_iota(jnp.int32, (LANES, rows), 0)

    def attend(p):
        lanes = pl.ds(pl.multiple_of(p * LANES, LANES), LANES)
        kp = k_s[:, lanes].astype(F32)
        vp = v_s[:, lanes].astype(F32)
        dop = dho_s[:, lanes]
        dof = dop.astype(F32)
        both = dof * ho_s[:, lanes].astype(F32)
        ups = []
        for h in (0, 1):
            own_lane = (lane < HD) if h == 0 else (lane >= HD)
            first = HD if h == 0 else 0
            center = jnp.sum(jnp.where(own_lane, both, 0.0), axis=-1, keepdims=True)
            hi = center.astype(BF).astype(F32)
            lo = (center - hi).astype(BF).astype(F32)
            rest = center - hi - lo
            extra = jnp.where(lane == first, -hi, jnp.where(lane == first + 1, -lo, jnp.where(lane == first + 2, -rest, 0.0)))
            ups.append(jnp.where(own_lane, dof, extra).astype(BF))
        turned = [None, None]
        for b in (0, 1):
            block = slice(b * half, (b + 1) * half)
            dks, dvs = [], []
            for h in (0, 1):
                own_lane = (lane_half < HD) if h == 0 else (lane_half >= HD)
                first = HD if h == 0 else 0
                extra = jnp.where(lane_half == first, mask_add[block], jnp.where(lane_half < first + 4, 1.0, 0.0))
                keys = jnp.where(own_lane, kp[block], extra).astype(BF)
                values = jnp.where(own_lane, vp[block], jnp.where(lane_half < first + 3, 1.0, 0.0)).astype(BF)
                qa = qa_s[2 * p + h]
                probs = jnp.exp(dot(keys, qa, NT))
                dvs.append(dot(probs.astype(BF), dop, NN))
                ds = (probs * dot(values, ups[h], NT)).astype(BF)
                dks.append(dot(ds, qa, NN))
                t = dot(keys, ds, TN)
                turned[h] = t if b == 0 else turned[h] + t
            here = pl.ds(b * half, half)
            dk_s[here, lanes] = jnp.where(lane_half < HD, dks[0], dks[1]).astype(BF)
            dv_s[here, lanes] = jnp.where(lane_half < HD, dvs[0], dvs[1]).astype(BF)
        dq = jnp.where(lane_turned < HD, turned[0], turned[1])
        dq_s[:, lanes] = (jnp.transpose(dq) * (HD**-0.5)).astype(BF)

    def pair(p, carry):
        attend(p)

        @pl.when((p == 1) | (p == 3))
        def _():
            u = 3 - p // 2
            go2(0, u)
            go2(1, u)

        @pl.when(p == 5)
        def _():
            go3(0, 3)
            go3(1, 3)

        for j in range(4):
            @pl.when(p == j + 1)
            def _(j=j):
                line_lo.outward(2, j)

        return carry

    lax.fori_loop(0, 6, pair, 0)
    def both(stage, u):
        stage(0, u)
        stage(1, u)

    both(go2, 1)
    both(z_step, 3)
    vs0[6:7] = jnp.sum(dq_s[...].astype(F32), axis=0, keepdims=True)
    vs0[7:8] = jnp.sum(dv_s[...].astype(F32), axis=0, keepdims=True)
    copies(8).wait()
    copies(9).wait()

    def last_product(n, carry):
        cols = pl.ds(pl.multiple_of(n * 256, 256), 256)
        acc[:, cols] = (
            dot(dq_s[...], wa[0, 0, :, cols], NN) + dot(dk_s[...], wa[0, 1, :, cols], NN) + dot(dv_s[...], wa[1, 0, :, cols], NN)
        )
        return carry

    lax.fori_loop(0, 3, last_product, 0)
    both(go3, 2)

    carry = (zero, zero)
    for i in range(rows // 32):
        block = pl.ds(i * 32, 32)
        through, gain_part, shift_part = norm_back(x_s[block].astype(F32), acc[block], gain1[...].reshape(1, 768))
        dho_s[block] = (r1_s[block] + through).astype(BF)
        carry = (carry[0] + gain_part, carry[1] + shift_part)
    n1g, n1s = carry
    vs0[0:1] = n1g
    vs0[1:2] = n1s
    both(z_step, 2)
    line_pg.begin()
    own_pg = pltpu.make_async_copy(dho_s, pg_all.at[m], own_sem.at[1])
    own_pg.start()

    lane_tile = lax.broadcasted_iota(jnp.int32, (384, LANES), 1)

    def turn(v):
        return pltpu.roll(v, HD, 1)

    def attention_grads(e, carry):
        def tile(n, inner):
            cols = pl.ds(pl.multiple_of(n * 384, 128), 384)
            heads = pl.ds(pl.multiple_of(e * 384, 128), 384)
            n1 = n1_s[:, cols]
            q, k, v = [dot(n1, t[:, heads], TN) for t in (dq_s, dk_s, dv_s)]
            o = dot(res_s[:, cols], ho_s[:, heads], TN)

            def block(t, i):
                return t[:, i * LANES : (i + 1) * LANES]

            def low(a, b):
                return jnp.where(lane_tile < HD, block(a, 1), turn(block(b, 1)))

            def high(a, b):
                return jnp.where(lane_tile < HD, turn(block(a, 1)), block(b, 1))

            even = [block(q, 0), low(q, k), block(k, 0), block(v, 0), low(v, o), block(o, 0)]
            odd = [high(q, k), block(q, 2), block(k, 2), high(v, o), block(v, 2), block(o, 2)]
            ue, uo = other_z(m, 2 * e), other_z(m, 2 * e + 1)
            for i in range(6):
                lanes = slice(i * LANES, (i + 1) * LANES)
                unit[2, ue, n, :, :, :, lanes] = even[i].astype(BF).reshape(2, 2, 96, LANES)
                unit[2, uo, n, :, :, :, lanes] = odd[i].astype(BF).reshape(2, 2, 96, LANES)
            return inner

        lax.fori_loop(0, 2, tile, 0)
        core_send(2, other_z(m, 2 * e)).start()
        core_send(2, other_z(m, 2 * e + 1)).start()
        return carry

    attention_grads(0, 0)
    both(go2, 0)
    both(go3, 1)
    attention_grads(1, 0)

    peers = ((pc, m), (px, m), (py, m))

    def small(i):
        return remote(vs0, vs_r.at[i], vss.at[i], vsr.at[i], peers[i])

    def small_add(i):
        small(i).wait()
        vs0[...] += vs_r[i]

    def small_z(k):
        return remote(vs0, vs_z.at[k - 1], vzs.at[k - 1], vzr.at[k - 1], (d, other_z(m, k)))

    small(0).start()
    for u in (3, 2, 1, 0):
        go1(2, u)
    line_pg.outward(1, 0)
    both(z_step, 1)
    small_add(0)
    small(1).start()
    line_pg.outward(1, 1)
    both(go3, 0)
    small_add(1)
    small(2).start()
    go2(2, 3)
    line_pg.outward(1, 2)
    go2(2, 2)
    small_add(2)
    for k in (1, 2, 3):
        small_z(k).start()
    line_pg.inward(0)
    line_pg.outward(1, 3)
    go2(2, 1)
    go3(2, 3)
    z_step(2, 3)
    line_pg.inward(1)
    go2(2, 0)
    go3(2, 2)
    line_pg.inward(2)
    line_pg.outward(2, 0)
    go3(2, 1)
    line_pg.inward(3)
    line_pg.outward(2, 1)
    go3(2, 0)
    z_step(2, 2)
    line_pg.outward(2, 2)
    line_pg.outward(2, 3)
    z_step(2, 1)
    line_lo.rest()
    total = vs0[...]
    for k in (1, 2, 3):
        small_z(k).wait_recv()
        total = total + vs_z[k - 1]
    sums[...] = total
    go4(0)
    go4(1)
    go4(2)
    line_pg.rest()
    line_lo.finish()
    line_pg.finish()
    own_lo.wait()
    own_pg.wait()
    for k in (1, 2, 3):
        small_z(k).wait_send()
    for a in range(3):
        for u in range(4):
            core_send(a, u).wait_send()
            for h in (0, 1):
                s1(a, u, h).wait_send()
                s2(a, u, h).wait_send()
        for dist in (1, 2, 3):
            for up in (True, False):

                @pl.when(z_has(up, dist))
                def _(a=a, dist=dist, up=up):
                    z_send(a, up, dist).wait_send()


def backward_call(fill, gain1, gain2, lo, g, x, qa, k, v, ho, n1, n2, r1, hid, gp, wa, wu, wd):
    rows, width = x.shape
    any_spec = pl.BlockSpec(memory_space=pl.ANY)
    vmem = pl.BlockSpec(memory_space=pltpu.VMEM)
    flat = (rows, width)
    outs = [
        jax.ShapeDtypeStruct((4, rows, width), BF),
        jax.ShapeDtypeStruct((4, rows, width), BF),
        jax.ShapeDtypeStruct((3, 96, 768), F32),
        jax.ShapeDtypeStruct((16, width), F32),
    ]
    dma = pltpu.SemaphoreType.DMA
    scratch = [
        pltpu.VMEM(flat, BF),
        pltpu.VMEM(flat, BF),
        pltpu.VMEM((12, rows, LANES), BF),
        pltpu.VMEM(flat, BF),
        pltpu.VMEM(flat, BF),
        pltpu.VMEM(flat, BF),
        pltpu.VMEM(flat, BF),
        pltpu.VMEM(flat, BF),
        pltpu.VMEM(flat, F32),
        pltpu.VMEM((2, 2, 768, 768), BF),
        pltpu.VMEM((2, rows, 768), BF),
        pltpu.VMEM((2, rows, 768), BF),
        pltpu.VMEM((2, 768, 768), BF),
        pltpu.VMEM((2, 768, 768), BF),
        pltpu.VMEM(flat, BF),
        pltpu.VMEM(flat, F32),
        pltpu.VMEM(flat, BF),
        pltpu.VMEM(flat, BF),
        pltpu.VMEM(flat, BF),
        pltpu.VMEM(flat, BF),
        pltpu.VMEM(flat, BF),
        pltpu.VMEM((3, 4, 2, 2, 2, 96, 768), BF),
        pltpu.VMEM((3, 4, 2, 2, 96, 768), BF),
        pltpu.VMEM((3, 4, 2, 2, 48, 768), BF),
        pltpu.VMEM((3, 4, 2, 48, 768), BF),
        pltpu.VMEM((3, 5, 96, 768), BF),
        pltpu.VMEM((16, width), F32),
        pltpu.VMEM((3, 16, width), F32),
        pltpu.VMEM((3, 16, width), F32),
        dma((2, 3, 4)),
        dma((2, 3, 4)),
        dma((2, 3, 4)),
        dma((2, 3, 4)),
        dma((3, 4)),
        dma((3, 4)),
        dma((3, 4, 2)),
        dma((3, 4, 2)),
        dma((3, 4, 2)),
        dma((3, 4, 2)),
        dma((3, 4)),
        dma((3, 5)),
        dma((3,)),
        dma((3,)),
        dma((3,)),
        dma((3,)),
        dma((10,)),
        dma((4, 2)),
        dma((2,)),
    ]
    return pl.pallas_call(
        backward_kernel,
        out_shape=outs,
        in_specs=[pl.BlockSpec(memory_space=pltpu.SMEM), vmem, vmem] + [any_spec] * 15,
        out_specs=[any_spec, any_spec, vmem, vmem],
        scratch_shapes=scratch,
        compiler_params=pltpu.CompilerParams(collective_id=1, has_side_effects=True, vmem_limit_bytes=62 << 20),
        name="backward",
    )(fill, gain1, gain2, lo, g, x, qa, k, v, ho, n1, n2, r1, hid, gp, wa, wu, wd)


def prepare(patches, fill_lengths, cotangent, norm1_gain, norm1_shift, w_qkv, qv_bias, w_out, out_bias, norm2_gain, norm2_shift, w_up, up_bias, w_down, down_bias):
    m = lax.axis_index("mp")
    length, width = patches.shape[1:]
    rows = -(-length // 32) * 32
    pad = ((0, rows - length), (0, 0))
    x = jnp.pad(lax.dynamic_index_in_dim(patches, m, 0, keepdims=False), pad)
    cot = jnp.pad(lax.dynamic_index_in_dim(cotangent, m, 0, keepdims=False), pad)
    weights = (
        jnp.transpose(w_qkv, (1, 2, 0)),
        w_out,
        w_up.reshape(2, 2, 192, width),
        w_down.reshape(2, 2, 192, width),
    )
    owner = lax.broadcasted_iota(jnp.int32, (2, 768), 1) // 192
    placed = jnp.where(owner == m, jnp.tile(qv_bias, (1, 4)), 0.0)
    vectors = (placed, up_bias, norm1_gain, norm1_shift, out_bias, norm2_gain, norm2_shift, down_bias)
    return x, cot, weights, vectors


def one_item(*args):
    length, width = args[0].shape[1:]
    x, cot, weights, vectors = prepare(*args)
    fill = args[1]
    lo, qa, k, v, ho, n1, n2, r1, hid, gp, wa, wu, wd = forward_call(fill, x, weights, vectors)
    wu = wu.reshape(4, width, 768)
    wd = wd.reshape(4, 768, width)
    lo_all, pg_all, grads, sums = backward_call(fill, vectors[2], vectors[5], lo, cot, x, qa, k, v, ho, n1, n2, r1, hid, gp, wa, wu, wd)
    d = lax.axis_index("dp")
    m = lax.axis_index("mp")
    layer_out = lo_all[:, :length]
    patches_grad = pg_all[:, :length].astype(F32)
    g = grads[2]
    is_even = m % 2 == 0

    def pick(even, odd):
        def join(parts):
            return jnp.concatenate([g[:, a:b] for a, b in parts], axis=1)

        return jnp.where(is_even, join(even), join(odd))

    q_grad = pick([(0, 192)], [(0, 64), (128, 256)])
    k_grad = pick([(256, 384), (192, 256)], [(64, 128), (256, 384)])
    v_grad = pick([(384, 576)], [(384, 448), (512, 640)])
    o_grad = pick([(640, 768), (576, 640)], [(448, 512), (640, 768)])
    mine = lax.dynamic_slice(sums, (0, d * 96), (8, 96))
    qv = lax.dynamic_slice(sums, (6, m * 192 + d * 24), (2, 24))
    up_grad = lax.dynamic_slice(sums, (8 + m, d * 96), (1, 96))[0]
    return (
        layer_out,
        patches_grad,
        mine[0],
        mine[1],
        jnp.stack([q_grad, k_grad, v_grad], axis=1),
        qv,
        o_grad.T,
        mine[2],
        mine[3],
        mine[4],
        grads[1],
        up_grad,
        grads[0].T,
        mine[5],
    )


def normalize(values, gain, shift):
    center = values - jnp.mean(values, axis=-1, keepdims=True)
    inverse = lax.rsqrt(jnp.mean(center * center, axis=-1, keepdims=True) + EPS)
    unit = center * inverse
    return (unit, inverse, unit * gain + shift)


def normalize_back(upstream, unit, inverse, gain):
    gain_grad = jnp.sum(upstream * unit, axis=(0, 1))
    shift_grad = jnp.sum(upstream, axis=(0, 1))
    scaled = upstream * gain
    result = inverse * (
        scaled
        - jnp.mean(scaled, axis=-1, keepdims=True)
        - unit * jnp.mean(scaled * unit, axis=-1, keepdims=True)
    )
    return (gain_grad, shift_grad, result)


def split_heads(rows):
    return rows.reshape(rows.shape[0], rows.shape[1] // HD, HD)


def masked_scores(queries, keyset, usable):
    scores = jnp.einsum("qhd,khd->hqk", queries, keyset, preferred_element_type=jnp.float32)
    return jnp.where(usable[None, None, :], scores, -1e30)


def attend_items(operands):
    query_rows, key_rows, value_rows, usable = operands
    scores = masked_scores(split_heads(query_rows), split_heads(key_rows), usable)
    peak = jnp.max(scores, axis=-1, keepdims=True)
    expsum = jnp.exp(scores - peak)
    total = jnp.sum(expsum, axis=-1, keepdims=True)
    weights = (expsum / total).astype(jnp.bfloat16)
    mixed = jnp.einsum(
        "hqk,khd->qhd", weights, split_heads(value_rows), preferred_element_type=jnp.float32
    )
    return (
        mixed.reshape(query_rows.shape).astype(jnp.bfloat16),
        peak[..., 0] + jnp.log(total[..., 0]),
    )


def attend_items_back(operands):
    query_rows, key_rows, value_rows, usable, logsum, upstream = operands
    queries = split_heads(query_rows)
    keyset = split_heads(key_rows)
    scores = masked_scores(queries, keyset, usable)
    probs = jnp.exp(scores - logsum[..., None])
    weights = probs.astype(jnp.bfloat16)
    grad_heads = split_heads(upstream)
    value_grad = jnp.einsum("hqk,qhd->khd", weights, grad_heads, preferred_element_type=jnp.float32)
    prob_grad = jnp.einsum(
        "qhd,khd->hqk", grad_heads, split_heads(value_rows), preferred_element_type=jnp.float32
    )
    center = jnp.sum(probs * prob_grad, axis=-1, keepdims=True)
    score_grad = (probs * (prob_grad - center)).astype(jnp.bfloat16)
    query_grad = jnp.einsum("hqk,khd->qhd", score_grad, keyset, preferred_element_type=jnp.float32)
    key_grad = jnp.einsum("hqk,qhd->khd", score_grad, queries, preferred_element_type=jnp.float32)
    shape = query_rows.shape
    return (
        query_grad.reshape(shape).astype(jnp.bfloat16),
        key_grad.reshape(shape).astype(jnp.bfloat16),
        value_grad.reshape(shape).astype(jnp.bfloat16),
    )


def shards(
    patches,
    fill_lengths,
    cotangent,
    norm1_gain,
    norm1_shift,
    w_qkv,
    qv_bias,
    w_out,
    out_bias,
    norm2_gain,
    norm2_shift,
    w_up,
    up_bias,
    w_down,
    down_bias,
):
    scaling = HD ** (-0.5)
    seq_len = patches.shape[1]
    inputs = patches.astype(jnp.float32)
    unit1, inverse1, normed1_full = normalize(inputs, norm1_gain, norm1_shift)
    normed1 = normed1_full.astype(jnp.bfloat16)
    projected = jnp.einsum("isd,dtc->istc", normed1, w_qkv, preferred_element_type=jnp.float32)
    queries = ((projected[:, :, 0] + qv_bias[0]) * scaling).astype(jnp.bfloat16)
    key_rows = projected[:, :, 1].astype(jnp.bfloat16)
    value_rows = (projected[:, :, 2] + qv_bias[1]).astype(jnp.bfloat16)
    usable = jnp.arange(seq_len, dtype=jnp.int32)[None, :] < fill_lengths[:, None]
    heads_out, logsum = lax.map(attend_items, (queries, key_rows, value_rows, usable))
    partial_attn = jnp.einsum("isc,cd->isd", heads_out, w_out, preferred_element_type=jnp.float32)
    attention = lax.psum(partial_attn, "mp")
    residual1 = inputs + attention + out_bias
    unit2, inverse2, normed2_full = normalize(residual1, norm2_gain, norm2_shift)
    normed2 = normed2_full.astype(jnp.bfloat16)
    preact = jnp.einsum("isd,df->isf", normed2, w_up, preferred_element_type=jnp.float32) + up_bias
    activated, gelu_back = jax.vjp(jax.nn.gelu, preact)
    hidden = activated.astype(jnp.bfloat16)
    partial_ff = jnp.einsum("isf,fd->isd", hidden, w_down, preferred_element_type=jnp.float32)
    feedforward = lax.psum(partial_ff, "mp")
    layer_out = (residual1 + feedforward + down_bias).astype(jnp.bfloat16)
    upstream = cotangent.astype(jnp.float32)
    down_bias_grad = jnp.sum(upstream, axis=(0, 1))
    w_down_grad = jnp.einsum("isf,isd->fd", hidden, cotangent, preferred_element_type=jnp.float32)
    hidden_grad = jnp.einsum("isd,fd->isf", cotangent, w_down, preferred_element_type=jnp.float32)
    preact_grad = gelu_back(hidden_grad)[0].astype(jnp.bfloat16)
    up_bias_grad = jnp.sum(preact_grad.astype(jnp.float32), axis=(0, 1))
    w_up_grad = jnp.einsum("isd,isf->df", normed2, preact_grad, preferred_element_type=jnp.float32)
    partial_norm2 = jnp.einsum("isf,df->isd", preact_grad, w_up, preferred_element_type=jnp.float32)
    normed2_grad = lax.psum(partial_norm2, "mp")
    norm2_gain_grad, norm2_shift_grad, through_norm2 = normalize_back(
        normed2_grad, unit2, inverse2, norm2_gain
    )
    residual1_grad = upstream + through_norm2
    out_bias_grad = jnp.sum(residual1_grad, axis=(0, 1))
    residual_low = residual1_grad.astype(jnp.bfloat16)
    w_out_grad = jnp.einsum(
        "isc,isd->cd", heads_out, residual_low, preferred_element_type=jnp.float32
    )
    heads_grad = jnp.einsum(
        "isd,cd->isc", residual_low, w_out, preferred_element_type=jnp.float32
    ).astype(jnp.bfloat16)
    query_grad, key_grad, value_grad = lax.map(
        attend_items_back, (queries, key_rows, value_rows, usable, logsum, heads_grad)
    )
    query_scaled = query_grad * scaling
    proj_grad = jnp.stack([query_scaled, key_grad, value_grad], axis=2)
    w_qkv_grad = jnp.einsum("isd,istc->dtc", normed1, proj_grad, preferred_element_type=jnp.float32)
    qv_bias_grad = jnp.stack(
        [
            jnp.sum(query_scaled.astype(jnp.float32), axis=(0, 1)),
            jnp.sum(value_grad.astype(jnp.float32), axis=(0, 1)),
        ]
    )
    partial_norm1 = jnp.einsum(
        "istc,dtc->isd", proj_grad, w_qkv, preferred_element_type=jnp.float32
    )
    normed1_grad = lax.psum(partial_norm1, "mp")
    norm1_gain_grad, norm1_shift_grad, through_norm1 = normalize_back(
        normed1_grad, unit1, inverse1, norm1_gain
    )
    patches_grad = residual1_grad + through_norm1
    summed = (
        lax.psum_scatter(norm1_gain_grad, "dp", scatter_dimension=0, tiled=True),
        lax.psum_scatter(norm1_shift_grad, "dp", scatter_dimension=0, tiled=True),
        lax.psum_scatter(w_qkv_grad, "dp", scatter_dimension=0, tiled=True),
        lax.psum_scatter(qv_bias_grad, "dp", scatter_dimension=1, tiled=True),
        lax.psum_scatter(w_out_grad, "dp", scatter_dimension=1, tiled=True),
        lax.psum_scatter(out_bias_grad, "dp", scatter_dimension=0, tiled=True),
        lax.psum_scatter(w_up_grad, "dp", scatter_dimension=0, tiled=True),
        lax.psum_scatter(up_bias_grad, "dp", scatter_dimension=0, tiled=True),
        lax.psum_scatter(w_down_grad, "dp", scatter_dimension=1, tiled=True),
        lax.psum_scatter(down_bias_grad, "dp", scatter_dimension=0, tiled=True),
        lax.psum_scatter(norm2_gain_grad, "dp", scatter_dimension=0, tiled=True),
        lax.psum_scatter(norm2_shift_grad, "dp", scatter_dimension=0, tiled=True),
    )
    return (
        layer_out,
        patches_grad,
        summed[0],
        summed[1],
        summed[2],
        summed[3],
        summed[4],
        summed[5],
        summed[10],
        summed[11],
        summed[6],
        summed[7],
        summed[8],
        summed[9],
    )


def solution(mesh):
    body = one_item if (mesh.shape['dp'], mesh.shape['mp']) == (8, 4) else shards
    return jax.shard_map(
        body,
        mesh=mesh,
        in_specs=(
            P("dp", None, None),
            P("dp"),
            P("dp", None, None),
            P(),
            P(),
            P(None, None, "mp"),
            P(None, "mp"),
            P("mp", None),
            P(),
            P(),
            P(),
            P(None, "mp"),
            P("mp"),
            P("mp", None),
            P(),
        ),
        out_specs=(
            P("dp", None, None),
            P("dp", None, None),
            P("dp"),
            P("dp"),
            P("dp", None, "mp"),
            P(None, ("mp", "dp")),
            P("mp", "dp"),
            P("dp"),
            P("dp"),
            P("dp"),
            P("dp", "mp"),
            P(("mp", "dp")),
            P("mp", "dp"),
            P("dp"),
        ),
        check_vma=False,
    )
```

```python
import functools
import jax
import jax.numpy as jnp
from jax import lax
from jax.experimental import pallas as pl
from jax.experimental.pallas import tpu as pltpu
from jax.sharding import PartitionSpec as P

MESH = pl.DeviceIdType.MESH
BF = jnp.bfloat16
F32 = jnp.float32
HD = 64
LANES = 128
EPS = 1e-6
MASKED = -1e30
GELU_A = 0.7978845608028654
GELU_B = 0.044715

NN = (((1,), (0,)), ((), ()))
NT = (((1,), (1,)), ((), ()))
TN = (((0,), (0,)), ((), ()))


def dot(a, b, dims):
    return lax.dot_general(a, b, dims, preferred_element_type=F32)


def place():
    d = lax.axis_index("dp")
    m = lax.axis_index("mp")
    y, x, c = d // 4, (d // 2) % 2, d % 2
    px = d + 2 - 4 * x
    py = d + 4 - 8 * y
    pc = d + 1 - 2 * c
    return d, m, y, x, c, px, py, pc


def other_z(m, k):
    low = (m % 2 + k % 2) % 2
    high = (m // 2 + k // 2) % 2
    return 2 * high + low


def enter(d, m, px, py, pc):
    barrier = pltpu.get_barrier_semaphore()
    for peer in ((px, m), (py, m), (pc, m)):
        pl.semaphore_signal(barrier, inc=1, device_id=peer, device_id_type=MESH)
    for k in (1, 2, 3):
        pl.semaphore_signal(barrier, inc=1, device_id=(d, other_z(m, k)), device_id_type=MESH)
    pl.semaphore_wait(barrier, 6)


def forward_kernel(
    fill_ref,
    x_in,
    g_in,
    wq_in,
    wo_in,
    wu_in,
    wd_in,
    qv_bias,
    up_bias,
    gain1,
    shift1,
    out_bias,
    gain2,
    shift2,
    down_bias,
    layer_out,
    qa_out,
    k_out,
    v_out,
    ho_out,
    n1_out,
    n2_out,
    r1_out,
    hid_out,
    gp_out,
    wa_out,
    wu_out,
    wd_out,
    x_out,
    g_out,
    wa,
    wu,
    wd,
    bias,
    q_s,
    k_s,
    v_s,
    ho_s,
    n1_s,
    n2_s,
    qa_s,
    r1_s,
    acc,
    hid_s,
    gp_s,
    lo_s,
    x_s,
    g_s,
    raw_x,
    raw_g,
    zs,
    zr,
    fs,
    s1s,
    s1r,
    s2s,
    s2r,
    cs,
    cr,
    bs,
    br,
    load,
    out,
    chunk_out,
):
    d, m, y, x, c, px, py, pc = place()
    rows = x_s.shape[0]
    length = x_in.shape[0]
    half = rows // 2

    def part(w, s, ys, xs, core, start, size):
        if w == 0:
            return wa.at[ys, xs, pl.ds(s * 192 + core * 96 + start, size)]
        full = wu if w == 1 else wd
        return full.at[s, ys, xs, pl.ds(core * 96 + start, size)]

    every = slice(None)

    def remote(src, dst, send, recv, peer):
        return pltpu.make_async_remote_copy(
            src_ref=src, dst_ref=dst, send_sem=send, recv_sem=recv, device_id=peer, device_id_type=MESH
        )

    inner = (m == 1) | (m == 2)
    k2 = 2 + ((m + 1) // 2) % 2
    k3 = 5 - k2

    def z_views(w, s):
        if w < 2:
            return (part(w, s, y, x, c, 0, 96),)
        return part(w, s, every, x, c, 0, 48), part(w, s, y, every, c, 48, 48)

    def z_copies(w, k):
        peer = (d, other_z(m, k))
        return [remote(v, v, zs.at[w, k - 1, h], zr.at[w, k - 1, h], peer) for h, v in enumerate(z_views(w, m))]

    def z_forwards(w, k):
        peer = (d, other_z(m, 1))
        views = z_views(w, other_z(m, k))
        return [remote(v, v, fs.at[w, k - 2, h], zr.at[w, 4 - k, h], peer) for h, v in enumerate(views)]

    def z_begin(w):
        for k in (1, k2):
            for one in z_copies(w, k):
                one.start()

    def z_wait(w, k):
        s = other_z(m, k)
        for h, v in enumerate(z_views(w, s)):
            remote(v, v, zs.at[w, k - 1, h], zr.at[w, k - 1, h], (d, s)).wait_recv()

    def forward(w, k):
        @pl.when(inner)
        def _():
            z_wait(w, k)
            for one in z_forwards(w, k):
                one.start()

    def arrive(w, k):
        if isinstance(k, int):
            z_wait(w, k)
        else:

            @pl.when((m == 0) | (m == 3))
            def _():
                z_wait(w, k)

    def s1(w, s, h):
        here = part(w, s, y, x, c, 48 * h, 48)
        peer = (px, m) if h == 0 else (py, m)
        return remote(here, here, s1s.at[w, s, h], s1r.at[w, s, h], peer)

    def s1_wait(w, s, h):
        here = part(w, s, y, 1 - x, c, 0, 48) if h == 0 else part(w, s, 1 - y, x, c, 48, 48)
        peer = (px, m) if h == 0 else (py, m)
        remote(here, here, s1s.at[w, s, h], s1r.at[w, s, h], peer).wait_recv()

    def s2(w, s, h):
        here = part(w, s, y, every, c, 0, 48) if h == 0 else part(w, s, every, x, c, 48, 48)
        peer = (py, m) if h == 0 else (px, m)
        return remote(here, here, s2s.at[w, s, h], s2r.at[w, s, h], peer)

    def s2_wait(w, s, h):
        here = part(w, s, 1 - y, every, c, 0, 48) if h == 0 else part(w, s, every, 1 - x, c, 48, 48)
        peer = (py, m) if h == 0 else (px, m)
        remote(here, here, s2s.at[w, s, h], s2r.at[w, s, h], peer).wait_recv()

    def core(w, s):
        here = part(w, s, every, every, c, 0, 96)
        return remote(here, here, cs.at[w, s], cr.at[w, s], (pc, m))

    def core_wait(w, k):
        s = other_z(m, k)
        here = part(w, s, every, every, 1 - c, 0, 96)
        remote(here, here, cs.at[w, s], cr.at[w, s], (pc, m)).wait_recv()

    def go1(w, k):
        s = other_z(m, k)
        arrive(w, k)
        if w < 2:
            s1(w, s, 0).start()
            s1(w, s, 1).start()
        else:
            last(s, 0).start()
            last(s, 1).start()

    def last(s, h):
        here = part(2, s, every, x, c, 0, 48) if h == 0 else part(2, s, y, every, c, 48, 48)
        peer = (px, m) if h == 0 else (py, m)
        return remote(here, here, s2s.at[2, s, h], s2r.at[2, s, h], peer)

    def last_wait(s, h):
        here = part(2, s, every, 1 - x, c, 0, 48) if h == 0 else part(2, s, 1 - y, every, c, 48, 48)
        peer = (px, m) if h == 0 else (py, m)
        remote(here, here, s2s.at[2, s, h], s2r.at[2, s, h], peer).wait_recv()

    def go2(w, k):
        s = other_z(m, k)
        s1_wait(w, s, 0)
        s2(w, s, 0).start()
        s1_wait(w, s, 1)
        s2(w, s, 1).start()

    def go3(w, k):
        s = other_z(m, k)
        wait = functools.partial(s2_wait, w) if w < 2 else last_wait
        wait(s, 0)
        wait(s, 1)
        core(w, s).start()

    def own(w):
        if w == 0:
            mine = pl.ds(m * 192, 192)
            return [pltpu.make_async_copy(wq_in.at[t], wa.at[t // 2, t % 2, mine], load.at[t]) for t in range(3)] + [
                pltpu.make_async_copy(wo_in, wa.at[1, 1, mine], load.at[3])
            ]
        src = wu_in if w == 1 else wd_in
        return [pltpu.make_async_copy(src, part(w, m, every, every, 0, 0, 192), load.at[3 + w])]

    def bias_copy(k):
        return remote(bias.at[m], bias.at[m], bs.at[k - 1], br.at[k - 1], (d, other_z(m, k)))

    def bias_wait(k):
        here = bias.at[other_z(m, k)]
        remote(here, here, bs.at[k - 1], br.at[k - 1], (d, other_z(m, k))).wait_recv()

    for w in range(3):
        for one in own(w):
            one.start()
    items = [
        pltpu.make_async_copy(src, dst.at[pl.ds(0, length)], load.at[6 + i])
        for i, (src, dst) in enumerate(((x_in, raw_x), (g_in, raw_g)))
    ]
    for one in items:
        one.start()
    bias[m, 0:1] = up_bias[...].reshape(1, 768)
    bias[m, 1:3] = qv_bias[...]
    bias[m, 3:8] = jnp.zeros((5, 768), F32)
    enter(d, m, px, py, pc)
    for one in own(0):
        one.wait()
    z_begin(0)
    for k in (1, 2, 3):
        bias_copy(k).start()
    for one in own(1):
        one.wait()
    z_begin(1)

    def norm(values, gain, shift):
        center = values - jnp.mean(values, axis=-1, keepdims=True)
        inverse = lax.rsqrt(jnp.mean(center * center, axis=-1, keepdims=True) + EPS)
        return center * inverse * gain + shift

    def blocks(body):
        for i in range(rows // 32):
            body(pl.ds(i * 32, 32))

    def take(raw, item, i):
        block = pl.ds(pl.multiple_of(i * 32, 32), 32)
        v = raw[block].astype(F32)
        which = lax.broadcasted_iota(jnp.int32, v.shape, 1)
        row = lax.broadcasted_iota(jnp.int32, v.shape, 0) + i * 32
        item[block] = jnp.sum(jnp.where((which == m) & (row < length), v, 0.0), axis=1).astype(BF)

    items[0].wait()

    def take_x(i, carry):
        take(raw_x, x_s, i)
        return carry

    lax.fori_loop(0, rows // 32, take_x, 0)

    def first_norm(block):
        n1_s[block] = norm(x_s[block].astype(F32), gain1[...].reshape(1, 768), shift1[...].reshape(1, 768)).astype(BF)

    blocks(first_norm)
    save = [pltpu.make_async_copy(n1_s, n1_out, out.at[0])]
    save[0].start()
    items[1].wait()

    def take_g(p):
        for i in range(3):

            @pl.when(3 * p + i < rows // 32)
            def _(i=i):
                take(raw_g, g_s, 3 * p + i)

    for one in own(2):
        one.wait()

    go1(0, 1)
    forward(0, 3)
    forward(0, 2)
    z_begin(2)
    go1(0, k2)
    go2(0, 1)
    forward(1, 3)
    go1(0, k3)
    go1(1, 1)
    go2(0, k2)
    forward(1, 2)
    go3(0, 1)
    for k in (1, 2, 3):
        bias_wait(k)
    core_wait(0, 1)

    group0 = m // 2
    key_row = lax.broadcasted_iota(jnp.int32, (rows, LANES), 0)
    lane = lax.broadcasted_iota(jnp.int32, (rows, LANES), 1)
    mask_add = jnp.where(key_row < fill_ref[m], 0.0, MASKED)
    lane_half = lax.broadcasted_iota(jnp.int32, (half, LANES), 1)

    def project(g):
        rows_w = pl.ds(pl.multiple_of(g * 384, 128), 384)
        lanes = rows_w
        qb = bias[0, 1:2, lanes] + bias[1, 1:2, lanes] + bias[2, 1:2, lanes] + bias[3, 1:2, lanes]
        vb = bias[0, 2:3, lanes] + bias[1, 2:3, lanes] + bias[2, 2:3, lanes] + bias[3, 2:3, lanes]
        n1 = n1_s[...]
        q_s[:, lanes] = ((dot(n1, wa[0, 0, rows_w], NT) + qb) * (HD**-0.5)).astype(BF)
        k_s[:, lanes] = dot(n1, wa[0, 1, rows_w], NT).astype(BF)
        v_s[:, lanes] = (dot(n1, wa[1, 0, rows_w], NT) + vb).astype(BF)

    def attend(p):
        lanes = pl.ds(pl.multiple_of(p * LANES, LANES), LANES)
        kp = k_s[:, lanes].astype(F32)
        vp = v_s[:, lanes]
        keys = []
        for h in (0, 1):
            own_lane = (lane < HD) if h == 0 else (lane >= HD)
            first = HD if h == 0 else 0
            extra = jnp.where(lane == first, mask_add, jnp.where(lane < first + 4, 1.0, 0.0))
            keys.append(jnp.where(own_lane, kp, extra).astype(BF))
        for b in (0, 1):
            block = pl.ds(b * half, half)
            qp = q_s[block, lanes].astype(F32)
            mixed = []
            for h in (0, 1):
                own_lane = (lane_half < HD) if h == 0 else (lane_half >= HD)
                first = HD if h == 0 else 0
                base = jnp.where(own_lane, qp, jnp.where(lane_half == first, 1.0, 0.0))
                s = dot(base.astype(BF), keys[h], NT)
                peak = jnp.max(s, axis=-1, keepdims=True)
                e = jnp.exp(s - peak)
                total = jnp.sum(e, axis=-1, keepdims=True)
                mixed.append(dot(e.astype(BF), vp, NN) / total)
                lse = peak + jnp.log(total)
                hi = lse.astype(BF).astype(F32)
                lo = (lse - hi).astype(BF).astype(F32)
                rest = lse - hi - lo
                extra = jnp.where(
                    lane_half == first + 1, -hi, jnp.where(lane_half == first + 2, -lo, jnp.where(lane_half == first + 3, -rest, 0.0))
                )
                extra = jnp.where(lane_half == first, 1.0, extra)
                qa_s[2 * p + h, block] = jnp.where(own_lane, qp, extra).astype(BF)
            ho_s[block, lanes] = jnp.where(lane_half < HD, mixed[0], mixed[1]).astype(BF)

    project(group0)

    def steps(j, lists):
        for i, todo in enumerate(lists):

            @pl.when(j == i)
            def _(todo=todo):
                for stage, w, k in todo:
                    stage(w, k)

    def first_group(j, carry):
        attend(group0 * 3 + j)
        take_g(j)
        steps(
            j,
            (
                ((go2, 0, k3), (go3, 0, k2), (go1, 1, k2), (go2, 1, 1), (forward, 2, 3)),
                ((go3, 0, k3), (go1, 1, k3), (go2, 1, k2), (forward, 2, 2), (go1, 2, 1)),
                ((go3, 1, 1), (go2, 1, k3)),
            ),
        )
        return carry

    lax.fori_loop(0, 3, first_group, 0)
    core_wait(0, 2)
    core_wait(0, 3)
    save.append(pltpu.make_async_copy(wa, wa_out, out.at[7]))
    save[-1].start()
    project(1 - group0)

    def second_group(j, carry):
        attend((1 - group0) * 3 + j)
        take_g(3 + j)
        steps(j, (((go3, 1, k2), (go1, 2, k2)), ((go3, 1, k3), (go3, 2, 1)), ((go1, 2, k3),)))
        return carry

    lax.fori_loop(0, 3, second_group, 0)
    pairs = ((qa_s, qa_out), (k_s, k_out), (v_s, v_out), (ho_s, ho_out))
    for i, (a, b) in enumerate(pairs):
        save.append(pltpu.make_async_copy(a, b, out.at[1 + i]))
        save[-1].start()
    for i, (a, b) in enumerate(((x_s, x_out), (g_s, g_out))):
        save.append(pltpu.make_async_copy(a, b, out.at[9 + i]))
        save[-1].start()

    def finish_attention(n, carry):
        cols = pl.ds(pl.multiple_of(n * 256, 256), 256)
        acc[:, cols] = dot(ho_s[...], wa[1, 1, :, cols], NN)
        return carry

    lax.fori_loop(0, 3, finish_attention, 0)

    def second_norm(block):
        r1 = x_s[block].astype(F32) + acc[block] + out_bias[...].reshape(1, 768)
        r1_s[block] = r1
        n2_s[block] = norm(r1, gain2[...].reshape(1, 768), shift2[...].reshape(1, 768)).astype(BF)
        acc[block] = r1 + down_bias[...].reshape(1, 768)

    blocks(second_norm)
    more = ((r1_s, r1_out), (n2_s, n2_out))
    for i, (a, b) in enumerate(more):
        save.append(pltpu.make_async_copy(a, b, out.at[5 + i]))
        save[-1].start()
    go3(2, k2)

    def in_order(k):
        return k + (k // 2) * (k2 - 2) * (5 - 2 * k)

    def chunk_save(k):
        mk = other_z(m, in_order(k))
        pairs = ((wu, wu_out), (wd, wd_out), (hid_s, hid_out), (gp_s, gp_out))
        return [pltpu.make_async_copy(a.at[mk], b.at[mk], chunk_out.at[i, k]) for i, (a, b) in enumerate(pairs)]

    def feed(k, carry):
        ke = in_order(k)
        mk = other_z(m, ke)

        @pl.when(k == 1)
        def _():
            go3(2, k3)

        @pl.when(k > 0)
        def _():
            core_wait(1, ke)
            core_wait(2, ke)

        for one in chunk_save(k)[:2]:
            one.start()

        def up(n, inner):
            cols = pl.ds(pl.multiple_of(n * 256, 256), 256)
            w = wu[mk, :, :, :, cols].reshape(768, 256)
            v = dot(n2_s[...], w, NN) + bias[mk, 0:1, cols]
            sq = v * v
            t = jnp.tanh(v * (GELU_A + GELU_A * GELU_B * sq))
            hid_s[mk, :, cols] = (0.5 * v * (1.0 + t)).astype(BF)
            slope = 0.5 * (1.0 + t) + 0.5 * v * (1.0 - t * t) * (GELU_A + 3.0 * GELU_A * GELU_B * sq)
            gp_s[mk, :, cols] = slope.astype(BF)
            return inner

        lax.fori_loop(0, 3, up, 0)
        for one in chunk_save(k)[2:]:
            one.start()

        def down(n, inner):
            cols = pl.ds(pl.multiple_of(n * 256, 256), 256)
            w = wd[mk, :, :, :, cols].reshape(768, 256)
            acc[:, cols] += dot(hid_s[mk], w, NN)
            return inner

        lax.fori_loop(0, 3, down, 0)
        return carry

    lax.fori_loop(0, 4, feed, 0)
    lo_s[...] = acc[...].astype(BF)
    save.append(pltpu.make_async_copy(lo_s, layer_out, out.at[8]))
    save[-1].start()
    for one in save:
        one.wait()
    for k in range(4):
        for one in chunk_save(k):
            one.wait()
    for k in (1, 2, 3):
        bias_copy(k).wait_send()
    for w in range(3):
        for k in (1, 2, 3):
            s = other_z(m, k)
            for h in (0, 1):
                if w < 2:
                    s1(w, s, h).wait_send()
                    s2(w, s, h).wait_send()
                else:
                    last(s, h).wait_send()
            core(w, s).wait_send()

        for k in (1, k2):
            for one in z_copies(w, k):
                one.wait_send()

        @pl.when(inner)
        def _(w=w):
            for k in (2, 3):
                for one in z_forwards(w, k):
                    one.wait_send()


def forward_call(fill, x, g, weights, vectors):
    length, items, width = x.shape
    rows = -(-length // 32) * 32
    any_spec = pl.BlockSpec(memory_space=pl.ANY)
    vmem = pl.BlockSpec(memory_space=pltpu.VMEM)
    flat = (rows, width)

    def hbm(shape, kind=BF):
        return jax.ShapeDtypeStruct(shape, kind)

    outs = [
        hbm(flat),
        hbm((12, rows, LANES)),
        hbm(flat),
        hbm(flat),
        hbm(flat),
        hbm(flat),
        hbm(flat),
        hbm(flat, F32),
        hbm((4, rows, 768)),
        hbm((4, rows, 768)),
        hbm((2, 2, 768, 768)),
        hbm((4, 2, 2, 192, 768)),
        hbm((4, 2, 2, 192, 768)),
        hbm(flat),
        hbm(flat),
    ]
    dma = pltpu.SemaphoreType.DMA
    scratch = [
        pltpu.VMEM((2, 2, 768, 768), BF),
        pltpu.VMEM((4, 2, 2, 192, 768), BF),
        pltpu.VMEM((4, 2, 2, 192, 768), BF),
        pltpu.VMEM((4, 8, 768), F32),
        pltpu.VMEM(flat, BF),
        pltpu.VMEM(flat, BF),
        pltpu.VMEM(flat, BF),
        pltpu.VMEM(flat, BF),
        pltpu.VMEM(flat, BF),
        pltpu.VMEM(flat, BF),
        pltpu.VMEM((12, rows, LANES), BF),
        pltpu.VMEM(flat, F32),
        pltpu.VMEM(flat, F32),
        pltpu.VMEM((4, rows, 768), BF),
        pltpu.VMEM((4, rows, 768), BF),
        pltpu.VMEM(flat, BF),
        pltpu.VMEM(flat, BF),
        pltpu.VMEM(flat, BF),
        pltpu.VMEM((rows, items, width), BF),
        pltpu.VMEM((rows, items, width), BF),
        dma((3, 3, 2)),
        dma((3, 3, 2)),
        dma((3, 2, 2)),
        dma((3, 4, 2)),
        dma((3, 4, 2)),
        dma((3, 4, 2)),
        dma((3, 4, 2)),
        dma((3, 4)),
        dma((3, 4)),
        dma((3,)),
        dma((3,)),
        dma((8,)),
        dma((11,)),
        dma((4, 4)),
    ]
    return pl.pallas_call(
        forward_kernel,
        out_shape=outs,
        in_specs=[pl.BlockSpec(memory_space=pltpu.SMEM)] + [any_spec] * 6 + [vmem] * 8,
        out_specs=[any_spec] * len(outs),
        scratch_shapes=scratch,
        compiler_params=pltpu.CompilerParams(collective_id=0, has_side_effects=True, vmem_limit_bytes=60 << 20),
        name="forward",
    )(fill, x, g, *weights, *vectors)


def backward_kernel(
    fill_ref,
    gain1,
    gain2,
    lo_in,
    g_in,
    x_in,
    qa_in,
    k_in,
    v_in,
    ho_in,
    n1_in,
    n2_in,
    r1_in,
    hid_in,
    gp_in,
    wa_in,
    wu_in,
    wd_in,
    lo_all,
    pg_all,
    grads,
    sums,
    g_s,
    x_s,
    qa_s,
    k_s,
    v_s,
    ho_s,
    n1_s,
    n2_s,
    r1_s,
    wa,
    hid_b,
    gp_b,
    wu_b,
    wd_b,
    pre_s,
    acc,
    res_s,
    dho_s,
    dq_s,
    dk_s,
    dv_s,
    unit,
    rc,
    rx,
    ry,
    rz,
    vs0,
    vs_r,
    vs_z,
    los,
    lor,
    pgs,
    pgr,
    cs,
    cr,
    s1s,
    s1r,
    s2s,
    s2r,
    zs,
    zr,
    vss,
    vsr,
    vzs,
    vzr,
    load,
    chunk_load,
    own_sem,
):
    d, m, y, x, c, px, py, pc = place()
    rows = g_in.shape[0]
    half = rows // 2
    every = slice(None)

    def remote(src, dst, send, recv, peer):
        return pltpu.make_async_remote_copy(
            src_ref=src, dst_ref=dst, send_sem=send, recv_sem=recv, device_id=peer, device_id_type=MESH
        )

    quarter = rows // 64 * 16
    starts = [(i * quarter, quarter if i < 3 else rows - 3 * quarter) for i in range(4)]

    class Line:
        def __init__(self, own, full, send, recv):
            self.own, self.full, self.send, self.recv = own, full, send, recv

        def copy(self, up, dist, j, sending):
            step = 1 if up else -1
            begin, size = starts[j]
            source = m - step * (dist - 1) if sending else m - step * dist
            there = self.full.at[source, pl.ds(begin, size)]
            here = self.own.at[pl.ds(begin, size)] if (sending and dist == 1) else there
            i = 0 if up else 1
            return remote(here, there, self.send.at[i, dist - 1, j], self.recv.at[i, dist - 1, j], (d, m + step if sending else m - step))

        def sends(self, up, dist):
            return ((m >= dist - 1) & (m <= 2)) if up else ((m <= 4 - dist) & (m >= 1))

        def gets(self, up, dist):
            return (m >= dist) if up else (m <= 3 - dist)

        def begin(self):
            for j in range(4):
                for up in (True, False):
                    @pl.when(self.sends(up, 1))
                    def _(up=up, j=j):
                        self.copy(up, 1, j, True).start()

        def pass_on(self, up, dist, j):
            self.copy(up, dist, j, False).wait_recv()
            self.copy(up, dist + 1, j, True).start()

        def outward(self, dist, j):
            for at, up in ((1, False), (2, True)):
                @pl.when(m == at)
                def _(up=up):
                    self.pass_on(up, dist, j)

        def inward(self, j):
            for at, up in ((1, True), (2, False)):
                @pl.when(m == at)
                def _(up=up):
                    self.pass_on(up, 1, j)

        def rest(self):
            for dist in (1, 2, 3):
                for j in range(4):
                    for up in (True, False):
                        stays = self.gets(up, dist)
                        if dist < 3:
                            stays = stays & ((m == 3) if up else (m == 0))

                        @pl.when(stays)
                        def _(up=up, dist=dist, j=j):
                            self.copy(up, dist, j, False).wait_recv()

        def finish(self):
            for dist in (1, 2, 3):
                for j in range(4):
                    for up in (True, False):
                        @pl.when(self.sends(up, dist))
                        def _(up=up, dist=dist, j=j):
                            self.copy(up, dist, j, True).wait_send()

    def core_send(a, u):
        return remote(unit.at[a, u, every, every, 1 - c], rc.at[a, u], cs.at[a, u], cr.at[a, u], (pc, m))

    def s1(a, u, h):
        if h == 0:
            return remote(unit.at[a, u, every, 1 - x, c, pl.ds(0, 48)], rx.at[a, u, 0], s1s.at[a, u, 0], s1r.at[a, u, 0], (px, m))
        return remote(unit.at[a, u, 1 - y, every, c, pl.ds(48, 48)], rx.at[a, u, 1], s1s.at[a, u, 1], s1r.at[a, u, 1], (py, m))

    def s2(a, u, h):
        if h == 0:
            return remote(unit.at[a, u, 1 - y, x, c, pl.ds(0, 48)], ry.at[a, u, 0], s2s.at[a, u, 0], s2r.at[a, u, 0], (py, m))
        return remote(unit.at[a, u, y, 1 - x, c, pl.ds(48, 48)], ry.at[a, u, 1], s2s.at[a, u, 1], s2r.at[a, u, 1], (px, m))

    def z_send(a, up, dist):
        p = m + dist if up else m - dist
        slot = 4 if (up and dist == 1) else p
        peer = m + 1 if up else m - 1
        return remote(unit.at[a, other_z(m, p), y, x, c], rz.at[a, slot], zs.at[a, p], zr.at[a, slot], (d, peer))

    def z_recv(a, slot):
        remote(rz.at[a, slot], rz.at[a, slot], zs.at[a, 0], zr.at[a, slot], (d, other_z(m, 1))).wait_recv()

    def z_has(up, dist):
        return (m + dist <= 3) if up else (m >= dist)

    def z_step(a, dist):
        for up in (True, False):

            @pl.when(z_has(up, dist))
            def _(up=up):
                p = m + dist if up else m - dist
                if dist < 3:

                    @pl.when((m > 0) if up else (m < 3))
                    def _():
                        z_recv(a, p)
                        u = other_z(m, p)
                        unit[a, u, y, x, c] = (unit[a, u, y, x, c].astype(F32) + rz[a, p].astype(F32)).astype(BF)

                z_send(a, up, dist).start()

    def go1(a, u):
        core_send(a, u).wait_recv()
        unit[a, u, :, :, c] = (unit[a, u, :, :, c].astype(F32) + rc[a, u].astype(F32)).astype(BF)
        s1(a, u, 0).start()
        s1(a, u, 1).start()

    def go2(a, u):
        s1(a, u, 0).wait_recv()
        unit[a, u, :, x, c, 0:48] = (unit[a, u, :, x, c, 0:48].astype(F32) + rx[a, u, 0].astype(F32)).astype(BF)
        s2(a, u, 0).start()
        s1(a, u, 1).wait_recv()
        unit[a, u, y, :, c, 48:96] = (unit[a, u, y, :, c, 48:96].astype(F32) + rx[a, u, 1].astype(F32)).astype(BF)
        s2(a, u, 1).start()

    def go3(a, u):
        for h in (0, 1):
            s2(a, u, h).wait_recv()
            part = pl.ds(48 * h, 48)
            unit[a, u, y, x, c, part] = (unit[a, u, y, x, c, part].astype(F32) + ry[a, u, h].astype(F32)).astype(BF)

    def go4(a):
        grads[a] = unit[a, 0, y, x, c].astype(F32)

        @pl.when(m < 3)
        def _():
            z_recv(a, m)
            grads[a] += rz[a, m].astype(F32)

        @pl.when(m > 0)
        def _():
            z_recv(a, 4)
            grads[a] += rz[a, 4].astype(F32)

    def copies(i):
        pairs = (
            (g_in, g_s),
            (n2_in, n2_s),
            (r1_in, r1_s),
            (ho_in, ho_s),
            (wa_in, wa),
            (qa_in, qa_s),
            (k_in, k_s),
            (v_in, v_s),
            (n1_in, n1_s),
            (x_in, x_s),
        )
        return pltpu.make_async_copy(pairs[i][0], pairs[i][1], load.at[i])

    def chunk(k):
        slot = k % 2
        mk = other_z(m, 3 - k)
        pairs = ((wd_in, wd_b), (gp_in, gp_b), (hid_in, hid_b), (wu_in, wu_b))
        return [pltpu.make_async_copy(a.at[mk], b.at[slot], chunk_load.at[i, slot]) for i, (a, b) in enumerate(pairs)]

    line_lo = Line(lo_in, lo_all, los, lor)
    line_pg = Line(dho_s, pg_all, pgs, pgr)

    copies(0).start()
    for one in chunk(0):
        one.start()
    enter(d, m, px, py, pc)
    line_lo.begin()
    own_lo = pltpu.make_async_copy(lo_in, lo_all.at[m], own_sem.at[0])
    own_lo.start()
    for i in range(1, 10):
        copies(i).start()
    copies(0).wait()
    copies(1).wait()
    sums_row = jnp.zeros((1, 768), F32)
    for i in range(vs0.shape[0]):
        vs0[i : i + 1] = sums_row
    acc[...] = jnp.zeros_like(acc)

    def feed(k, carry):
        slot = k % 2
        u = 3 - k
        mk = other_z(m, u)

        @pl.when(k < 3)
        def _():
            for one in chunk(k + 1):
                one.start()

        for one in chunk(k):
            one.wait()

        def first(n, inner):
            cols = pl.ds(pl.multiple_of(n * 256, 256), 256)
            hg = dot(g_s[...], wd_b[slot, cols], NT)
            low = (hg * gp_b[slot, :, cols].astype(F32)).astype(BF)
            pre_s[:, cols] = low
            vs0[pl.ds(8 + mk, 1), cols] = jnp.sum(low.astype(F32), axis=0, keepdims=True)
            return inner

        lax.fori_loop(0, 3, first, 0)

        def second(n, inner):
            cols = pl.ds(pl.multiple_of(n * 384, 128), 384)
            unit[0, u, n] = dot(g_s[:, cols], hid_b[slot], TN).astype(BF).reshape(2, 2, 96, 768)
            unit[1, u, n] = dot(n2_s[:, cols], pre_s[...], TN).astype(BF).reshape(2, 2, 96, 768)
            return inner

        lax.fori_loop(0, 2, second, 0)
        core_send(0, u).start()
        core_send(1, u).start()

        def third(n, inner):
            cols = pl.ds(pl.multiple_of(n * 256, 256), 256)
            acc[:, cols] += dot(pre_s[...], wu_b[slot, cols], NT)
            return inner

        @pl.when(k > 0)
        def _():
            go1(0, u + 1)
            go1(1, u + 1)

        lax.fori_loop(0, 3, third, 0)
        return carry

    lax.fori_loop(0, 4, feed, 0)
    line_lo.outward(1, 0)
    line_lo.inward(0)
    line_lo.outward(1, 1)
    line_lo.inward(1)

    def norm_back(values, upstream, gain):
        center = values - jnp.mean(values, axis=-1, keepdims=True)
        inverse = lax.rsqrt(jnp.mean(center * center, axis=-1, keepdims=True) + EPS)
        n = center * inverse
        scaled = upstream * gain
        result = inverse * (
            scaled - jnp.mean(scaled, axis=-1, keepdims=True) - n * jnp.mean(scaled * n, axis=-1, keepdims=True)
        )
        gain_part = jnp.sum(upstream * n, axis=0, keepdims=True)
        return result, gain_part, jnp.sum(upstream, axis=0, keepdims=True)

    for i in (2, 3, 4):
        copies(i).wait()

    zero = jnp.zeros((1, 768), F32)
    carry = (zero, zero, zero, zero)
    for i in range(rows // 32):
        block = pl.ds(i * 32, 32)
        upstream = acc[block]
        through, gain_part, shift_part = norm_back(r1_s[block], upstream, gain2[...].reshape(1, 768))
        g = g_s[block].astype(F32)
        res = g + through
        r1_s[block] = res
        res_s[block] = res.astype(BF)
        parts = (gain_part, shift_part, jnp.sum(res, axis=0, keepdims=True), jnp.sum(g, axis=0, keepdims=True))
        carry = tuple(a + b for a, b in zip(carry, parts))
    n2g, n2s, ob, db = carry
    go1(0, 0)
    go1(1, 0)
    line_lo.outward(1, 2)
    line_lo.inward(2)
    vs0[2:3] = ob
    vs0[3:4] = n2g
    vs0[4:5] = n2s
    vs0[5:6] = db

    def heads_grad(n, carry):
        cols = pl.ds(pl.multiple_of(n * 256, 256), 256)
        dho_s[:, cols] = dot(res_s[...], wa[1, 1, cols], NT).astype(BF)
        return carry

    lax.fori_loop(0, 3, heads_grad, 0)
    line_lo.outward(1, 3)
    line_lo.inward(3)
    for i in (5, 6, 7):
        copies(i).wait()

    key_row = lax.broadcasted_iota(jnp.int32, (rows, LANES), 0)
    lane = lax.broadcasted_iota(jnp.int32, (rows, LANES), 1)
    mask_add = jnp.where(key_row < fill_ref[m], 0.0, MASKED)
    lane_half = lax.broadcasted_iota(jnp.int32, (half, LANES), 1)
    lane_turned = lax.broadcasted_iota(jnp.int32, (LANES, rows), 0)

    def attend(p):
        lanes = pl.ds(pl.multiple_of(p * LANES, LANES), LANES)
        kp = k_s[:, lanes].astype(F32)
        vp = v_s[:, lanes].astype(F32)
        dop = dho_s[:, lanes]
        dof = dop.astype(F32)
        both = dof * ho_s[:, lanes].astype(F32)
        ups = []
        for h in (0, 1):
            own_lane = (lane < HD) if h == 0 else (lane >= HD)
            first = HD if h == 0 else 0
            center = jnp.sum(jnp.where(own_lane, both, 0.0), axis=-1, keepdims=True)
            hi = center.astype(BF).astype(F32)
            lo = (center - hi).astype(BF).astype(F32)
            rest = center - hi - lo
            extra = jnp.where(lane == first, -hi, jnp.where(lane == first + 1, -lo, jnp.where(lane == first + 2, -rest, 0.0)))
            ups.append(jnp.where(own_lane, dof, extra).astype(BF))
        turned = [None, None]
        for b in (0, 1):
            block = slice(b * half, (b + 1) * half)
            dks, dvs = [], []
            for h in (0, 1):
                own_lane = (lane_half < HD) if h == 0 else (lane_half >= HD)
                first = HD if h == 0 else 0
                extra = jnp.where(lane_half == first, mask_add[block], jnp.where(lane_half < first + 4, 1.0, 0.0))
                keys = jnp.where(own_lane, kp[block], extra).astype(BF)
                values = jnp.where(own_lane, vp[block], jnp.where(lane_half < first + 3, 1.0, 0.0)).astype(BF)
                qa = qa_s[2 * p + h]
                probs = jnp.exp(dot(keys, qa, NT))
                dvs.append(dot(probs.astype(BF), dop, NN))
                ds = (probs * dot(values, ups[h], NT)).astype(BF)
                dks.append(dot(ds, qa, NN))
                t = dot(keys, ds, TN)
                turned[h] = t if b == 0 else turned[h] + t
            here = pl.ds(b * half, half)
            dk_s[here, lanes] = jnp.where(lane_half < HD, dks[0], dks[1]).astype(BF)
            dv_s[here, lanes] = jnp.where(lane_half < HD, dvs[0], dvs[1]).astype(BF)
        dq = jnp.where(lane_turned < HD, turned[0], turned[1])
        dq_s[:, lanes] = (jnp.transpose(dq) * (HD**-0.5)).astype(BF)

    def pair(p, carry):
        attend(p)

        @pl.when((p == 1) | (p == 3))
        def _():
            u = 3 - p // 2
            go2(0, u)
            go2(1, u)

        @pl.when(p == 5)
        def _():
            go3(0, 3)
            go3(1, 3)

        for j in range(4):
            @pl.when(p == j + 1)
            def _(j=j):
                line_lo.outward(2, j)

        return carry

    lax.fori_loop(0, 6, pair, 0)
    def both(stage, u):
        stage(0, u)
        stage(1, u)

    both(go2, 1)
    both(z_step, 3)
    vs0[6:7] = jnp.sum(dq_s[...].astype(F32), axis=0, keepdims=True)
    vs0[7:8] = jnp.sum(dv_s[...].astype(F32), axis=0, keepdims=True)
    copies(8).wait()
    copies(9).wait()

    def last_product(n, carry):
        cols = pl.ds(pl.multiple_of(n * 256, 256), 256)
        acc[:, cols] = (
            dot(dq_s[...], wa[0, 0, :, cols], NN) + dot(dk_s[...], wa[0, 1, :, cols], NN) + dot(dv_s[...], wa[1, 0, :, cols], NN)
        )
        return carry

    lax.fori_loop(0, 3, last_product, 0)
    both(go3, 2)

    carry = (zero, zero)
    for i in range(rows // 32):
        block = pl.ds(i * 32, 32)
        through, gain_part, shift_part = norm_back(x_s[block].astype(F32), acc[block], gain1[...].reshape(1, 768))
        dho_s[block] = (r1_s[block] + through).astype(BF)
        carry = (carry[0] + gain_part, carry[1] + shift_part)
    n1g, n1s = carry
    vs0[0:1] = n1g
    vs0[1:2] = n1s
    both(z_step, 2)
    line_pg.begin()
    own_pg = pltpu.make_async_copy(dho_s, pg_all.at[m], own_sem.at[1])
    own_pg.start()

    lane_tile = lax.broadcasted_iota(jnp.int32, (384, LANES), 1)

    def turn(v):
        return pltpu.roll(v, HD, 1)

    def attention_grads(e, carry):
        def tile(n, inner):
            cols = pl.ds(pl.multiple_of(n * 384, 128), 384)
            heads = pl.ds(pl.multiple_of(e * 384, 128), 384)
            n1 = n1_s[:, cols]
            q, k, v = [dot(n1, t[:, heads], TN) for t in (dq_s, dk_s, dv_s)]
            o = dot(res_s[:, cols], ho_s[:, heads], TN)

            def block(t, i):
                return t[:, i * LANES : (i + 1) * LANES]

            def low(a, b):
                return jnp.where(lane_tile < HD, block(a, 1), turn(block(b, 1)))

            def high(a, b):
                return jnp.where(lane_tile < HD, turn(block(a, 1)), block(b, 1))

            even = [block(q, 0), low(q, k), block(k, 0), block(v, 0), low(v, o), block(o, 0)]
            odd = [high(q, k), block(q, 2), block(k, 2), high(v, o), block(v, 2), block(o, 2)]
            ue, uo = other_z(m, 2 * e), other_z(m, 2 * e + 1)
            for i in range(6):
                lanes = slice(i * LANES, (i + 1) * LANES)
                unit[2, ue, n, :, :, :, lanes] = even[i].astype(BF).reshape(2, 2, 96, LANES)
                unit[2, uo, n, :, :, :, lanes] = odd[i].astype(BF).reshape(2, 2, 96, LANES)
            return inner

        lax.fori_loop(0, 2, tile, 0)
        core_send(2, other_z(m, 2 * e)).start()
        core_send(2, other_z(m, 2 * e + 1)).start()
        return carry

    attention_grads(0, 0)
    both(go2, 0)
    both(go3, 1)
    attention_grads(1, 0)

    peers = ((pc, m), (px, m), (py, m))

    def small(i):
        return remote(vs0, vs_r.at[i], vss.at[i], vsr.at[i], peers[i])

    def small_add(i):
        small(i).wait()
        vs0[...] += vs_r[i]

    def small_z(k):
        return remote(vs0, vs_z.at[k - 1], vzs.at[k - 1], vzr.at[k - 1], (d, other_z(m, k)))

    small(0).start()
    for u in (3, 2, 1, 0):
        go1(2, u)
    line_pg.outward(1, 0)
    both(z_step, 1)
    small_add(0)
    small(1).start()
    line_pg.outward(1, 1)
    both(go3, 0)
    small_add(1)
    small(2).start()
    go2(2, 3)
    line_pg.outward(1, 2)
    go2(2, 2)
    small_add(2)
    for k in (1, 2, 3):
        small_z(k).start()
    line_pg.inward(0)
    line_pg.outward(1, 3)
    go2(2, 1)
    go3(2, 3)
    z_step(2, 3)
    line_pg.inward(1)
    go2(2, 0)
    go3(2, 2)
    line_pg.inward(2)
    line_pg.outward(2, 0)
    go3(2, 1)
    line_pg.inward(3)
    line_pg.outward(2, 1)
    go3(2, 0)
    z_step(2, 2)
    line_pg.outward(2, 2)
    line_pg.outward(2, 3)
    z_step(2, 1)
    line_lo.rest()
    total = vs0[...]
    for k in (1, 2, 3):
        small_z(k).wait_recv()
        total = total + vs_z[k - 1]
    sums[...] = total
    go4(0)
    go4(1)
    go4(2)
    line_pg.rest()
    line_lo.finish()
    line_pg.finish()
    own_lo.wait()
    own_pg.wait()
    for k in (1, 2, 3):
        small_z(k).wait_send()
    for a in range(3):
        for u in range(4):
            core_send(a, u).wait_send()
            for h in (0, 1):
                s1(a, u, h).wait_send()
                s2(a, u, h).wait_send()
        for dist in (1, 2, 3):
            for up in (True, False):

                @pl.when(z_has(up, dist))
                def _(a=a, dist=dist, up=up):
                    z_send(a, up, dist).wait_send()


def backward_call(fill, gain1, gain2, lo, g, x, qa, k, v, ho, n1, n2, r1, hid, gp, wa, wu, wd):
    rows, width = x.shape
    any_spec = pl.BlockSpec(memory_space=pl.ANY)
    vmem = pl.BlockSpec(memory_space=pltpu.VMEM)
    flat = (rows, width)
    outs = [
        jax.ShapeDtypeStruct((4, rows, width), BF),
        jax.ShapeDtypeStruct((4, rows, width), BF),
        jax.ShapeDtypeStruct((3, 96, 768), F32),
        jax.ShapeDtypeStruct((16, width), F32),
    ]
    dma = pltpu.SemaphoreType.DMA
    scratch = [
        pltpu.VMEM(flat, BF),
        pltpu.VMEM(flat, BF),
        pltpu.VMEM((12, rows, LANES), BF),
        pltpu.VMEM(flat, BF),
        pltpu.VMEM(flat, BF),
        pltpu.VMEM(flat, BF),
        pltpu.VMEM(flat, BF),
        pltpu.VMEM(flat, BF),
        pltpu.VMEM(flat, F32),
        pltpu.VMEM((2, 2, 768, 768), BF),
        pltpu.VMEM((2, rows, 768), BF),
        pltpu.VMEM((2, rows, 768), BF),
        pltpu.VMEM((2, 768, 768), BF),
        pltpu.VMEM((2, 768, 768), BF),
        pltpu.VMEM(flat, BF),
        pltpu.VMEM(flat, F32),
        pltpu.VMEM(flat, BF),
        pltpu.VMEM(flat, BF),
        pltpu.VMEM(flat, BF),
        pltpu.VMEM(flat, BF),
        pltpu.VMEM(flat, BF),
        pltpu.VMEM((3, 4, 2, 2, 2, 96, 768), BF),
        pltpu.VMEM((3, 4, 2, 2, 96, 768), BF),
        pltpu.VMEM((3, 4, 2, 2, 48, 768), BF),
        pltpu.VMEM((3, 4, 2, 48, 768), BF),
        pltpu.VMEM((3, 5, 96, 768), BF),
        pltpu.VMEM((16, width), F32),
        pltpu.VMEM((3, 16, width), F32),
        pltpu.VMEM((3, 16, width), F32),
        dma((2, 3, 4)),
        dma((2, 3, 4)),
        dma((2, 3, 4)),
        dma((2, 3, 4)),
        dma((3, 4)),
        dma((3, 4)),
        dma((3, 4, 2)),
        dma((3, 4, 2)),
        dma((3, 4, 2)),
        dma((3, 4, 2)),
        dma((3, 4)),
        dma((3, 5)),
        dma((3,)),
        dma((3,)),
        dma((3,)),
        dma((3,)),
        dma((10,)),
        dma((4, 2)),
        dma((2,)),
    ]
    return pl.pallas_call(
        backward_kernel,
        out_shape=outs,
        in_specs=[pl.BlockSpec(memory_space=pltpu.SMEM), vmem, vmem] + [any_spec] * 15,
        out_specs=[any_spec, any_spec, vmem, vmem],
        scratch_shapes=scratch,
        compiler_params=pltpu.CompilerParams(collective_id=1, has_side_effects=True, vmem_limit_bytes=62 << 20),
        name="backward",
    )(fill, gain1, gain2, lo, g, x, qa, k, v, ho, n1, n2, r1, hid, gp, wa, wu, wd)


def prepare(patches, fill_lengths, cotangent, norm1_gain, norm1_shift, w_qkv, qv_bias, w_out, out_bias, norm2_gain, norm2_shift, w_up, up_bias, w_down, down_bias):
    m = lax.axis_index("mp")
    width = patches.shape[2]
    x = jnp.transpose(patches, (1, 0, 2))
    cot = jnp.transpose(cotangent, (1, 0, 2))
    weights = (
        jnp.transpose(w_qkv, (1, 2, 0)),
        w_out,
        w_up.reshape(2, 2, 192, width),
        w_down.reshape(2, 2, 192, width),
    )
    owner = lax.broadcasted_iota(jnp.int32, (2, 768), 1) // 192
    placed = jnp.where(owner == m, jnp.tile(qv_bias, (1, 4)), 0.0)
    vectors = (placed, up_bias, norm1_gain, norm1_shift, out_bias, norm2_gain, norm2_shift, down_bias)
    return x, cot, weights, vectors


def one_item(*args):
    length, width = args[0].shape[1:]
    x, cot, weights, vectors = prepare(*args)
    fill = args[1]
    lo, qa, k, v, ho, n1, n2, r1, hid, gp, wa, wu, wd, x, cot = forward_call(fill, x, cot, weights, vectors)
    wu = wu.reshape(4, width, 768)
    wd = wd.reshape(4, 768, width)
    lo_all, pg_all, grads, sums = backward_call(fill, vectors[2], vectors[5], lo, cot, x, qa, k, v, ho, n1, n2, r1, hid, gp, wa, wu, wd)
    d = lax.axis_index("dp")
    m = lax.axis_index("mp")
    layer_out = lo_all[:, :length]
    patches_grad = pg_all[:, :length].astype(F32)
    g = grads[2]
    is_even = m % 2 == 0

    def pick(even, odd):
        def join(parts):
            return jnp.concatenate([g[:, a:b] for a, b in parts], axis=1)

        return jnp.where(is_even, join(even), join(odd))

    q_grad = pick([(0, 192)], [(0, 64), (128, 256)])
    k_grad = pick([(256, 384), (192, 256)], [(64, 128), (256, 384)])
    v_grad = pick([(384, 576)], [(384, 448), (512, 640)])
    o_grad = pick([(640, 768), (576, 640)], [(448, 512), (640, 768)])
    mine = lax.dynamic_slice(sums, (0, d * 96), (8, 96))
    qv = lax.dynamic_slice(sums, (6, m * 192 + d * 24), (2, 24))
    up_grad = lax.dynamic_slice(sums, (8 + m, d * 96), (1, 96))[0]
    return (
        layer_out,
        patches_grad,
        mine[0],
        mine[1],
        jnp.stack([q_grad, k_grad, v_grad], axis=1),
        qv,
        o_grad.T,
        mine[2],
        mine[3],
        mine[4],
        grads[1],
        up_grad,
        grads[0].T,
        mine[5],
    )


def normalize(values, gain, shift):
    center = values - jnp.mean(values, axis=-1, keepdims=True)
    inverse = lax.rsqrt(jnp.mean(center * center, axis=-1, keepdims=True) + EPS)
    unit = center * inverse
    return (unit, inverse, unit * gain + shift)


def normalize_back(upstream, unit, inverse, gain):
    gain_grad = jnp.sum(upstream * unit, axis=(0, 1))
    shift_grad = jnp.sum(upstream, axis=(0, 1))
    scaled = upstream * gain
    result = inverse * (
        scaled
        - jnp.mean(scaled, axis=-1, keepdims=True)
        - unit * jnp.mean(scaled * unit, axis=-1, keepdims=True)
    )
    return (gain_grad, shift_grad, result)


def split_heads(rows):
    return rows.reshape(rows.shape[0], rows.shape[1] // HD, HD)


def masked_scores(queries, keyset, usable):
    scores = jnp.einsum("qhd,khd->hqk", queries, keyset, preferred_element_type=jnp.float32)
    return jnp.where(usable[None, None, :], scores, -1e30)


def attend_items(operands):
    query_rows, key_rows, value_rows, usable = operands
    scores = masked_scores(split_heads(query_rows), split_heads(key_rows), usable)
    peak = jnp.max(scores, axis=-1, keepdims=True)
    expsum = jnp.exp(scores - peak)
    total = jnp.sum(expsum, axis=-1, keepdims=True)
    weights = (expsum / total).astype(jnp.bfloat16)
    mixed = jnp.einsum(
        "hqk,khd->qhd", weights, split_heads(value_rows), preferred_element_type=jnp.float32
    )
    return (
        mixed.reshape(query_rows.shape).astype(jnp.bfloat16),
        peak[..., 0] + jnp.log(total[..., 0]),
    )


def attend_items_back(operands):
    query_rows, key_rows, value_rows, usable, logsum, upstream = operands
    queries = split_heads(query_rows)
    keyset = split_heads(key_rows)
    scores = masked_scores(queries, keyset, usable)
    probs = jnp.exp(scores - logsum[..., None])
    weights = probs.astype(jnp.bfloat16)
    grad_heads = split_heads(upstream)
    value_grad = jnp.einsum("hqk,qhd->khd", weights, grad_heads, preferred_element_type=jnp.float32)
    prob_grad = jnp.einsum(
        "qhd,khd->hqk", grad_heads, split_heads(value_rows), preferred_element_type=jnp.float32
    )
    center = jnp.sum(probs * prob_grad, axis=-1, keepdims=True)
    score_grad = (probs * (prob_grad - center)).astype(jnp.bfloat16)
    query_grad = jnp.einsum("hqk,khd->qhd", score_grad, keyset, preferred_element_type=jnp.float32)
    key_grad = jnp.einsum("hqk,qhd->khd", score_grad, queries, preferred_element_type=jnp.float32)
    shape = query_rows.shape
    return (
        query_grad.reshape(shape).astype(jnp.bfloat16),
        key_grad.reshape(shape).astype(jnp.bfloat16),
        value_grad.reshape(shape).astype(jnp.bfloat16),
    )


def shards(
    patches,
    fill_lengths,
    cotangent,
    norm1_gain,
    norm1_shift,
    w_qkv,
    qv_bias,
    w_out,
    out_bias,
    norm2_gain,
    norm2_shift,
    w_up,
    up_bias,
    w_down,
    down_bias,
):
    scaling = HD ** (-0.5)
    seq_len = patches.shape[1]
    inputs = patches.astype(jnp.float32)
    unit1, inverse1, normed1_full = normalize(inputs, norm1_gain, norm1_shift)
    normed1 = normed1_full.astype(jnp.bfloat16)
    projected = jnp.einsum("isd,dtc->istc", normed1, w_qkv, preferred_element_type=jnp.float32)
    queries = ((projected[:, :, 0] + qv_bias[0]) * scaling).astype(jnp.bfloat16)
    key_rows = projected[:, :, 1].astype(jnp.bfloat16)
    value_rows = (projected[:, :, 2] + qv_bias[1]).astype(jnp.bfloat16)
    usable = jnp.arange(seq_len, dtype=jnp.int32)[None, :] < fill_lengths[:, None]
    heads_out, logsum = lax.map(attend_items, (queries, key_rows, value_rows, usable))
    partial_attn = jnp.einsum("isc,cd->isd", heads_out, w_out, preferred_element_type=jnp.float32)
    attention = lax.psum(partial_attn, "mp")
    residual1 = inputs + attention + out_bias
    unit2, inverse2, normed2_full = normalize(residual1, norm2_gain, norm2_shift)
    normed2 = normed2_full.astype(jnp.bfloat16)
    preact = jnp.einsum("isd,df->isf", normed2, w_up, preferred_element_type=jnp.float32) + up_bias
    activated, gelu_back = jax.vjp(jax.nn.gelu, preact)
    hidden = activated.astype(jnp.bfloat16)
    partial_ff = jnp.einsum("isf,fd->isd", hidden, w_down, preferred_element_type=jnp.float32)
    feedforward = lax.psum(partial_ff, "mp")
    layer_out = (residual1 + feedforward + down_bias).astype(jnp.bfloat16)
    upstream = cotangent.astype(jnp.float32)
    down_bias_grad = jnp.sum(upstream, axis=(0, 1))
    w_down_grad = jnp.einsum("isf,isd->fd", hidden, cotangent, preferred_element_type=jnp.float32)
    hidden_grad = jnp.einsum("isd,fd->isf", cotangent, w_down, preferred_element_type=jnp.float32)
    preact_grad = gelu_back(hidden_grad)[0].astype(jnp.bfloat16)
    up_bias_grad = jnp.sum(preact_grad.astype(jnp.float32), axis=(0, 1))
    w_up_grad = jnp.einsum("isd,isf->df", normed2, preact_grad, preferred_element_type=jnp.float32)
    partial_norm2 = jnp.einsum("isf,df->isd", preact_grad, w_up, preferred_element_type=jnp.float32)
    normed2_grad = lax.psum(partial_norm2, "mp")
    norm2_gain_grad, norm2_shift_grad, through_norm2 = normalize_back(
        normed2_grad, unit2, inverse2, norm2_gain
    )
    residual1_grad = upstream + through_norm2
    out_bias_grad = jnp.sum(residual1_grad, axis=(0, 1))
    residual_low = residual1_grad.astype(jnp.bfloat16)
    w_out_grad = jnp.einsum(
        "isc,isd->cd", heads_out, residual_low, preferred_element_type=jnp.float32
    )
    heads_grad = jnp.einsum(
        "isd,cd->isc", residual_low, w_out, preferred_element_type=jnp.float32
    ).astype(jnp.bfloat16)
    query_grad, key_grad, value_grad = lax.map(
        attend_items_back, (queries, key_rows, value_rows, usable, logsum, heads_grad)
    )
    query_scaled = query_grad * scaling
    proj_grad = jnp.stack([query_scaled, key_grad, value_grad], axis=2)
    w_qkv_grad = jnp.einsum("isd,istc->dtc", normed1, proj_grad, preferred_element_type=jnp.float32)
    qv_bias_grad = jnp.stack(
        [
            jnp.sum(query_scaled.astype(jnp.float32), axis=(0, 1)),
            jnp.sum(value_grad.astype(jnp.float32), axis=(0, 1)),
        ]
    )
    partial_norm1 = jnp.einsum(
        "istc,dtc->isd", proj_grad, w_qkv, preferred_element_type=jnp.float32
    )
    normed1_grad = lax.psum(partial_norm1, "mp")
    norm1_gain_grad, norm1_shift_grad, through_norm1 = normalize_back(
        normed1_grad, unit1, inverse1, norm1_gain
    )
    patches_grad = residual1_grad + through_norm1
    summed = (
        lax.psum_scatter(norm1_gain_grad, "dp", scatter_dimension=0, tiled=True),
        lax.psum_scatter(norm1_shift_grad, "dp", scatter_dimension=0, tiled=True),
        lax.psum_scatter(w_qkv_grad, "dp", scatter_dimension=0, tiled=True),
        lax.psum_scatter(qv_bias_grad, "dp", scatter_dimension=1, tiled=True),
        lax.psum_scatter(w_out_grad, "dp", scatter_dimension=1, tiled=True),
        lax.psum_scatter(out_bias_grad, "dp", scatter_dimension=0, tiled=True),
        lax.psum_scatter(w_up_grad, "dp", scatter_dimension=0, tiled=True),
        lax.psum_scatter(up_bias_grad, "dp", scatter_dimension=0, tiled=True),
        lax.psum_scatter(w_down_grad, "dp", scatter_dimension=1, tiled=True),
        lax.psum_scatter(down_bias_grad, "dp", scatter_dimension=0, tiled=True),
        lax.psum_scatter(norm2_gain_grad, "dp", scatter_dimension=0, tiled=True),
        lax.psum_scatter(norm2_shift_grad, "dp", scatter_dimension=0, tiled=True),
    )
    return (
        layer_out,
        patches_grad,
        summed[0],
        summed[1],
        summed[2],
        summed[3],
        summed[4],
        summed[5],
        summed[10],
        summed[11],
        summed[6],
        summed[7],
        summed[8],
        summed[9],
    )


def solution(mesh):
    body = one_item if (mesh.shape['dp'], mesh.shape['mp']) == (8, 4) else shards
    return jax.shard_map(
        body,
        mesh=mesh,
        in_specs=(
            P("dp", None, None),
            P("dp"),
            P("dp", None, None),
            P(),
            P(),
            P(None, None, "mp"),
            P(None, "mp"),
            P("mp", None),
            P(),
            P(),
            P(),
            P(None, "mp"),
            P("mp"),
            P("mp", None),
            P(),
        ),
        out_specs=(
            P("dp", None, None),
            P("dp", None, None),
            P("dp"),
            P("dp"),
            P("dp", None, "mp"),
            P(None, ("mp", "dp")),
            P("mp", "dp"),
            P("dp"),
            P("dp"),
            P("dp"),
            P("dp", "mp"),
            P(("mp", "dp")),
            P("mp", "dp"),
            P("dp"),
        ),
        check_vma=False,
    )
```

```python
import functools
import jax
import jax.numpy as jnp
from jax import lax
from jax.experimental import pallas as pl
from jax.experimental.pallas import tpu as pltpu
from jax.sharding import PartitionSpec as P

MESH = pl.DeviceIdType.MESH
BF = jnp.bfloat16
F32 = jnp.float32
HD = 64
LANES = 128
EPS = 1e-6
MASKED = -1e30
GELU_A = 0.7978845608028654
GELU_B = 0.044715

NN = (((1,), (0,)), ((), ()))
NT = (((1,), (1,)), ((), ()))
TN = (((0,), (0,)), ((), ()))


def dot(a, b, dims):
    return lax.dot_general(a, b, dims, preferred_element_type=F32)


def place():
    d = lax.axis_index("dp")
    m = lax.axis_index("mp")
    y, x, c = d // 4, (d // 2) % 2, d % 2
    px = d + 2 - 4 * x
    py = d + 4 - 8 * y
    pc = d + 1 - 2 * c
    return d, m, y, x, c, px, py, pc


def other_z(m, k):
    low = (m % 2 + k % 2) % 2
    high = (m // 2 + k // 2) % 2
    return 2 * high + low


def enter(d, m, px, py, pc):
    barrier = pltpu.get_barrier_semaphore()
    for peer in ((px, m), (py, m), (pc, m)):
        pl.semaphore_signal(barrier, inc=1, device_id=peer, device_id_type=MESH)
    for k in (1, 2, 3):
        pl.semaphore_signal(barrier, inc=1, device_id=(d, other_z(m, k)), device_id_type=MESH)
    pl.semaphore_wait(barrier, 6)


def forward_kernel(
    fill_ref,
    x_in,
    g_in,
    wq_in,
    wo_in,
    wu_in,
    wd_in,
    qv_bias,
    up_bias,
    gain1,
    shift1,
    out_bias,
    gain2,
    shift2,
    down_bias,
    layer_out,
    qa_out,
    k_out,
    v_out,
    ho_out,
    n1_out,
    n2_out,
    r1_out,
    hid_out,
    gp_out,
    wa_out,
    wu_out,
    wd_out,
    x_out,
    g_out,
    wa,
    wu,
    wd,
    bias,
    q_s,
    k_s,
    v_s,
    ho_s,
    n1_s,
    n2_s,
    qa_s,
    r1_s,
    acc,
    hid_s,
    gp_s,
    lo_s,
    x_s,
    g_s,
    raw_x,
    raw_g,
    zs,
    zr,
    fs,
    s1s,
    s1r,
    s2s,
    s2r,
    cs,
    cr,
    bs,
    br,
    load,
    out,
    chunk_out,
):
    d, m, y, x, c, px, py, pc = place()
    rows = x_s.shape[0]
    length = x_in.shape[0]
    half = rows // 2

    def part(w, s, ys, xs, core, start, size):
        if w == 0:
            return wa.at[ys, xs, pl.ds(s * 192 + core * 96 + start, size)]
        full = wu if w == 1 else wd
        return full.at[s, ys, xs, pl.ds(core * 96 + start, size)]

    every = slice(None)

    def remote(src, dst, send, recv, peer):
        return pltpu.make_async_remote_copy(
            src_ref=src, dst_ref=dst, send_sem=send, recv_sem=recv, device_id=peer, device_id_type=MESH
        )

    inner = (m == 1) | (m == 2)
    k2 = 2 + ((m + 1) // 2) % 2
    k3 = 5 - k2

    def z_views(w, s):
        if w < 2:
            return (part(w, s, y, x, c, 0, 96),)
        return part(w, s, every, x, c, 0, 48), part(w, s, y, every, c, 48, 48)

    def z_copies(w, k):
        peer = (d, other_z(m, k))
        return [remote(v, v, zs.at[w, k - 1, h], zr.at[w, k - 1, h], peer) for h, v in enumerate(z_views(w, m))]

    def z_forwards(w, k):
        peer = (d, other_z(m, 1))
        views = z_views(w, other_z(m, k))
        return [remote(v, v, fs.at[w, k - 2, h], zr.at[w, 4 - k, h], peer) for h, v in enumerate(views)]

    def z_begin(w):
        for k in (1, k2):
            for one in z_copies(w, k):
                one.start()

    def z_wait(w, k):
        s = other_z(m, k)
        for h, v in enumerate(z_views(w, s)):
            remote(v, v, zs.at[w, k - 1, h], zr.at[w, k - 1, h], (d, s)).wait_recv()

    def forward(w, k):
        @pl.when(inner)
        def _():
            z_wait(w, k)
            for one in z_forwards(w, k):
                one.start()

    def arrive(w, k):
        if isinstance(k, int):
            z_wait(w, k)
        else:

            @pl.when((m == 0) | (m == 3))
            def _():
                z_wait(w, k)

    def s1(w, s, h):
        here = part(w, s, y, x, c, 48 * h, 48)
        peer = (px, m) if h == 0 else (py, m)
        return remote(here, here, s1s.at[w, s, h], s1r.at[w, s, h], peer)

    def s1_wait(w, s, h):
        here = part(w, s, y, 1 - x, c, 0, 48) if h == 0 else part(w, s, 1 - y, x, c, 48, 48)
        peer = (px, m) if h == 0 else (py, m)
        remote(here, here, s1s.at[w, s, h], s1r.at[w, s, h], peer).wait_recv()

    def s2(w, s, h):
        here = part(w, s, y, every, c, 0, 48) if h == 0 else part(w, s, every, x, c, 48, 48)
        peer = (py, m) if h == 0 else (px, m)
        return remote(here, here, s2s.at[w, s, h], s2r.at[w, s, h], peer)

    def s2_wait(w, s, h):
        here = part(w, s, 1 - y, every, c, 0, 48) if h == 0 else part(w, s, every, 1 - x, c, 48, 48)
        peer = (py, m) if h == 0 else (px, m)
        remote(here, here, s2s.at[w, s, h], s2r.at[w, s, h], peer).wait_recv()

    def core(w, s):
        here = part(w, s, every, every, c, 0, 96)
        return remote(here, here, cs.at[w, s], cr.at[w, s], (pc, m))

    def core_wait(w, k):
        s = other_z(m, k)
        here = part(w, s, every, every, 1 - c, 0, 96)
        remote(here, here, cs.at[w, s], cr.at[w, s], (pc, m)).wait_recv()

    def go1(w, k):
        s = other_z(m, k)
        arrive(w, k)
        if w < 2:
            s1(w, s, 0).start()
            s1(w, s, 1).start()
        else:
            last(s, 0).start()
            last(s, 1).start()

    def last(s, h):
        here = part(2, s, every, x, c, 0, 48) if h == 0 else part(2, s, y, every, c, 48, 48)
        peer = (px, m) if h == 0 else (py, m)
        return remote(here, here, s2s.at[2, s, h], s2r.at[2, s, h], peer)

    def last_wait(s, h):
        here = part(2, s, every, 1 - x, c, 0, 48) if h == 0 else part(2, s, 1 - y, every, c, 48, 48)
        peer = (px, m) if h == 0 else (py, m)
        remote(here, here, s2s.at[2, s, h], s2r.at[2, s, h], peer).wait_recv()

    def go2(w, k):
        s = other_z(m, k)
        s1_wait(w, s, 0)
        s2(w, s, 0).start()
        s1_wait(w, s, 1)
        s2(w, s, 1).start()

    def go3(w, k):
        s = other_z(m, k)
        wait = functools.partial(s2_wait, w) if w < 2 else last_wait
        wait(s, 0)
        wait(s, 1)
        core(w, s).start()

    def own(w):
        if w == 0:
            mine = pl.ds(m * 192, 192)
            return [pltpu.make_async_copy(wq_in.at[t], wa.at[t // 2, t % 2, mine], load.at[t]) for t in range(3)] + [
                pltpu.make_async_copy(wo_in, wa.at[1, 1, mine], load.at[3])
            ]
        src = wu_in if w == 1 else wd_in
        return [pltpu.make_async_copy(src, part(w, m, every, every, 0, 0, 192), load.at[3 + w])]

    def bias_copy(k):
        return remote(bias.at[m], bias.at[m], bs.at[k - 1], br.at[k - 1], (d, other_z(m, k)))

    def bias_wait(k):
        here = bias.at[other_z(m, k)]
        remote(here, here, bs.at[k - 1], br.at[k - 1], (d, other_z(m, k))).wait_recv()

    for w in range(3):
        for one in own(w):
            one.start()
    items = [
        pltpu.make_async_copy(src, dst.at[pl.ds(0, length)], load.at[6 + i])
        for i, (src, dst) in enumerate(((x_in, raw_x), (g_in, raw_g)))
    ]
    for one in items:
        one.start()
    bias[m, 0:1] = up_bias[...].reshape(1, 768)
    bias[m, 1:8] = jnp.zeros((7, 768), F32)
    for plane in range(4):

        @pl.when(m == plane)
        def _(plane=plane):
            bias[plane, 1:3, plane * 192 : (plane + 1) * 192] = qv_bias[...]

    enter(d, m, px, py, pc)
    for one in own(0):
        one.wait()
    z_begin(0)
    for k in (1, 2, 3):
        bias_copy(k).start()
    for one in own(1):
        one.wait()
    z_begin(1)

    def norm(values, gain, shift):
        center = values - jnp.mean(values, axis=-1, keepdims=True)
        inverse = lax.rsqrt(jnp.mean(center * center, axis=-1, keepdims=True) + EPS)
        return center * inverse * gain + shift

    def blocks(body):
        for i in range(rows // 32):
            body(pl.ds(i * 32, 32))

    def take(raw, item, i):
        block = pl.ds(pl.multiple_of(i * 32, 32), 32)
        v = raw[block].astype(F32)
        which = lax.broadcasted_iota(jnp.int32, v.shape, 1)
        row = lax.broadcasted_iota(jnp.int32, v.shape, 0) + i * 32
        item[block] = jnp.sum(jnp.where((which == m) & (row < length), v, 0.0), axis=1).astype(BF)

    items[0].wait()

    def take_x(i, carry):
        take(raw_x, x_s, i)
        return carry

    lax.fori_loop(0, rows // 32, take_x, 0)

    def first_norm(block):
        n1_s[block] = norm(x_s[block].astype(F32), gain1[...].reshape(1, 768), shift1[...].reshape(1, 768)).astype(BF)

    blocks(first_norm)
    save = [pltpu.make_async_copy(n1_s, n1_out, out.at[0])]
    save[0].start()
    items[1].wait()

    def take_g(p):
        for i in range(3):

            @pl.when(3 * p + i < rows // 32)
            def _(i=i):
                take(raw_g, g_s, 3 * p + i)

    for one in own(2):
        one.wait()

    go1(0, 1)
    forward(0, 3)
    forward(0, 2)
    z_begin(2)
    go1(0, k2)
    go2(0, 1)
    forward(1, 3)
    go1(0, k3)
    go1(1, 1)
    go2(0, k2)
    forward(1, 2)
    go3(0, 1)
    for k in (1, 2, 3):
        bias_wait(k)
    core_wait(0, 1)

    group0 = m // 2
    key_row = lax.broadcasted_iota(jnp.int32, (rows, LANES), 0)
    lane = lax.broadcasted_iota(jnp.int32, (rows, LANES), 1)
    mask_add = jnp.where(key_row < fill_ref[m], 0.0, MASKED)
    lane_half = lax.broadcasted_iota(jnp.int32, (half, LANES), 1)

    def project(g):
        rows_w = pl.ds(pl.multiple_of(g * 384, 128), 384)
        lanes = rows_w
        qb = bias[0, 1:2, lanes] + bias[1, 1:2, lanes] + bias[2, 1:2, lanes] + bias[3, 1:2, lanes]
        vb = bias[0, 2:3, lanes] + bias[1, 2:3, lanes] + bias[2, 2:3, lanes] + bias[3, 2:3, lanes]
        n1 = n1_s[...]
        q_s[:, lanes] = ((dot(n1, wa[0, 0, rows_w], NT) + qb) * (HD**-0.5)).astype(BF)
        k_s[:, lanes] = dot(n1, wa[0, 1, rows_w], NT).astype(BF)
        v_s[:, lanes] = (dot(n1, wa[1, 0, rows_w], NT) + vb).astype(BF)

    def attend(p):
        lanes = pl.ds(pl.multiple_of(p * LANES, LANES), LANES)
        kp = k_s[:, lanes].astype(F32)
        vp = v_s[:, lanes]
        keys = []
        for h in (0, 1):
            own_lane = (lane < HD) if h == 0 else (lane >= HD)
            first = HD if h == 0 else 0
            extra = jnp.where(lane == first, mask_add, jnp.where(lane < first + 4, 1.0, 0.0))
            keys.append(jnp.where(own_lane, kp, extra).astype(BF))
        for b in (0, 1):
            block = pl.ds(b * half, half)
            qp = q_s[block, lanes].astype(F32)
            mixed = []
            for h in (0, 1):
                own_lane = (lane_half < HD) if h == 0 else (lane_half >= HD)
                first = HD if h == 0 else 0
                base = jnp.where(own_lane, qp, jnp.where(lane_half == first, 1.0, 0.0))
                s = dot(base.astype(BF), keys[h], NT)
                peak = jnp.max(s, axis=-1, keepdims=True)
                e = jnp.exp(s - peak)
                total = jnp.sum(e, axis=-1, keepdims=True)
                mixed.append(dot(e.astype(BF), vp, NN) / total)
                lse = peak + jnp.log(total)
                hi = lse.astype(BF).astype(F32)
                lo = (lse - hi).astype(BF).astype(F32)
                rest = lse - hi - lo
                extra = jnp.where(
                    lane_half == first + 1, -hi, jnp.where(lane_half == first + 2, -lo, jnp.where(lane_half == first + 3, -rest, 0.0))
                )
                extra = jnp.where(lane_half == first, 1.0, extra)
                qa_s[2 * p + h, block] = jnp.where(own_lane, qp, extra).astype(BF)
            ho_s[block, lanes] = jnp.where(lane_half < HD, mixed[0], mixed[1]).astype(BF)

    project(group0)

    def steps(j, lists):
        for i, todo in enumerate(lists):

            @pl.when(j == i)
            def _(todo=todo):
                for stage, w, k in todo:
                    stage(w, k)

    def first_group(j, carry):
        attend(group0 * 3 + j)
        take_g(j)
        steps(
            j,
            (
                ((go2, 0, k3), (go3, 0, k2), (go1, 1, k2), (go2, 1, 1), (forward, 2, 3)),
                ((go3, 0, k3), (go1, 1, k3), (go2, 1, k2), (forward, 2, 2), (go1, 2, 1)),
                ((go3, 1, 1), (go2, 1, k3)),
            ),
        )
        return carry

    lax.fori_loop(0, 3, first_group, 0)
    core_wait(0, 2)
    core_wait(0, 3)
    save.append(pltpu.make_async_copy(wa, wa_out, out.at[7]))
    save[-1].start()
    project(1 - group0)

    def second_group(j, carry):
        attend((1 - group0) * 3 + j)
        take_g(3 + j)
        steps(j, (((go3, 1, k2), (go1, 2, k2)), ((go3, 1, k3), (go3, 2, 1)), ((go1, 2, k3),)))
        return carry

    lax.fori_loop(0, 3, second_group, 0)
    pairs = ((qa_s, qa_out), (k_s, k_out), (v_s, v_out), (ho_s, ho_out))
    for i, (a, b) in enumerate(pairs):
        save.append(pltpu.make_async_copy(a, b, out.at[1 + i]))
        save[-1].start()
    for i, (a, b) in enumerate(((x_s, x_out), (g_s, g_out))):
        save.append(pltpu.make_async_copy(a, b, out.at[9 + i]))
        save[-1].start()

    def finish_attention(n, carry):
        cols = pl.ds(pl.multiple_of(n * 256, 256), 256)
        acc[:, cols] = dot(ho_s[...], wa[1, 1, :, cols], NN)
        return carry

    lax.fori_loop(0, 3, finish_attention, 0)

    def second_norm(block):
        r1 = x_s[block].astype(F32) + acc[block] + out_bias[...].reshape(1, 768)
        r1_s[block] = r1
        n2_s[block] = norm(r1, gain2[...].reshape(1, 768), shift2[...].reshape(1, 768)).astype(BF)
        acc[block] = r1 + down_bias[...].reshape(1, 768)

    blocks(second_norm)
    more = ((r1_s, r1_out), (n2_s, n2_out))
    for i, (a, b) in enumerate(more):
        save.append(pltpu.make_async_copy(a, b, out.at[5 + i]))
        save[-1].start()
    go3(2, k2)

    def in_order(k):
        return k + (k // 2) * (k2 - 2) * (5 - 2 * k)

    def chunk_save(k):
        mk = other_z(m, in_order(k))
        pairs = ((wu, wu_out), (wd, wd_out), (hid_s, hid_out), (gp_s, gp_out))
        return [pltpu.make_async_copy(a.at[mk], b.at[mk], chunk_out.at[i, k]) for i, (a, b) in enumerate(pairs)]

    def feed(k, carry):
        ke = in_order(k)
        mk = other_z(m, ke)

        @pl.when(k == 1)
        def _():
            go3(2, k3)

        @pl.when(k > 0)
        def _():
            core_wait(1, ke)
            core_wait(2, ke)

        for one in chunk_save(k)[:2]:
            one.start()

        def up(n, inner):
            cols = pl.ds(pl.multiple_of(n * 256, 256), 256)
            w = wu[mk, :, :, :, cols].reshape(768, 256)
            v = dot(n2_s[...], w, NN) + bias[mk, 0:1, cols]
            sq = v * v
            t = jnp.tanh(v * (GELU_A + GELU_A * GELU_B * sq))
            hid_s[mk, :, cols] = (0.5 * v * (1.0 + t)).astype(BF)
            slope = 0.5 * (1.0 + t) + 0.5 * v * (1.0 - t * t) * (GELU_A + 3.0 * GELU_A * GELU_B * sq)
            gp_s[mk, :, cols] = slope.astype(BF)
            return inner

        lax.fori_loop(0, 3, up, 0)
        for one in chunk_save(k)[2:]:
            one.start()

        def down(n, inner):
            cols = pl.ds(pl.multiple_of(n * 256, 256), 256)
            w = wd[mk, :, :, :, cols].reshape(768, 256)
            acc[:, cols] += dot(hid_s[mk], w, NN)
            return inner

        lax.fori_loop(0, 3, down, 0)
        return carry

    lax.fori_loop(0, 4, feed, 0)
    lo_s[...] = acc[...].astype(BF)
    save.append(pltpu.make_async_copy(lo_s, layer_out, out.at[8]))
    save[-1].start()
    for one in save:
        one.wait()
    for k in range(4):
        for one in chunk_save(k):
            one.wait()
    for k in (1, 2, 3):
        bias_copy(k).wait_send()
    for w in range(3):
        for k in (1, 2, 3):
            s = other_z(m, k)
            for h in (0, 1):
                if w < 2:
                    s1(w, s, h).wait_send()
                    s2(w, s, h).wait_send()
                else:
                    last(s, h).wait_send()
            core(w, s).wait_send()

        for k in (1, k2):
            for one in z_copies(w, k):
                one.wait_send()

        @pl.when(inner)
        def _(w=w):
            for k in (2, 3):
                for one in z_forwards(w, k):
                    one.wait_send()


def forward_call(fill, x, g, weights, vectors):
    length, items, width = x.shape
    rows = -(-length // 32) * 32
    any_spec = pl.BlockSpec(memory_space=pl.ANY)
    vmem = pl.BlockSpec(memory_space=pltpu.VMEM)
    flat = (rows, width)

    def hbm(shape, kind=BF):
        return jax.ShapeDtypeStruct(shape, kind)

    outs = [
        hbm(flat),
        hbm((12, rows, LANES)),
        hbm(flat),
        hbm(flat),
        hbm(flat),
        hbm(flat),
        hbm(flat),
        hbm(flat, F32),
        hbm((4, rows, 768)),
        hbm((4, rows, 768)),
        hbm((2, 2, 768, 768)),
        hbm((4, 2, 2, 192, 768)),
        hbm((4, 2, 2, 192, 768)),
        hbm(flat),
        hbm(flat),
    ]
    dma = pltpu.SemaphoreType.DMA
    scratch = [
        pltpu.VMEM((2, 2, 768, 768), BF),
        pltpu.VMEM((4, 2, 2, 192, 768), BF),
        pltpu.VMEM((4, 2, 2, 192, 768), BF),
        pltpu.VMEM((4, 8, 768), F32),
        pltpu.VMEM(flat, BF),
        pltpu.VMEM(flat, BF),
        pltpu.VMEM(flat, BF),
        pltpu.VMEM(flat, BF),
        pltpu.VMEM(flat, BF),
        pltpu.VMEM(flat, BF),
        pltpu.VMEM((12, rows, LANES), BF),
        pltpu.VMEM(flat, F32),
        pltpu.VMEM(flat, F32),
        pltpu.VMEM((4, rows, 768), BF),
        pltpu.VMEM((4, rows, 768), BF),
        pltpu.VMEM(flat, BF),
        pltpu.VMEM(flat, BF),
        pltpu.VMEM(flat, BF),
        pltpu.VMEM((rows, items, width), BF),
        pltpu.VMEM((rows, items, width), BF),
        dma((3, 3, 2)),
        dma((3, 3, 2)),
        dma((3, 2, 2)),
        dma((3, 4, 2)),
        dma((3, 4, 2)),
        dma((3, 4, 2)),
        dma((3, 4, 2)),
        dma((3, 4)),
        dma((3, 4)),
        dma((3,)),
        dma((3,)),
        dma((8,)),
        dma((11,)),
        dma((4, 4)),
    ]
    return pl.pallas_call(
        forward_kernel,
        out_shape=outs,
        in_specs=[pl.BlockSpec(memory_space=pltpu.SMEM)] + [any_spec] * 6 + [vmem] * 8,
        out_specs=[any_spec] * len(outs),
        scratch_shapes=scratch,
        compiler_params=pltpu.CompilerParams(collective_id=0, has_side_effects=True, vmem_limit_bytes=60 << 20),
        name="forward",
    )(fill, x, g, *weights, *vectors)


def backward_kernel(
    fill_ref,
    gain1,
    gain2,
    lo_in,
    g_in,
    x_in,
    qa_in,
    k_in,
    v_in,
    ho_in,
    n1_in,
    n2_in,
    r1_in,
    hid_in,
    gp_in,
    wa_in,
    wu_in,
    wd_in,
    lo_all,
    pg_all,
    grads,
    sums,
    g_s,
    x_s,
    qa_s,
    k_s,
    v_s,
    ho_s,
    n1_s,
    n2_s,
    r1_s,
    wa,
    hid_b,
    gp_b,
    wu_b,
    wd_b,
    pre_s,
    acc,
    res_s,
    dho_s,
    dq_s,
    dk_s,
    dv_s,
    unit,
    rc,
    rx,
    ry,
    rz,
    vs0,
    vs_r,
    vs_z,
    los,
    lor,
    pgs,
    pgr,
    cs,
    cr,
    s1s,
    s1r,
    s2s,
    s2r,
    zs,
    zr,
    vss,
    vsr,
    vzs,
    vzr,
    load,
    chunk_load,
    own_sem,
):
    d, m, y, x, c, px, py, pc = place()
    rows = g_in.shape[0]
    half = rows // 2
    every = slice(None)

    def remote(src, dst, send, recv, peer):
        return pltpu.make_async_remote_copy(
            src_ref=src, dst_ref=dst, send_sem=send, recv_sem=recv, device_id=peer, device_id_type=MESH
        )

    quarter = rows // 64 * 16
    starts = [(i * quarter, quarter if i < 3 else rows - 3 * quarter) for i in range(4)]

    class Line:
        def __init__(self, own, full, send, recv):
            self.own, self.full, self.send, self.recv = own, full, send, recv

        def copy(self, up, dist, j, sending):
            step = 1 if up else -1
            begin, size = starts[j]
            source = m - step * (dist - 1) if sending else m - step * dist
            there = self.full.at[source, pl.ds(begin, size)]
            here = self.own.at[pl.ds(begin, size)] if (sending and dist == 1) else there
            i = 0 if up else 1
            return remote(here, there, self.send.at[i, dist - 1, j], self.recv.at[i, dist - 1, j], (d, m + step if sending else m - step))

        def sends(self, up, dist):
            return ((m >= dist - 1) & (m <= 2)) if up else ((m <= 4 - dist) & (m >= 1))

        def gets(self, up, dist):
            return (m >= dist) if up else (m <= 3 - dist)

        def begin(self):
            for j in range(4):
                for up in (True, False):
                    @pl.when(self.sends(up, 1))
                    def _(up=up, j=j):
                        self.copy(up, 1, j, True).start()

        def pass_on(self, up, dist, j):
            self.copy(up, dist, j, False).wait_recv()
            self.copy(up, dist + 1, j, True).start()

        def outward(self, dist, j):
            for at, up in ((1, False), (2, True)):
                @pl.when(m == at)
                def _(up=up):
                    self.pass_on(up, dist, j)

        def inward(self, j):
            for at, up in ((1, True), (2, False)):
                @pl.when(m == at)
                def _(up=up):
                    self.pass_on(up, 1, j)

        def rest(self):
            for dist in (1, 2, 3):
                for j in range(4):
                    for up in (True, False):
                        stays = self.gets(up, dist)
                        if dist < 3:
                            stays = stays & ((m == 3) if up else (m == 0))

                        @pl.when(stays)
                        def _(up=up, dist=dist, j=j):
                            self.copy(up, dist, j, False).wait_recv()

        def finish(self):
            for dist in (1, 2, 3):
                for j in range(4):
                    for up in (True, False):
                        @pl.when(self.sends(up, dist))
                        def _(up=up, dist=dist, j=j):
                            self.copy(up, dist, j, True).wait_send()

    def core_send(a, u):
        return remote(unit.at[a, u, every, every, 1 - c], rc.at[a, u], cs.at[a, u], cr.at[a, u], (pc, m))

    def s1(a, u, h):
        if h == 0:
            return remote(unit.at[a, u, every, 1 - x, c, pl.ds(0, 48)], rx.at[a, u, 0], s1s.at[a, u, 0], s1r.at[a, u, 0], (px, m))
        return remote(unit.at[a, u, 1 - y, every, c, pl.ds(48, 48)], rx.at[a, u, 1], s1s.at[a, u, 1], s1r.at[a, u, 1], (py, m))

    def s2(a, u, h):
        if h == 0:
            return remote(unit.at[a, u, 1 - y, x, c, pl.ds(0, 48)], ry.at[a, u, 0], s2s.at[a, u, 0], s2r.at[a, u, 0], (py, m))
        return remote(unit.at[a, u, y, 1 - x, c, pl.ds(48, 48)], ry.at[a, u, 1], s2s.at[a, u, 1], s2r.at[a, u, 1], (px, m))

    def z_send(a, up, dist):
        p = m + dist if up else m - dist
        slot = 4 if (up and dist == 1) else p
        peer = m + 1 if up else m - 1
        return remote(unit.at[a, other_z(m, p), y, x, c], rz.at[a, slot], zs.at[a, p], zr.at[a, slot], (d, peer))

    def z_recv(a, slot):
        remote(rz.at[a, slot], rz.at[a, slot], zs.at[a, 0], zr.at[a, slot], (d, other_z(m, 1))).wait_recv()

    def z_has(up, dist):
        return (m + dist <= 3) if up else (m >= dist)

    def z_step(a, dist):
        for up in (True, False):

            @pl.when(z_has(up, dist))
            def _(up=up):
                p = m + dist if up else m - dist
                if dist < 3:

                    @pl.when((m > 0) if up else (m < 3))
                    def _():
                        z_recv(a, p)
                        u = other_z(m, p)
                        unit[a, u, y, x, c] = (unit[a, u, y, x, c].astype(F32) + rz[a, p].astype(F32)).astype(BF)

                z_send(a, up, dist).start()

    def go1(a, u):
        core_send(a, u).wait_recv()
        unit[a, u, :, :, c] = (unit[a, u, :, :, c].astype(F32) + rc[a, u].astype(F32)).astype(BF)
        s1(a, u, 0).start()
        s1(a, u, 1).start()

    def go2(a, u):
        s1(a, u, 0).wait_recv()
        unit[a, u, :, x, c, 0:48] = (unit[a, u, :, x, c, 0:48].astype(F32) + rx[a, u, 0].astype(F32)).astype(BF)
        s2(a, u, 0).start()
        s1(a, u, 1).wait_recv()
        unit[a, u, y, :, c, 48:96] = (unit[a, u, y, :, c, 48:96].astype(F32) + rx[a, u, 1].astype(F32)).astype(BF)
        s2(a, u, 1).start()

    def go3(a, u):
        for h in (0, 1):
            s2(a, u, h).wait_recv()
            part = pl.ds(48 * h, 48)
            unit[a, u, y, x, c, part] = (unit[a, u, y, x, c, part].astype(F32) + ry[a, u, h].astype(F32)).astype(BF)

    def go4(a):
        grads[a] = unit[a, 0, y, x, c].astype(F32)

        @pl.when(m < 3)
        def _():
            z_recv(a, m)
            grads[a] += rz[a, m].astype(F32)

        @pl.when(m > 0)
        def _():
            z_recv(a, 4)
            grads[a] += rz[a, 4].astype(F32)

    def copies(i):
        pairs = (
            (g_in, g_s),
            (n2_in, n2_s),
            (r1_in, r1_s),
            (ho_in, ho_s),
            (wa_in, wa),
            (qa_in, qa_s),
            (k_in, k_s),
            (v_in, v_s),
            (n1_in, n1_s),
            (x_in, x_s),
        )
        return pltpu.make_async_copy(pairs[i][0], pairs[i][1], load.at[i])

    def chunk(k):
        slot = k % 2
        mk = other_z(m, 3 - k)
        pairs = ((wd_in, wd_b), (gp_in, gp_b), (hid_in, hid_b), (wu_in, wu_b))
        return [pltpu.make_async_copy(a.at[mk], b.at[slot], chunk_load.at[i, slot]) for i, (a, b) in enumerate(pairs)]

    line_lo = Line(lo_in, lo_all, los, lor)
    line_pg = Line(dho_s, pg_all, pgs, pgr)

    copies(0).start()
    for one in chunk(0):
        one.start()
    enter(d, m, px, py, pc)
    line_lo.begin()
    own_lo = pltpu.make_async_copy(lo_in, lo_all.at[m], own_sem.at[0])
    own_lo.start()
    for i in range(1, 10):
        copies(i).start()
    copies(0).wait()
    copies(1).wait()
    sums_row = jnp.zeros((1, 768), F32)
    for i in range(vs0.shape[0]):
        vs0[i : i + 1] = sums_row
    acc[...] = jnp.zeros_like(acc)

    def feed(k, carry):
        slot = k % 2
        u = 3 - k
        mk = other_z(m, u)

        @pl.when(k < 3)
        def _():
            for one in chunk(k + 1):
                one.start()

        for one in chunk(k):
            one.wait()

        def first(n, inner):
            cols = pl.ds(pl.multiple_of(n * 256, 256), 256)
            hg = dot(g_s[...], wd_b[slot, cols], NT)
            low = (hg * gp_b[slot, :, cols].astype(F32)).astype(BF)
            pre_s[:, cols] = low
            vs0[pl.ds(8 + mk, 1), cols] = jnp.sum(low.astype(F32), axis=0, keepdims=True)
            return inner

        lax.fori_loop(0, 3, first, 0)

        def second(n, inner):
            cols = pl.ds(pl.multiple_of(n * 384, 128), 384)
            unit[0, u, n] = dot(g_s[:, cols], hid_b[slot], TN).astype(BF).reshape(2, 2, 96, 768)
            unit[1, u, n] = dot(n2_s[:, cols], pre_s[...], TN).astype(BF).reshape(2, 2, 96, 768)
            return inner

        lax.fori_loop(0, 2, second, 0)
        core_send(0, u).start()
        core_send(1, u).start()

        def third(n, inner):
            cols = pl.ds(pl.multiple_of(n * 256, 256), 256)
            acc[:, cols] += dot(pre_s[...], wu_b[slot, cols], NT)
            return inner

        @pl.when(k > 0)
        def _():
            go1(0, u + 1)
            go1(1, u + 1)

        lax.fori_loop(0, 3, third, 0)
        return carry

    lax.fori_loop(0, 4, feed, 0)
    line_lo.outward(1, 0)
    line_lo.inward(0)
    line_lo.outward(1, 1)
    line_lo.inward(1)

    def norm_back(values, upstream, gain):
        center = values - jnp.mean(values, axis=-1, keepdims=True)
        inverse = lax.rsqrt(jnp.mean(center * center, axis=-1, keepdims=True) + EPS)
        n = center * inverse
        scaled = upstream * gain
        result = inverse * (
            scaled - jnp.mean(scaled, axis=-1, keepdims=True) - n * jnp.mean(scaled * n, axis=-1, keepdims=True)
        )
        gain_part = jnp.sum(upstream * n, axis=0, keepdims=True)
        return result, gain_part, jnp.sum(upstream, axis=0, keepdims=True)

    for i in (2, 3, 4):
        copies(i).wait()

    zero = jnp.zeros((1, 768), F32)
    carry = (zero, zero, zero, zero)
    for i in range(rows // 32):
        block = pl.ds(i * 32, 32)
        upstream = acc[block]
        through, gain_part, shift_part = norm_back(r1_s[block], upstream, gain2[...].reshape(1, 768))
        g = g_s[block].astype(F32)
        res = g + through
        r1_s[block] = res
        res_s[block] = res.astype(BF)
        parts = (gain_part, shift_part, jnp.sum(res, axis=0, keepdims=True), jnp.sum(g, axis=0, keepdims=True))
        carry = tuple(a + b for a, b in zip(carry, parts))
    n2g, n2s, ob, db = carry
    go1(0, 0)
    go1(1, 0)
    line_lo.outward(1, 2)
    line_lo.inward(2)
    vs0[2:3] = ob
    vs0[3:4] = n2g
    vs0[4:5] = n2s
    vs0[5:6] = db

    def heads_grad(n, carry):
        cols = pl.ds(pl.multiple_of(n * 256, 256), 256)
        dho_s[:, cols] = dot(res_s[...], wa[1, 1, cols], NT).astype(BF)
        return carry

    lax.fori_loop(0, 3, heads_grad, 0)
    line_lo.outward(1, 3)
    line_lo.inward(3)
    for i in (5, 6, 7):
        copies(i).wait()

    key_row = lax.broadcasted_iota(jnp.int32, (rows, LANES), 0)
    lane = lax.broadcasted_iota(jnp.int32, (rows, LANES), 1)
    mask_add = jnp.where(key_row < fill_ref[m], 0.0, MASKED)
    lane_half = lax.broadcasted_iota(jnp.int32, (half, LANES), 1)
    lane_turned = lax.broadcasted_iota(jnp.int32, (LANES, rows), 0)

    def attend(p):
        lanes = pl.ds(pl.multiple_of(p * LANES, LANES), LANES)
        kp = k_s[:, lanes].astype(F32)
        vp = v_s[:, lanes].astype(F32)
        dop = dho_s[:, lanes]
        dof = dop.astype(F32)
        both = dof * ho_s[:, lanes].astype(F32)
        ups = []
        for h in (0, 1):
            own_lane = (lane < HD) if h == 0 else (lane >= HD)
            first = HD if h == 0 else 0
            center = jnp.sum(jnp.where(own_lane, both, 0.0), axis=-1, keepdims=True)
            hi = center.astype(BF).astype(F32)
            lo = (center - hi).astype(BF).astype(F32)
            rest = center - hi - lo
            extra = jnp.where(lane == first, -hi, jnp.where(lane == first + 1, -lo, jnp.where(lane == first + 2, -rest, 0.0)))
            ups.append(jnp.where(own_lane, dof, extra).astype(BF))
        turned = [None, None]
        for b in (0, 1):
            block = slice(b * half, (b + 1) * half)
            dks, dvs = [], []
            for h in (0, 1):
                own_lane = (lane_half < HD) if h == 0 else (lane_half >= HD)
                first = HD if h == 0 else 0
                extra = jnp.where(lane_half == first, mask_add[block], jnp.where(lane_half < first + 4, 1.0, 0.0))
                keys = jnp.where(own_lane, kp[block], extra).astype(BF)
                values = jnp.where(own_lane, vp[block], jnp.where(lane_half < first + 3, 1.0, 0.0)).astype(BF)
                qa = qa_s[2 * p + h]
                probs = jnp.exp(dot(keys, qa, NT))
                dvs.append(dot(probs.astype(BF), dop, NN))
                ds = (probs * dot(values, ups[h], NT)).astype(BF)
                dks.append(dot(ds, qa, NN))
                t = dot(keys, ds, TN)
                turned[h] = t if b == 0 else turned[h] + t
            here = pl.ds(b * half, half)
            dk_s[here, lanes] = jnp.where(lane_half < HD, dks[0], dks[1]).astype(BF)
            dv_s[here, lanes] = jnp.where(lane_half < HD, dvs[0], dvs[1]).astype(BF)
        dq = jnp.where(lane_turned < HD, turned[0], turned[1])
        dq_s[:, lanes] = (jnp.transpose(dq) * (HD**-0.5)).astype(BF)

    def pair(p, carry):
        attend(p)

        @pl.when((p == 1) | (p == 3))
        def _():
            u = 3 - p // 2
            go2(0, u)
            go2(1, u)

        @pl.when(p == 5)
        def _():
            go3(0, 3)
            go3(1, 3)

        for j in range(4):
            @pl.when(p == j + 1)
            def _(j=j):
                line_lo.outward(2, j)

        return carry

    lax.fori_loop(0, 6, pair, 0)
    def both(stage, u):
        stage(0, u)
        stage(1, u)

    both(go2, 1)
    both(z_step, 3)
    vs0[6:7] = jnp.sum(dq_s[...].astype(F32), axis=0, keepdims=True)
    vs0[7:8] = jnp.sum(dv_s[...].astype(F32), axis=0, keepdims=True)
    copies(8).wait()
    copies(9).wait()

    def last_product(n, carry):
        cols = pl.ds(pl.multiple_of(n * 256, 256), 256)
        acc[:, cols] = (
            dot(dq_s[...], wa[0, 0, :, cols], NN) + dot(dk_s[...], wa[0, 1, :, cols], NN) + dot(dv_s[...], wa[1, 0, :, cols], NN)
        )
        return carry

    lax.fori_loop(0, 3, last_product, 0)
    both(go3, 2)

    carry = (zero, zero)
    for i in range(rows // 32):
        block = pl.ds(i * 32, 32)
        through, gain_part, shift_part = norm_back(x_s[block].astype(F32), acc[block], gain1[...].reshape(1, 768))
        dho_s[block] = (r1_s[block] + through).astype(BF)
        carry = (carry[0] + gain_part, carry[1] + shift_part)
    n1g, n1s = carry
    vs0[0:1] = n1g
    vs0[1:2] = n1s
    both(z_step, 2)
    line_pg.begin()
    own_pg = pltpu.make_async_copy(dho_s, pg_all.at[m], own_sem.at[1])
    own_pg.start()

    lane_tile = lax.broadcasted_iota(jnp.int32, (384, LANES), 1)

    def turn(v):
        return pltpu.roll(v, HD, 1)

    def attention_grads(e, carry):
        def tile(n, inner):
            cols = pl.ds(pl.multiple_of(n * 384, 128), 384)
            heads = pl.ds(pl.multiple_of(e * 384, 128), 384)
            n1 = n1_s[:, cols]
            q, k, v = [dot(n1, t[:, heads], TN) for t in (dq_s, dk_s, dv_s)]
            o = dot(res_s[:, cols], ho_s[:, heads], TN)

            def block(t, i):
                return t[:, i * LANES : (i + 1) * LANES]

            def low(a, b):
                return jnp.where(lane_tile < HD, block(a, 1), turn(block(b, 1)))

            def high(a, b):
                return jnp.where(lane_tile < HD, turn(block(a, 1)), block(b, 1))

            even = [block(q, 0), low(q, k), block(k, 0), block(v, 0), low(v, o), block(o, 0)]
            odd = [high(q, k), block(q, 2), block(k, 2), high(v, o), block(v, 2), block(o, 2)]
            ue, uo = other_z(m, 2 * e), other_z(m, 2 * e + 1)
            for i in range(6):
                lanes = slice(i * LANES, (i + 1) * LANES)
                unit[2, ue, n, :, :, :, lanes] = even[i].astype(BF).reshape(2, 2, 96, LANES)
                unit[2, uo, n, :, :, :, lanes] = odd[i].astype(BF).reshape(2, 2, 96, LANES)
            return inner

        lax.fori_loop(0, 2, tile, 0)
        core_send(2, other_z(m, 2 * e)).start()
        core_send(2, other_z(m, 2 * e + 1)).start()
        return carry

    attention_grads(0, 0)
    both(go2, 0)
    both(go3, 1)
    attention_grads(1, 0)

    peers = ((pc, m), (px, m), (py, m))

    def small(i):
        return remote(vs0, vs_r.at[i], vss.at[i], vsr.at[i], peers[i])

    def small_add(i):
        small(i).wait()
        vs0[...] += vs_r[i]

    def small_z(k):
        return remote(vs0, vs_z.at[k - 1], vzs.at[k - 1], vzr.at[k - 1], (d, other_z(m, k)))

    small(0).start()
    for u in (3, 2, 1, 0):
        go1(2, u)
    line_pg.outward(1, 0)
    both(z_step, 1)
    small_add(0)
    small(1).start()
    line_pg.outward(1, 1)
    both(go3, 0)
    small_add(1)
    small(2).start()
    go2(2, 3)
    line_pg.outward(1, 2)
    go2(2, 2)
    small_add(2)
    for k in (1, 2, 3):
        small_z(k).start()
    line_pg.inward(0)
    line_pg.outward(1, 3)
    go2(2, 1)
    go3(2, 3)
    z_step(2, 3)
    line_pg.inward(1)
    go2(2, 0)
    go3(2, 2)
    line_pg.inward(2)
    line_pg.outward(2, 0)
    go3(2, 1)
    line_pg.inward(3)
    line_pg.outward(2, 1)
    go3(2, 0)
    z_step(2, 2)
    line_pg.outward(2, 2)
    line_pg.outward(2, 3)
    z_step(2, 1)
    line_lo.rest()
    total = vs0[...]
    for k in (1, 2, 3):
        small_z(k).wait_recv()
        total = total + vs_z[k - 1]
    up = jnp.zeros((1, 768), F32)
    for plane in range(4):
        up = jnp.where(m == plane, total[8 + plane : 9 + plane], up)
    rows_of = jnp.concatenate([total[0:8], up, jnp.zeros((7, 768), F32)], axis=0)
    mine = jnp.zeros((16, 96), F32)
    for i in range(8):
        mine = jnp.where(d == i, rows_of[:, i * 96 : (i + 1) * 96], mine)
    sums[0:16, 0:96] = mine
    of_plane = jnp.zeros((8, 192), F32)
    for plane in range(4):
        of_plane = jnp.where(m == plane, total[0:8, plane * 192 : (plane + 1) * 192], of_plane)
    few = jnp.zeros((8, 24), F32)
    for i in range(8):
        few = jnp.where(d == i, of_plane[:, i * 24 : (i + 1) * 24], few)
    sums[16:24, 0:24] = few
    go4(0)
    go4(1)
    go4(2)
    line_pg.rest()
    line_lo.finish()
    line_pg.finish()
    own_lo.wait()
    own_pg.wait()
    for k in (1, 2, 3):
        small_z(k).wait_send()
    for a in range(3):
        for u in range(4):
            core_send(a, u).wait_send()
            for h in (0, 1):
                s1(a, u, h).wait_send()
                s2(a, u, h).wait_send()
        for dist in (1, 2, 3):
            for up in (True, False):

                @pl.when(z_has(up, dist))
                def _(a=a, dist=dist, up=up):
                    z_send(a, up, dist).wait_send()


def backward_call(fill, gain1, gain2, lo, g, x, qa, k, v, ho, n1, n2, r1, hid, gp, wa, wu, wd):
    rows, width = x.shape
    any_spec = pl.BlockSpec(memory_space=pl.ANY)
    vmem = pl.BlockSpec(memory_space=pltpu.VMEM)
    flat = (rows, width)
    outs = [
        jax.ShapeDtypeStruct((4, rows, width), BF),
        jax.ShapeDtypeStruct((4, rows, width), BF),
        jax.ShapeDtypeStruct((3, 96, 768), F32),
        jax.ShapeDtypeStruct((24, LANES), F32),
    ]
    dma = pltpu.SemaphoreType.DMA
    scratch = [
        pltpu.VMEM(flat, BF),
        pltpu.VMEM(flat, BF),
        pltpu.VMEM((12, rows, LANES), BF),
        pltpu.VMEM(flat, BF),
        pltpu.VMEM(flat, BF),
        pltpu.VMEM(flat, BF),
        pltpu.VMEM(flat, BF),
        pltpu.VMEM(flat, BF),
        pltpu.VMEM(flat, F32),
        pltpu.VMEM((2, 2, 768, 768), BF),
        pltpu.VMEM((2, rows, 768), BF),
        pltpu.VMEM((2, rows, 768), BF),
        pltpu.VMEM((2, 768, 768), BF),
        pltpu.VMEM((2, 768, 768), BF),
        pltpu.VMEM(flat, BF),
        pltpu.VMEM(flat, F32),
        pltpu.VMEM(flat, BF),
        pltpu.VMEM(flat, BF),
        pltpu.VMEM(flat, BF),
        pltpu.VMEM(flat, BF),
        pltpu.VMEM(flat, BF),
        pltpu.VMEM((3, 4, 2, 2, 2, 96, 768), BF),
        pltpu.VMEM((3, 4, 2, 2, 96, 768), BF),
        pltpu.VMEM((3, 4, 2, 2, 48, 768), BF),
        pltpu.VMEM((3, 4, 2, 48, 768), BF),
        pltpu.VMEM((3, 5, 96, 768), BF),
        pltpu.VMEM((16, width), F32),
        pltpu.VMEM((3, 16, width), F32),
        pltpu.VMEM((3, 16, width), F32),
        dma((2, 3, 4)),
        dma((2, 3, 4)),
        dma((2, 3, 4)),
        dma((2, 3, 4)),
        dma((3, 4)),
        dma((3, 4)),
        dma((3, 4, 2)),
        dma((3, 4, 2)),
        dma((3, 4, 2)),
        dma((3, 4, 2)),
        dma((3, 4)),
        dma((3, 5)),
        dma((3,)),
        dma((3,)),
        dma((3,)),
        dma((3,)),
        dma((10,)),
        dma((4, 2)),
        dma((2,)),
    ]
    return pl.pallas_call(
        backward_kernel,
        out_shape=outs,
        in_specs=[pl.BlockSpec(memory_space=pltpu.SMEM), vmem, vmem] + [any_spec] * 15,
        out_specs=[any_spec, any_spec, vmem, vmem],
        scratch_shapes=scratch,
        compiler_params=pltpu.CompilerParams(collective_id=1, has_side_effects=True, vmem_limit_bytes=62 << 20),
        name="backward",
    )(fill, gain1, gain2, lo, g, x, qa, k, v, ho, n1, n2, r1, hid, gp, wa, wu, wd)


def prepare(patches, fill_lengths, cotangent, norm1_gain, norm1_shift, w_qkv, qv_bias, w_out, out_bias, norm2_gain, norm2_shift, w_up, up_bias, w_down, down_bias):
    m = lax.axis_index("mp")
    width = patches.shape[2]
    x = jnp.transpose(patches, (1, 0, 2))
    cot = jnp.transpose(cotangent, (1, 0, 2))
    weights = (
        jnp.transpose(w_qkv, (1, 2, 0)),
        w_out,
        w_up.reshape(2, 2, 192, width),
        w_down.reshape(2, 2, 192, width),
    )
    vectors = (qv_bias, up_bias, norm1_gain, norm1_shift, out_bias, norm2_gain, norm2_shift, down_bias)
    return x, cot, weights, vectors


def one_item(*args):
    length, width = args[0].shape[1:]
    x, cot, weights, vectors = prepare(*args)
    fill = args[1]
    lo, qa, k, v, ho, n1, n2, r1, hid, gp, wa, wu, wd, x, cot = forward_call(fill, x, cot, weights, vectors)
    wu = wu.reshape(4, width, 768)
    wd = wd.reshape(4, 768, width)
    lo_all, pg_all, grads, sums = backward_call(fill, vectors[2], vectors[5], lo, cot, x, qa, k, v, ho, n1, n2, r1, hid, gp, wa, wu, wd)
    m = lax.axis_index("mp")
    layer_out = lo_all[:, :length]
    patches_grad = pg_all[:, :length].astype(F32)
    g = grads[2]
    is_even = m % 2 == 0

    def pick(even, odd):
        def join(parts):
            return jnp.concatenate([g[:, a:b] for a, b in parts], axis=1)

        return jnp.where(is_even, join(even), join(odd))

    q_grad = pick([(0, 192)], [(0, 64), (128, 256)])
    k_grad = pick([(256, 384), (192, 256)], [(64, 128), (256, 384)])
    v_grad = pick([(384, 576)], [(384, 448), (512, 640)])
    o_grad = pick([(640, 768), (576, 640)], [(448, 512), (640, 768)])
    mine = sums[0:9, 0:96]
    qv = sums[22:24, 0:24]
    up_grad = mine[8]
    return (
        layer_out,
        patches_grad,
        mine[0],
        mine[1],
        jnp.stack([q_grad, k_grad, v_grad], axis=1),
        qv,
        o_grad.T,
        mine[2],
        mine[3],
        mine[4],
        grads[1],
        up_grad,
        grads[0].T,
        mine[5],
    )


def normalize(values, gain, shift):
    center = values - jnp.mean(values, axis=-1, keepdims=True)
    inverse = lax.rsqrt(jnp.mean(center * center, axis=-1, keepdims=True) + EPS)
    unit = center * inverse
    return (unit, inverse, unit * gain + shift)


def normalize_back(upstream, unit, inverse, gain):
    gain_grad = jnp.sum(upstream * unit, axis=(0, 1))
    shift_grad = jnp.sum(upstream, axis=(0, 1))
    scaled = upstream * gain
    result = inverse * (
        scaled
        - jnp.mean(scaled, axis=-1, keepdims=True)
        - unit * jnp.mean(scaled * unit, axis=-1, keepdims=True)
    )
    return (gain_grad, shift_grad, result)


def split_heads(rows):
    return rows.reshape(rows.shape[0], rows.shape[1] // HD, HD)


def masked_scores(queries, keyset, usable):
    scores = jnp.einsum("qhd,khd->hqk", queries, keyset, preferred_element_type=jnp.float32)
    return jnp.where(usable[None, None, :], scores, -1e30)


def attend_items(operands):
    query_rows, key_rows, value_rows, usable = operands
    scores = masked_scores(split_heads(query_rows), split_heads(key_rows), usable)
    peak = jnp.max(scores, axis=-1, keepdims=True)
    expsum = jnp.exp(scores - peak)
    total = jnp.sum(expsum, axis=-1, keepdims=True)
    weights = (expsum / total).astype(jnp.bfloat16)
    mixed = jnp.einsum(
        "hqk,khd->qhd", weights, split_heads(value_rows), preferred_element_type=jnp.float32
    )
    return (
        mixed.reshape(query_rows.shape).astype(jnp.bfloat16),
        peak[..., 0] + jnp.log(total[..., 0]),
    )


def attend_items_back(operands):
    query_rows, key_rows, value_rows, usable, logsum, upstream = operands
    queries = split_heads(query_rows)
    keyset = split_heads(key_rows)
    scores = masked_scores(queries, keyset, usable)
    probs = jnp.exp(scores - logsum[..., None])
    weights = probs.astype(jnp.bfloat16)
    grad_heads = split_heads(upstream)
    value_grad = jnp.einsum("hqk,qhd->khd", weights, grad_heads, preferred_element_type=jnp.float32)
    prob_grad = jnp.einsum(
        "qhd,khd->hqk", grad_heads, split_heads(value_rows), preferred_element_type=jnp.float32
    )
    center = jnp.sum(probs * prob_grad, axis=-1, keepdims=True)
    score_grad = (probs * (prob_grad - center)).astype(jnp.bfloat16)
    query_grad = jnp.einsum("hqk,khd->qhd", score_grad, keyset, preferred_element_type=jnp.float32)
    key_grad = jnp.einsum("hqk,qhd->khd", score_grad, queries, preferred_element_type=jnp.float32)
    shape = query_rows.shape
    return (
        query_grad.reshape(shape).astype(jnp.bfloat16),
        key_grad.reshape(shape).astype(jnp.bfloat16),
        value_grad.reshape(shape).astype(jnp.bfloat16),
    )


def shards(
    patches,
    fill_lengths,
    cotangent,
    norm1_gain,
    norm1_shift,
    w_qkv,
    qv_bias,
    w_out,
    out_bias,
    norm2_gain,
    norm2_shift,
    w_up,
    up_bias,
    w_down,
    down_bias,
):
    scaling = HD ** (-0.5)
    seq_len = patches.shape[1]
    inputs = patches.astype(jnp.float32)
    unit1, inverse1, normed1_full = normalize(inputs, norm1_gain, norm1_shift)
    normed1 = normed1_full.astype(jnp.bfloat16)
    projected = jnp.einsum("isd,dtc->istc", normed1, w_qkv, preferred_element_type=jnp.float32)
    queries = ((projected[:, :, 0] + qv_bias[0]) * scaling).astype(jnp.bfloat16)
    key_rows = projected[:, :, 1].astype(jnp.bfloat16)
    value_rows = (projected[:, :, 2] + qv_bias[1]).astype(jnp.bfloat16)
    usable = jnp.arange(seq_len, dtype=jnp.int32)[None, :] < fill_lengths[:, None]
    heads_out, logsum = lax.map(attend_items, (queries, key_rows, value_rows, usable))
    partial_attn = jnp.einsum("isc,cd->isd", heads_out, w_out, preferred_element_type=jnp.float32)
    attention = lax.psum(partial_attn, "mp")
    residual1 = inputs + attention + out_bias
    unit2, inverse2, normed2_full = normalize(residual1, norm2_gain, norm2_shift)
    normed2 = normed2_full.astype(jnp.bfloat16)
    preact = jnp.einsum("isd,df->isf", normed2, w_up, preferred_element_type=jnp.float32) + up_bias
    activated, gelu_back = jax.vjp(jax.nn.gelu, preact)
    hidden = activated.astype(jnp.bfloat16)
    partial_ff = jnp.einsum("isf,fd->isd", hidden, w_down, preferred_element_type=jnp.float32)
    feedforward = lax.psum(partial_ff, "mp")
    layer_out = (residual1 + feedforward + down_bias).astype(jnp.bfloat16)
    upstream = cotangent.astype(jnp.float32)
    down_bias_grad = jnp.sum(upstream, axis=(0, 1))
    w_down_grad = jnp.einsum("isf,isd->fd", hidden, cotangent, preferred_element_type=jnp.float32)
    hidden_grad = jnp.einsum("isd,fd->isf", cotangent, w_down, preferred_element_type=jnp.float32)
    preact_grad = gelu_back(hidden_grad)[0].astype(jnp.bfloat16)
    up_bias_grad = jnp.sum(preact_grad.astype(jnp.float32), axis=(0, 1))
    w_up_grad = jnp.einsum("isd,isf->df", normed2, preact_grad, preferred_element_type=jnp.float32)
    partial_norm2 = jnp.einsum("isf,df->isd", preact_grad, w_up, preferred_element_type=jnp.float32)
    normed2_grad = lax.psum(partial_norm2, "mp")
    norm2_gain_grad, norm2_shift_grad, through_norm2 = normalize_back(
        normed2_grad, unit2, inverse2, norm2_gain
    )
    residual1_grad = upstream + through_norm2
    out_bias_grad = jnp.sum(residual1_grad, axis=(0, 1))
    residual_low = residual1_grad.astype(jnp.bfloat16)
    w_out_grad = jnp.einsum(
        "isc,isd->cd", heads_out, residual_low, preferred_element_type=jnp.float32
    )
    heads_grad = jnp.einsum(
        "isd,cd->isc", residual_low, w_out, preferred_element_type=jnp.float32
    ).astype(jnp.bfloat16)
    query_grad, key_grad, value_grad = lax.map(
        attend_items_back, (queries, key_rows, value_rows, usable, logsum, heads_grad)
    )
    query_scaled = query_grad * scaling
    proj_grad = jnp.stack([query_scaled, key_grad, value_grad], axis=2)
    w_qkv_grad = jnp.einsum("isd,istc->dtc", normed1, proj_grad, preferred_element_type=jnp.float32)
    qv_bias_grad = jnp.stack(
        [
            jnp.sum(query_scaled.astype(jnp.float32), axis=(0, 1)),
            jnp.sum(value_grad.astype(jnp.float32), axis=(0, 1)),
        ]
    )
    partial_norm1 = jnp.einsum(
        "istc,dtc->isd", proj_grad, w_qkv, preferred_element_type=jnp.float32
    )
    normed1_grad = lax.psum(partial_norm1, "mp")
    norm1_gain_grad, norm1_shift_grad, through_norm1 = normalize_back(
        normed1_grad, unit1, inverse1, norm1_gain
    )
    patches_grad = residual1_grad + through_norm1
    summed = (
        lax.psum_scatter(norm1_gain_grad, "dp", scatter_dimension=0, tiled=True),
        lax.psum_scatter(norm1_shift_grad, "dp", scatter_dimension=0, tiled=True),
        lax.psum_scatter(w_qkv_grad, "dp", scatter_dimension=0, tiled=True),
        lax.psum_scatter(qv_bias_grad, "dp", scatter_dimension=1, tiled=True),
        lax.psum_scatter(w_out_grad, "dp", scatter_dimension=1, tiled=True),
        lax.psum_scatter(out_bias_grad, "dp", scatter_dimension=0, tiled=True),
        lax.psum_scatter(w_up_grad, "dp", scatter_dimension=0, tiled=True),
        lax.psum_scatter(up_bias_grad, "dp", scatter_dimension=0, tiled=True),
        lax.psum_scatter(w_down_grad, "dp", scatter_dimension=1, tiled=True),
        lax.psum_scatter(down_bias_grad, "dp", scatter_dimension=0, tiled=True),
        lax.psum_scatter(norm2_gain_grad, "dp", scatter_dimension=0, tiled=True),
        lax.psum_scatter(norm2_shift_grad, "dp", scatter_dimension=0, tiled=True),
    )
    return (
        layer_out,
        patches_grad,
        summed[0],
        summed[1],
        summed[2],
        summed[3],
        summed[4],
        summed[5],
        summed[10],
        summed[11],
        summed[6],
        summed[7],
        summed[8],
        summed[9],
    )


def solution(mesh):
    body = one_item if (mesh.shape['dp'], mesh.shape['mp']) == (8, 4) else shards
    return jax.shard_map(
        body,
        mesh=mesh,
        in_specs=(
            P("dp", None, None),
            P("dp"),
            P("dp", None, None),
            P(),
            P(),
            P(None, None, "mp"),
            P(None, "mp"),
            P("mp", None),
            P(),
            P(),
            P(),
            P(None, "mp"),
            P("mp"),
            P("mp", None),
            P(),
        ),
        out_specs=(
            P("dp", None, None),
            P("dp", None, None),
            P("dp"),
            P("dp"),
            P("dp", None, "mp"),
            P(None, ("mp", "dp")),
            P("mp", "dp"),
            P("dp"),
            P("dp"),
            P("dp"),
            P("dp", "mp"),
            P(("mp", "dp")),
            P("mp", "dp"),
            P("dp"),
        ),
        check_vma=False,
    )
```
